32 devices in a mesh: ka: 4 (over z), row: 4 (over y, x), col: 2 (over core).
Axes of the slice: x: 2, y: 2, z: 4, core: 2. Of those that a mesh axis runs over, the one named last changes fastest.
Arguments:
- exciton: bfloat16 [4, 4, 128, 128], P('ka'), may hold values from -6 to 6
- orb_cond: bfloat16 [4, 128, 2048], P('ka', None, 'row'), may hold values from -0.5 to 0.5
- orb_val: bfloat16 [4, 128, 2048], P('ka', None, 'col'), may hold values from -0.5 to 0.5
- screened: bfloat16 [4, 2048, 2048], P(None, 'row', 'col'), may hold values from -3 to 3
- q_table: int32 [4, 4], replicated, may hold values from 0 to 3, as said below
Outputs:
- applied: float32 [4, 4, 128, 128], P('ka', None, 'col')
The draws below stay inside these ranges and needn't reach their ends.
Inputs may be any that keep to these rules, and one draw needn't show every extreme that they name: q_table is the difference table of the k-points of a cyclic grid of 4 points under a relabeling of points and of differences: every row and every column holds each of 0 to 3 once.
All inputs are finite; a program needn't handle non-finite values.
Results may differ from the reference program's by a relative error of at most 0.019.
Values may be sent and summed in bfloat16 or wider, within the bound.
No kernel may reach another device: no remote copies, remote signals or barrier semaphores. Data moves between devices by JAX's collectives and lax.ppermute only.
A program may use at most 64 MiB of HBM per device.

```python
import math
import jax
import jax.numpy as jnp
from jax import lax

NV = 128
NC = 128
NMU = 2048
NB = 4
NK = 4


def draw_q_table(key, part):
    first_key, second_key = jax.random.split(jax.random.fold_in(key, 7))
    positions = jax.random.permutation(first_key, NK).astype(jnp.int32)
    labels = jax.random.permutation(second_key, NK).astype(jnp.int32)
    difference = (positions[:, None] - positions[None, :]) % NK
    return labels[difference].astype(jnp.int32)


def shard_levels(rng, extent, shards, least, top_value):
    def one(dim, blocks):
        draws = jax.random.uniform(jax.random.fold_in(jax.random.fold_in(rng, 6), dim), (blocks,), jnp.float32, least / len(shards), top_value / len(shards))
        return jnp.repeat(jnp.exp(draws), extent[dim] // blocks).reshape((-1,) + (1,) * (len(extent) - dim - 1))

    factor_of = one(*shards[0])
    for cut in shards[1:]:
        factor_of = factor_of * one(*cut)
    return factor_of


def noise(rng, extent, deviation, reach, cuts=(), held_as=jnp.bfloat16):
    result = deviation * jax.random.normal(rng, extent, jnp.float32)
    if cuts:
        result = result * shard_levels(rng, extent, cuts, -0.22, 0.18)
    return jnp.clip(result, -reach, reach).astype(held_as)


def setup_inputs(seed: int = 0) -> dict:
    keys = jax.random.split(jax.random.key(seed), 6)
    return {
        "exciton": noise(keys[0], (NK, NB, NV, NC), 1.0, 6.0, ((0, 4),)),
        "orb_cond": noise(keys[1], (NK, NC, NMU), NC ** -0.5, 0.5, ((0, 4), (2, 4))),
        "orb_val": noise(keys[2], (NK, NV, NMU), NV ** -0.5, 0.5, ((0, 4), (2, 2))),
        "screened": noise(keys[3], (NK, NMU, NMU), NK ** -0.5, 3.0, ((1, 4), (2, 2))),
        "q_table": draw_q_table(jax.random.fold_in(keys[5], 71), 0),
    }


def reference(exciton, orb_cond, orb_val, screened, q_table):
    highest = lax.Precision.HIGHEST
    panels = jnp.einsum('kbvc,kcm->kbvm', exciton.astype(jnp.float32), orb_cond.astype(jnp.float32), precision=highest).astype(jnp.bfloat16)

    def make_pairs(k_point):
        return jnp.einsum('bvm,vn->bmn', panels[k_point].astype(jnp.float32), orb_val[k_point].astype(jnp.float32), precision=highest).astype(jnp.bfloat16)
    pair_block = lax.map(make_pairs, jnp.arange(NK, dtype=jnp.int32))
    factor = math.sqrt(NV * NC) / NMU

    def per_point(k_point):
        columns = q_table[:, k_point]

        def accumulate(running, k_other):
            weights = screened[columns[k_other]].astype(jnp.float32)
            return (running + weights[None] * pair_block[k_other].astype(jnp.float32), None)
        direct, unused = lax.scan(accumulate, jnp.zeros((NB, NMU, NMU), jnp.float32), jnp.arange(NK, dtype=jnp.int32))
        direct = direct.astype(jnp.bfloat16)
        half_sums = jnp.einsum('bmn,vn->bmv', direct.astype(jnp.float32), orb_val[k_point].astype(jnp.float32), precision=highest).astype(jnp.bfloat16)
        return jnp.einsum('cm,bmv->bvc', orb_cond[k_point].astype(jnp.float32), half_sums.astype(jnp.float32), precision=highest) * factor
    return lax.map(per_point, jnp.arange(NK, dtype=jnp.int32))
```

```python
import functools
import math

import jax
import jax.numpy as jnp
from jax import lax
from jax.experimental import pallas as pl
from jax.experimental.pallas import tpu as pltpu
from jax.sharding import PartitionSpec as P

BF16 = jnp.bfloat16
F32 = jnp.float32
LANES = 128


def swap(value, axis, size, flip):
    return lax.ppermute(value, axis, [(i, i ^ flip) for i in range(size)])


def pack_kernel(sizes, exciton_ref, cond_ref, val_ref, cond_part_ref, rest_ref):
    n_row, n_col = sizes
    row, col = lax.axis_index("row"), lax.axis_index("col")
    part = cond_part_ref.shape[0]
    cond_part_ref[...] = cond_ref[pl.ds(pl.multiple_of(col * part, part), part), :]
    part = val_ref.shape[0] // n_row
    blocks = val_ref.shape[1] // LANES
    for block in range(blocks):
        rest_ref[block * part:(block + 1) * part, :] = val_ref[
            pl.ds(pl.multiple_of(row * part, part), part), block * LANES:(block + 1) * LANES
        ]
    part_x = exciton_ref.shape[0] // n_row
    rest_ref[blocks * part:, :] = exciton_ref[
        pl.ds(pl.multiple_of(row * part_x, part_x), part_x), :
    ]


def main_kernel(sizes, factor, tile, chunk, *refs):
    n_ka, n_row, n_col = sizes
    q_ref, exciton_ref, cond_ref, val_ref, w_ref = refs[:5]
    cond_parts = refs[5:5 + (n_ka - 1) * n_col]
    rests = refs[5 + (n_ka - 1) * n_col:5 + (n_ka - 1) * (n_col + n_row)]
    keep_ref = refs[5 + (n_ka - 1) * (n_col + n_row)]
    outs = refs[6 + (n_ka - 1) * (n_col + n_row):5 + (n_ka - 1) * (n_col + n_row) + n_col]
    x_all, cond_all, val_all, panels, half, total = refs[-6:]
    step = pl.program_id(0)
    me, row, col = (lax.axis_index(name) for name in ("ka", "row", "col"))
    n_v, n_nu = val_ref.shape
    n_b = exciton_ref.shape[0] // n_v

    @pl.when(step == 0)
    def assemble():
        x_all[0] = exciton_ref[...]
        cond_all[0] = cond_ref[...]
        val_all[0] = val_ref[...]
        part_c, part_v, part_x = n_v // n_col, n_v // n_row, exciton_ref.shape[0] // n_row
        blocks = n_nu // LANES
        for flip in range(1, n_ka):
            for other in range(n_col):
                place = pl.multiple_of((col ^ other) * part_c, part_c)
                cond_all[flip, pl.ds(place, part_c), :] = cond_parts[(flip - 1) * n_col + other][...]
            for other in range(n_row):
                source = rests[(flip - 1) * n_row + other]
                place = pl.multiple_of((row ^ other) * part_v, part_v)
                for block in range(blocks):
                    val_all[flip, pl.ds(place, part_v), block * LANES:(block + 1) * LANES] = source[
                        block * part_v:(block + 1) * part_v, :
                    ]
                place = pl.multiple_of((row ^ other) * part_x, part_x)
                x_all[flip, pl.ds(place, part_x), :] = source[blocks * part_v:, :]
        total[...] = jnp.zeros_like(total)

    columns = pl.ds(pl.multiple_of(step * tile, tile), tile)
    for flip in range(n_ka):
        cond_tile = cond_all[flip, :, columns]
        for b in range(n_b):
            panels[flip, b * tile:(b + 1) * tile, :] = lax.dot_general(
                cond_tile, x_all[flip, b * n_v:(b + 1) * n_v, :],
                (((0,), (1,)), ((), ())), preferred_element_type=F32,
            ).astype(BF16)
    for j in range(n_nu // chunk):
        at = slice(j * chunk, (j + 1) * chunk)
        direct = None
        for flip in range(n_ka):
            pairs = jnp.dot(panels[flip], val_all[flip, :, at], preferred_element_type=F32)
            weights = w_ref[q_ref[me ^ flip, me], :, at].astype(F32)
            term = pairs.reshape(n_b, tile, chunk) * weights[None]
            direct = term if direct is None else direct + term
        direct = direct.reshape(n_b * tile, chunk).astype(BF16)
        sums = lax.dot_general(
            direct, val_ref[:, at], (((1,), (1,)), ((), ())), preferred_element_type=F32
        )
        if j == 0:
            half[...] = sums
        else:
            half[...] += sums
    cond_tile = cond_ref[:, columns]
    for b in range(n_b):
        total[b] += lax.dot_general(
            half[b * tile:(b + 1) * tile, :].astype(BF16), cond_tile,
            (((0,), (1,)), ((), ())), preferred_element_type=F32,
        )

    @pl.when(step == pl.num_programs(0) - 1)
    def finish():
        part = n_v // n_col
        for other in range(n_col):
            place = pl.multiple_of((col ^ other) * part, part)
            value = total[:, pl.ds(place, part), :] * factor
            if other == 0:
                keep_ref[...] = value
            else:
                outs[other - 1][...] = value.astype(BF16)


def local(sizes, exciton, orb_cond, orb_val, screened, q_table):
    n_ka, n_row, n_col = sizes
    n_b, n_v, n_c = exciton.shape[1:]
    cond, val = orb_cond[0], orb_val[0]
    n_mu, n_nu = cond.shape[1], val.shape[1]
    x_rows = exciton.reshape(n_b * n_v, n_c)
    rest_rows = val.size // n_row // LANES + x_rows.shape[0] // n_row
    cond_part, rest = pl.pallas_call(
        functools.partial(pack_kernel, (n_row, n_col)),
        out_shape=(
            jax.ShapeDtypeStruct((n_c // n_col, n_mu), BF16),
            jax.ShapeDtypeStruct((rest_rows, LANES), BF16),
        ),
        name="pack",
    )(x_rows, cond, val)
    cond_parts, rests = [], []
    for flip in range(1, n_ka):
        first = swap(cond_part, "ka", n_ka, flip)
        cond_parts += [first] + [swap(first, "col", n_col, d) for d in range(1, n_col)]
        first = swap(rest, "ka", n_ka, flip)
        rests += [first] + [swap(first, "row", n_row, d) for d in range(1, n_row)]

    factor = math.sqrt(n_v * n_c) / (n_mu * n_row)
    tile = 128
    chunk = 256
    part = n_v // n_col
    whole = pl.BlockSpec(memory_space=pltpu.VMEM)
    small = [cond_part.shape] * len(cond_parts) + [rest.shape] * len(rests)
    kept, *sent = pl.pallas_call(
        functools.partial(main_kernel, sizes, factor, tile, chunk),
        grid=(n_mu // tile,),
        in_specs=[pl.BlockSpec(memory_space=pltpu.SMEM), whole, whole, whole,
                  pl.BlockSpec((screened.shape[0], tile, n_nu), lambda i: (0, i, 0))]
        + [whole] * len(small),
        out_specs=[whole] * n_col,
        out_shape=[jax.ShapeDtypeStruct((n_b, part, n_c), F32)]
        + [jax.ShapeDtypeStruct((n_b, part, n_c), BF16)] * (n_col - 1),
        scratch_shapes=[
            pltpu.VMEM((n_ka, n_b * n_v, n_c), BF16),
            pltpu.VMEM((n_ka, n_c, n_mu), BF16),
            pltpu.VMEM((n_ka, n_v, n_nu), BF16),
            pltpu.VMEM((n_ka, n_b * tile, n_v), BF16),
            pltpu.VMEM((n_b * tile, n_v), F32),
            pltpu.VMEM((n_b, n_v, n_c), F32),
        ],
        compiler_params=pltpu.CompilerParams(vmem_limit_bytes=40 * 2**20),
        name="direct_term",
    )(q_table, x_rows, cond, val, screened, *cond_parts, *rests)
    mine = kept
    for flip in range(1, n_col):
        mine = mine + swap(sent[flip - 1], "col", n_col, flip).astype(F32)
    mine = mine.astype(BF16)
    terms = [mine] + [swap(mine, "row", n_row, flip) for flip in range(1, n_row)]
    terms = [term.astype(F32) for term in terms]
    while len(terms) > 1:
        terms = [a + b for a, b in zip(terms[::2], terms[1::2])]
    return terms[0][None]


def solution(mesh):
    placed = (
        P("ka", None, None, None),
        P("ka", None, "row"),
        P("ka", None, "col"),
        P(None, "row", "col"),
        P(),
    )
    sizes = tuple(mesh.shape[name] for name in ("ka", "row", "col"))
    return jax.shard_map(
        functools.partial(local, sizes), mesh=mesh, in_specs=placed,
        out_specs=P("ka", None, "col", None), check_vma=False,
    )
```

```python
import functools
import math

import jax
import jax.numpy as jnp
from jax import lax
from jax.experimental import pallas as pl
from jax.experimental.pallas import tpu as pltpu
from jax.sharding import PartitionSpec as P

BF16 = jnp.bfloat16
F32 = jnp.float32
LANES = 128


def swap(value, axis, size, flip):
    return lax.ppermute(value, axis, [(i, i ^ flip) for i in range(size)])


def pack_kernel(sizes, exciton_ref, cond_ref, val_ref, cond_part_ref, rest_ref):
    n_row, n_col = sizes
    row, col = lax.axis_index("row"), lax.axis_index("col")
    part = cond_part_ref.shape[0]
    cond_part_ref[...] = cond_ref[pl.ds(pl.multiple_of(col * part, part), part), :]
    part = val_ref.shape[0] // n_row
    blocks = val_ref.shape[1] // LANES
    for block in range(blocks):
        rest_ref[block * part:(block + 1) * part, :] = val_ref[
            pl.ds(pl.multiple_of(row * part, part), part), block * LANES:(block + 1) * LANES
        ]
    part_x = exciton_ref.shape[0] // n_row
    rest_ref[blocks * part:, :] = exciton_ref[
        pl.ds(pl.multiple_of(row * part_x, part_x), part_x), :
    ]


def main_kernel(sizes, factor, tile, chunk, *refs):
    n_ka, n_row, n_col = sizes
    q_ref, exciton_ref, cond_ref, val_ref, w_ref = refs[:5]
    cond_parts = refs[5:5 + (n_ka - 1) * n_col]
    rests = refs[5 + (n_ka - 1) * n_col:5 + (n_ka - 1) * (n_col + n_row)]
    keep_ref = refs[5 + (n_ka - 1) * (n_col + n_row)]
    outs = refs[6 + (n_ka - 1) * (n_col + n_row):5 + (n_ka - 1) * (n_col + n_row) + n_col]
    x_all, cond_all, val_all, panels, half, total = refs[-6:]
    step = pl.program_id(0)
    me, row, col = (lax.axis_index(name) for name in ("ka", "row", "col"))
    n_v, n_nu = val_ref.shape
    n_b = exciton_ref.shape[0] // n_v

    @pl.when(step == 0)
    def assemble():
        x_all[0] = exciton_ref[...]
        cond_all[0] = cond_ref[...]
        val_all[0] = val_ref[...]
        part_c, part_v, part_x = n_v // n_col, n_v // n_row, exciton_ref.shape[0] // n_row
        blocks = n_nu // LANES
        for flip in range(1, n_ka):
            for other in range(n_col):
                place = pl.multiple_of((col ^ other) * part_c, part_c)
                cond_all[flip, pl.ds(place, part_c), :] = cond_parts[(flip - 1) * n_col + other][...]
            for other in range(n_row):
                source = rests[(flip - 1) * n_row + other]
                place = pl.multiple_of((row ^ other) * part_v, part_v)
                for block in range(blocks):
                    val_all[flip, pl.ds(place, part_v), block * LANES:(block + 1) * LANES] = source[
                        block * part_v:(block + 1) * part_v, :
                    ]
                place = pl.multiple_of((row ^ other) * part_x, part_x)
                x_all[flip, pl.ds(place, part_x), :] = source[blocks * part_v:, :]
        total[...] = jnp.zeros_like(total)

    columns = pl.ds(pl.multiple_of(step * tile, tile), tile)
    for flip in range(n_ka):
        cond_tile = cond_all[flip, :, columns]
        for b in range(n_b):
            panels[flip, b * tile:(b + 1) * tile, :] = lax.dot_general(
                cond_tile, x_all[flip, b * n_v:(b + 1) * n_v, :],
                (((0,), (1,)), ((), ())), preferred_element_type=F32,
            ).astype(BF16)
    for j in range(n_nu // chunk):
        at = slice(j * chunk, (j + 1) * chunk)
        direct = None
        for flip in range(n_ka):
            pairs = jnp.dot(panels[flip], val_all[flip, :, at], preferred_element_type=F32)
            weights = w_ref[q_ref[me ^ flip, me], :, at].astype(F32)
            term = pairs.reshape(n_b, tile, chunk) * weights[None]
            direct = term if direct is None else direct + term
        direct = direct.reshape(n_b * tile, chunk).astype(BF16)
        sums = lax.dot_general(
            direct, val_ref[:, at], (((1,), (1,)), ((), ())), preferred_element_type=F32
        )
        if j == 0:
            half[...] = sums
        else:
            half[...] += sums
    cond_tile = cond_ref[:, columns]
    for b in range(n_b):
        total[b] += lax.dot_general(
            half[b * tile:(b + 1) * tile, :].astype(BF16), cond_tile,
            (((0,), (1,)), ((), ())), preferred_element_type=F32,
        )

    @pl.when(step == pl.num_programs(0) - 1)
    def finish():
        part = n_v // n_col
        for other in range(n_col):
            place = pl.multiple_of((col ^ other) * part, part)
            value = total[:, pl.ds(place, part), :] * factor
            if other == 0:
                keep_ref[...] = value
            else:
                outs[other - 1][...] = value.astype(BF16)


def local(sizes, exciton, orb_cond, orb_val, screened, q_table):
    n_ka, n_row, n_col = sizes
    n_b, n_v, n_c = exciton.shape[1:]
    cond, val = orb_cond[0], orb_val[0]
    n_mu, n_nu = cond.shape[1], val.shape[1]
    x_rows = exciton.reshape(n_b * n_v, n_c)
    rest_rows = val.size // n_row // LANES + x_rows.shape[0] // n_row
    cond_part, rest = pl.pallas_call(
        functools.partial(pack_kernel, (n_row, n_col)),
        out_shape=(
            jax.ShapeDtypeStruct((n_c // n_col, n_mu), BF16),
            jax.ShapeDtypeStruct((rest_rows, LANES), BF16),
        ),
        name="pack",
    )(x_rows, cond, val)
    cond_parts, rests = [], []
    for flip in range(1, n_ka):
        first = swap(cond_part, "ka", n_ka, flip)
        cond_parts += [first] + [swap(first, "col", n_col, d) for d in range(1, n_col)]
        first = swap(rest, "ka", n_ka, flip)
        rests += [first] + [swap(first, "row", n_row, d) for d in range(1, n_row)]

    factor = math.sqrt(n_v * n_c) / (n_mu * n_row)
    tile = 128
    chunk = 256
    part = n_v // n_col
    whole = pl.BlockSpec(memory_space=pltpu.VMEM)
    small = [cond_part.shape] * len(cond_parts) + [rest.shape] * len(rests)
    kept, *sent = pl.pallas_call(
        functools.partial(main_kernel, sizes, factor, tile, chunk),
        grid=(n_mu // tile,),
        in_specs=[pl.BlockSpec(memory_space=pltpu.SMEM), whole, whole, whole,
                  pl.BlockSpec((screened.shape[0], tile, n_nu), lambda i: (0, i, 0))]
        + [whole] * len(small),
        out_specs=[whole] * n_col,
        out_shape=[jax.ShapeDtypeStruct((n_b, part, n_c), F32)]
        + [jax.ShapeDtypeStruct((n_b, part, n_c), BF16)] * (n_col - 1),
        scratch_shapes=[
            pltpu.VMEM((n_ka, n_b * n_v, n_c), BF16),
            pltpu.VMEM((n_ka, n_c, n_mu), BF16),
            pltpu.VMEM((n_ka, n_v, n_nu), BF16),
            pltpu.VMEM((n_ka, n_b * tile, n_v), BF16),
            pltpu.VMEM((n_b * tile, n_v), F32),
            pltpu.VMEM((n_b, n_v, n_c), F32),
        ],
        compiler_params=pltpu.CompilerParams(vmem_limit_bytes=60 * 2**20),
        name="direct_term",
    )(q_table, x_rows, cond, val, screened, *cond_parts, *rests)
    mine = kept
    for flip in range(1, n_col):
        mine = mine + swap(sent[flip - 1], "col", n_col, flip).astype(F32)
    mine = mine.astype(BF16)
    copies = jnp.broadcast_to(mine[None], (n_row, *mine.shape))
    terms = lax.all_to_all(copies, "row", 0, 0, tiled=True).astype(F32)
    return jnp.sum(terms, axis=0)[None]


def solution(mesh):
    placed = (
        P("ka", None, None, None),
        P("ka", None, "row"),
        P("ka", None, "col"),
        P(None, "row", "col"),
        P(),
    )
    sizes = tuple(mesh.shape[name] for name in ("ka", "row", "col"))
    return jax.shard_map(
        functools.partial(local, sizes), mesh=mesh, in_specs=placed,
        out_specs=P("ka", None, "col", None), check_vma=False,
    )
```

```python
import functools
import math

import jax
import jax.numpy as jnp
from jax import lax
from jax.experimental import pallas as pl
from jax.experimental.pallas import tpu as pltpu
from jax.sharding import PartitionSpec as P

BF16 = jnp.bfloat16
F32 = jnp.float32
LANES = 128


def swap(value, axis, size, flip):
    return lax.ppermute(value, axis, [(i, i ^ flip) for i in range(size)])


def pack_kernel(sizes, exciton_ref, cond_ref, val_ref, core_ref, plane_ref):
    n_row, n_col = sizes
    row, col = lax.axis_index("row"), lax.axis_index("col")
    part = cond_ref.shape[0] // n_col
    blocks = cond_ref.shape[1] // LANES
    for block in range(blocks):
        core_ref[block * part:(block + 1) * part, :] = cond_ref[
            pl.ds(pl.multiple_of(col * part, part), part), block * LANES:(block + 1) * LANES
        ]
    part_x = exciton_ref.shape[0] // n_col
    core_ref[blocks * part:, :] = exciton_ref[
        pl.ds(pl.multiple_of(col * part_x, part_x), part_x), :
    ]
    part = plane_ref.shape[0]
    plane_ref[...] = val_ref[pl.ds(pl.multiple_of(row * part, part), part), :]


def join_kernel(*refs):
    *parts, out = refs
    at = 0
    for part in parts:
        out[at:at + part.shape[0], :] = part[...]
        at += part.shape[0]


def join(parts):
    if len(parts) == 1:
        return parts[0]
    rows = sum(part.shape[0] for part in parts)
    return pl.pallas_call(
        join_kernel, out_shape=jax.ShapeDtypeStruct((rows, parts[0].shape[1]), BF16), name="join"
    )(*parts)


def main_kernel(sizes, groups, factor, tile, chunk, *refs):
    n_ka, n_row, n_col = sizes
    q_ref, exciton_ref, cond_ref, val_ref, w_ref = refs[:5]
    n_core, n_plane = (n_ka - 1) * n_col, len(groups) * n_row
    cores = refs[5:5 + n_core]
    planes = refs[5 + n_core:5 + n_core + n_plane]
    keep_ref = refs[5 + n_core + n_plane]
    outs = refs[6 + n_core + n_plane:5 + n_core + n_plane + n_col]
    x_all, cond_all, val_all, panels, half, total = refs[-6:]
    step = pl.program_id(0)
    me, row, col = (lax.axis_index(name) for name in ("ka", "row", "col"))
    n_v, n_nu = val_ref.shape
    n_c, n_mu = cond_ref.shape
    n_b = exciton_ref.shape[0] // n_v

    @pl.when(step == 0)
    def assemble():
        x_all[0] = exciton_ref[...]
        cond_all[0] = cond_ref[...]
        val_all[0] = val_ref[...]
        part_c, part_v, part_x = n_c // n_col, n_v // n_row, exciton_ref.shape[0] // n_col
        blocks = n_mu // LANES
        for flip in range(1, n_ka):
            for other in range(n_col):
                source = cores[(flip - 1) * n_col + other]
                place = pl.multiple_of((col ^ other) * part_c, part_c)
                for block in range(blocks):
                    cond_all[flip, pl.ds(place, part_c), block * LANES:(block + 1) * LANES] = source[
                        block * part_c:(block + 1) * part_c, :
                    ]
                place = pl.multiple_of((col ^ other) * part_x, part_x)
                x_all[flip, pl.ds(place, part_x), :] = source[blocks * part_c:, :]
        for number, group in enumerate(groups):
            for other in range(n_row):
                source = planes[number * n_row + other]
                place = pl.multiple_of((row ^ other) * part_v, part_v)
                for i, flip in enumerate(group):
                    val_all[flip, pl.ds(place, part_v), :] = source[i * part_v:(i + 1) * part_v, :]
        total[...] = jnp.zeros_like(total)

    columns = pl.ds(pl.multiple_of(step * tile, tile), tile)
    for flip in range(n_ka):
        by_point = lax.dot_general(
            cond_all[flip, :, columns], x_all[flip],
            (((0,), (1,)), ((), ())), preferred_element_type=F32,
        ).astype(BF16)
        for b in range(n_b):
            panels[flip, b * tile:(b + 1) * tile, :] = by_point[:, b * n_v:(b + 1) * n_v]
    for j in range(n_nu // chunk):
        at = slice(j * chunk, (j + 1) * chunk)
        direct = None
        for flip in range(n_ka):
            pairs = jnp.dot(panels[flip], val_all[flip, :, at], preferred_element_type=F32)
            weights = w_ref[q_ref[me ^ flip, me], :, at].astype(F32)
            term = pairs.reshape(n_b, tile, chunk) * weights[None]
            direct = term if direct is None else direct + term
        direct = direct.reshape(n_b * tile, chunk).astype(BF16)
        sums = lax.dot_general(
            direct, val_ref[:, at], (((1,), (1,)), ((), ())), preferred_element_type=F32
        )
        if j == 0:
            half[...] = sums
        else:
            half[...] += sums
    cond_tile = cond_ref[:, columns]
    for b in range(n_b):
        total[b] += lax.dot_general(
            half[b * tile:(b + 1) * tile, :].astype(BF16), cond_tile,
            (((0,), (1,)), ((), ())), preferred_element_type=F32,
        )

    @pl.when(step == pl.num_programs(0) - 1)
    def finish():
        part = n_v // n_col
        for other in range(n_col):
            place = pl.multiple_of((col ^ other) * part, part)
            value = total[:, pl.ds(place, part), :] * factor
            if other == 0:
                keep_ref[...] = value
            else:
                outs[other - 1][...] = value.astype(BF16)


def local(sizes, exciton, orb_cond, orb_val, screened, q_table):
    n_ka, n_row, n_col = sizes
    n_b, n_v, n_c = exciton.shape[1:]
    cond, val = orb_cond[0], orb_val[0]
    n_mu, n_nu = cond.shape[1], val.shape[1]
    x_rows = exciton.reshape(n_b * n_v, n_c)
    core_rows = (n_c * n_mu // LANES + x_rows.shape[0]) // n_col
    core, plane = pl.pallas_call(
        functools.partial(pack_kernel, (n_row, n_col)),
        out_shape=(
            jax.ShapeDtypeStruct((core_rows, LANES), BF16),
            jax.ShapeDtypeStruct((n_v // n_row, n_nu), BF16),
        ),
        name="pack",
    )(x_rows, cond, val)
    by_flip = [(core, plane)]
    for flip in range(1, n_ka):
        last = flip & -flip
        core, plane = by_flip[flip - last]
        by_flip.append((swap(core, "ka", n_ka, last), swap(plane, "ka", n_ka, last)))
    groups = []
    for count in range(1, n_ka.bit_length()):
        groups.append([flip for flip in range(1, n_ka) if flip.bit_count() == count])
    planes = []
    for group in groups:
        joined = join([by_flip[flip][1] for flip in group])
        planes += [joined] + [swap(joined, "row", n_row, d) for d in range(1, n_row)]
    cores = []
    for core, _ in by_flip[1:]:
        cores += [core] + [swap(core, "col", n_col, d) for d in range(1, n_col)]

    factor = math.sqrt(n_v * n_c) / (n_mu * n_row)
    tile = 128
    chunk = 256
    part = n_v // n_col
    whole = pl.BlockSpec(memory_space=pltpu.VMEM)
    kept, *sent = pl.pallas_call(
        functools.partial(main_kernel, sizes, groups, factor, tile, chunk),
        grid=(n_mu // tile,),
        in_specs=[pl.BlockSpec(memory_space=pltpu.SMEM), whole, whole, whole,
                  pl.BlockSpec((screened.shape[0], tile, n_nu), lambda i: (0, i, 0))]
        + [whole] * (len(cores) + len(planes)),
        out_specs=[whole] * n_col,
        out_shape=[jax.ShapeDtypeStruct((n_b, part, n_c), F32)]
        + [jax.ShapeDtypeStruct((n_b, part, n_c), BF16)] * (n_col - 1),
        scratch_shapes=[
            pltpu.VMEM((n_ka, n_b * n_v, n_c), BF16),
            pltpu.VMEM((n_ka, n_c, n_mu), BF16),
            pltpu.VMEM((n_ka, n_v, n_nu), BF16),
            pltpu.VMEM((n_ka, n_b * tile, n_v), BF16),
            pltpu.VMEM((n_b * tile, n_v), F32),
            pltpu.VMEM((n_b, n_v, n_c), F32),
        ],
        compiler_params=pltpu.CompilerParams(vmem_limit_bytes=60 * 2**20),
        name="direct_term",
    )(q_table, x_rows, cond, val, screened, *cores, *planes)
    mine = kept
    for flip in range(1, n_col):
        mine = mine + swap(sent[flip - 1], "col", n_col, flip).astype(F32)
    mine = mine.astype(BF16)
    terms = [mine] + [swap(mine, "row", n_row, flip) for flip in range(1, n_row)]
    terms = [term.astype(F32) for term in terms]
    while len(terms) > 1:
        terms = [a + b for a, b in zip(terms[::2], terms[1::2])]
    return terms[0][None]


def solution(mesh):
    placed = (
        P("ka", None, None, None),
        P("ka", None, "row"),
        P("ka", None, "col"),
        P(None, "row", "col"),
        P(),
    )
    sizes = tuple(mesh.shape[name] for name in ("ka", "row", "col"))
    return jax.shard_map(
        functools.partial(local, sizes), mesh=mesh, in_specs=placed,
        out_specs=P("ka", None, "col", None), check_vma=False,
    )
```

```python
import functools
import math

import jax
import jax.numpy as jnp
from jax import lax
from jax.experimental import pallas as pl
from jax.experimental.pallas import tpu as pltpu
from jax.sharding import PartitionSpec as P

BF16 = jnp.bfloat16
F32 = jnp.float32
LANES = 128
ROWS = 16


def swap(value, axis, size, flip):
    return lax.ppermute(value, axis, [(i, i ^ flip) for i in range(size)])


def run(copies):
    for copy in copies:
        copy.start()
    for copy in copies:
        copy.wait()


def pack_plane_kernel(n_row, val_ref, plane_ref, sem):
    part = plane_ref.shape[0]
    rows = pl.ds(pl.multiple_of(lax.axis_index("row") * part, part), part)
    run([pltpu.make_async_copy(val_ref.at[rows, :], plane_ref, sem)])


def pack_core_kernel(n_col, exciton_ref, cond_ref, after_ref, core_ref, sems):
    col = lax.axis_index("col")
    part = cond_ref.shape[0] // n_col
    blocks = cond_ref.shape[1] // LANES
    rows = pl.ds(pl.multiple_of(col * part, part), part)
    copies = [
        pltpu.make_async_copy(
            cond_ref.at[rows, block * LANES:(block + 1) * LANES],
            core_ref.at[block * part:(block + 1) * part, :], sems.at[block],
        )
        for block in range(blocks)
    ]
    part_x = exciton_ref.shape[0] // n_col
    rows = pl.ds(pl.multiple_of(col * part_x, part_x), part_x)
    copies.append(pltpu.make_async_copy(
        exciton_ref.at[rows, :], core_ref.at[blocks * part:, :], sems.at[blocks]
    ))
    run(copies)


def join_kernel(*refs):
    *parts, out = refs
    at = 0
    for part in parts:
        out[at:at + part.shape[0], :] = part[...]
        at += part.shape[0]


def join(parts):
    if len(parts) == 1:
        return parts[0]
    rows = sum(part.shape[0] for part in parts)
    return pl.pallas_call(
        join_kernel, out_shape=jax.ShapeDtypeStruct((rows, parts[0].shape[1]), BF16), name="join"
    )(*parts)


def load_kernel(q_ref, exciton_ref, cond_ref, val_ref, w_ref, after_ref, x, cond, val, w, sems):
    me = lax.axis_index("ka")
    n_ka = w.shape[0]
    copies = [
        pltpu.make_async_copy(w_ref.at[q_ref[me ^ flip, me]], w.at[flip], sems.at[flip])
        for flip in range(n_ka)
    ]
    for i, (source, target) in enumerate(((exciton_ref, x), (cond_ref, cond), (val_ref, val))):
        copies.append(pltpu.make_async_copy(source, target, sems.at[n_ka + i]))
    run(copies)


def main_kernel(sizes, groups, factor, tile, chunk, *refs):
    n_ka, n_row, n_col = sizes
    exciton_ref, cond_ref, val_ref, w = refs[:4]
    n_core, n_plane = (n_ka - 1) * n_col, len(groups) * n_row
    cores = refs[4:4 + n_core]
    planes = refs[4 + n_core:4 + n_core + n_plane]
    keep_ref = refs[4 + n_core + n_plane]
    outs = refs[5 + n_core + n_plane:4 + n_core + n_plane + n_col]
    x_all, cond_all, val_all, panels, products, direct, total = refs[-7:]
    row, col = lax.axis_index("row"), lax.axis_index("col")
    n_v, n_nu = val_ref.shape
    n_c, n_mu = cond_ref.shape
    n_b = exciton_ref.shape[0] // n_v
    n_tiles, n_slots = n_mu // tile, products.shape[0]

    x_all[0] = exciton_ref[...]
    cond_all[0] = cond_ref[...]
    val_all[0] = val_ref[...]
    part_c, part_v, part_x = n_c // n_col, n_v // n_row, exciton_ref.shape[0] // n_col
    blocks = n_mu // LANES
    for flip in range(1, n_ka):
        for other in range(n_col):
            source = cores[(flip - 1) * n_col + other]
            place = pl.multiple_of((col ^ other) * part_c, part_c)
            for block in range(blocks):
                cond_all[flip, pl.ds(place, part_c), block * LANES:(block + 1) * LANES] = source[
                    block * part_c:(block + 1) * part_c, :
                ]
            place = pl.multiple_of((col ^ other) * part_x, part_x)
            x_all[flip, pl.ds(place, part_x), :] = source[blocks * part_c:, :]
    for number, group in enumerate(groups):
        for other in range(n_row):
            source = planes[number * n_row + other]
            place = pl.multiple_of((row ^ other) * part_v, part_v)
            for i, flip in enumerate(group):
                val_all[flip, pl.ds(place, part_v), :] = source[i * part_v:(i + 1) * part_v, :]
    total[...] = jnp.zeros_like(total)

    @pl.loop(0, n_tiles)
    def one_tile(number):
        start = pl.multiple_of(number * tile, tile)
        columns = pl.ds(start, tile)
        for flip in range(n_ka):
            by_point = lax.dot_general(
                cond_all[flip, :, columns], x_all[flip],
                (((0,), (1,)), ((), ())), preferred_element_type=F32,
            ).astype(BF16)
            for b in range(n_b):
                panels[flip, b * tile:(b + 1) * tile, :] = by_point[:, b * n_v:(b + 1) * n_v]
        for j in range(n_nu // chunk):
            at = slice(j * chunk, (j + 1) * chunk)
            slot = j % n_slots
            for flip in range(n_ka):
                products[slot, flip] = jnp.dot(
                    panels[flip], val_all[flip, :, at], preferred_element_type=F32
                )
            for m in range(0, tile, ROWS):
                weights = [
                    w[flip, pl.ds(start + m, ROWS), at].astype(F32) for flip in range(n_ka)
                ]
                for b in range(n_b):
                    rows = slice(b * tile + m, b * tile + m + ROWS)
                    value = products[slot, 0, rows, :] * weights[0]
                    for flip in range(1, n_ka):
                        value += products[slot, flip, rows, :] * weights[flip]
                    direct[rows, at] = value.astype(BF16)
        half = lax.dot_general(
            direct[...], val_all[0], (((1,), (1,)), ((), ())), preferred_element_type=F32
        ).astype(BF16)
        cond_tile = cond_all[0, :, columns]
        for b in range(n_b):
            total[b] += lax.dot_general(
                half[b * tile:(b + 1) * tile, :], cond_tile,
                (((0,), (1,)), ((), ())), preferred_element_type=F32,
            )

    part = n_v // n_col
    for other in range(n_col):
        place = pl.multiple_of((col ^ other) * part, part)
        value = total[:, pl.ds(place, part), :] * factor
        if other == 0:
            keep_ref[...] = value
        else:
            outs[other - 1][...] = value.astype(BF16)


def local(sizes, exciton, orb_cond, orb_val, screened, q_table):
    n_ka, n_row, n_col = sizes
    n_b, n_v, n_c = exciton.shape[1:]
    cond, val = orb_cond[0], orb_val[0]
    n_mu, n_nu = cond.shape[1], val.shape[1]
    x_rows, cond, val, screened, q_table = (
        pltpu.with_memory_space_constraint(array, pltpu.HBM)
        for array in (exciton.reshape(n_b * n_v, n_c), cond, val, screened, q_table)
    )
    core_rows = (n_c * n_mu // LANES + x_rows.shape[0]) // n_col
    in_hbm, in_vmem = pl.BlockSpec(memory_space=pltpu.HBM), pl.BlockSpec(memory_space=pltpu.VMEM)
    plane = pl.pallas_call(
        functools.partial(pack_plane_kernel, n_row),
        in_specs=[in_hbm],
        out_specs=in_vmem,
        out_shape=jax.ShapeDtypeStruct((n_v // n_row, n_nu), BF16),
        scratch_shapes=[pltpu.SemaphoreType.DMA],
        name="pack_plane",
    )(val)
    planes_by_flip = [plane]
    for flip in range(1, n_ka):
        last = flip & -flip
        planes_by_flip.append(swap(planes_by_flip[flip - last], "ka", n_ka, last))
    core = pl.pallas_call(
        functools.partial(pack_core_kernel, n_col),
        in_specs=[in_hbm, in_hbm, pl.BlockSpec(memory_space=pl.ANY)],
        out_specs=in_vmem,
        out_shape=jax.ShapeDtypeStruct((core_rows, LANES), BF16),
        scratch_shapes=[pltpu.SemaphoreType.DMA((n_mu // LANES + 1,))],
        name="pack_core",
    )(x_rows, cond, planes_by_flip[1])
    cores_by_flip = [core]
    for flip in range(1, n_ka):
        last = flip & -flip
        cores_by_flip.append(swap(cores_by_flip[flip - last], "ka", n_ka, last))
    own_blocks = pl.pallas_call(
        load_kernel,
        in_specs=[pl.BlockSpec(memory_space=pltpu.SMEM)] + [in_hbm] * 4
        + [pl.BlockSpec(memory_space=pl.ANY)],
        out_specs=[in_vmem] * 4,
        out_shape=[
            jax.ShapeDtypeStruct(block.shape, BF16) for block in (x_rows, cond, val, screened)
        ],
        scratch_shapes=[pltpu.SemaphoreType.DMA((n_ka + 3,))],
        cost_estimate=pl.CostEstimate(
            flops=0, bytes_accessed=4 * screened.size, transcendentals=0
        ),
        name="load",
    )(q_table, x_rows, cond, val, screened, cores_by_flip[n_ka // 2])
    groups = []
    for count in range(1, n_ka.bit_length()):
        groups.append([flip for flip in range(1, n_ka) if flip.bit_count() == count])
    planes = []
    for group in groups:
        joined = join([planes_by_flip[flip] for flip in group])
        planes += [joined] + [swap(joined, "row", n_row, d) for d in range(1, n_row)]
    cores = []
    for core in cores_by_flip[1:]:
        cores += [core] + [swap(core, "col", n_col, d) for d in range(1, n_col)]

    factor = math.sqrt(n_v * n_c) / (n_mu * n_row)
    tile = 128
    chunk = 256
    part = n_v // n_col
    slots = min(2, n_nu // chunk)
    kept, *sent = pl.pallas_call(
        functools.partial(main_kernel, sizes, groups, factor, tile, chunk),
        in_specs=[in_vmem] * (4 + len(cores) + len(planes)),
        out_specs=[in_vmem] * n_col,
        out_shape=[jax.ShapeDtypeStruct((n_b, part, n_c), F32)]
        + [jax.ShapeDtypeStruct((n_b, part, n_c), BF16)] * (n_col - 1),
        scratch_shapes=[
            pltpu.VMEM((n_ka, n_b * n_v, n_c), BF16),
            pltpu.VMEM((n_ka, n_c, n_mu), BF16),
            pltpu.VMEM((n_ka, n_v, n_nu), BF16),
            pltpu.VMEM((n_ka, n_b * tile, n_v), BF16),
            pltpu.VMEM((slots, n_ka, n_b * tile, chunk), F32),
            pltpu.VMEM((n_b * tile, n_nu), BF16),
            pltpu.VMEM((n_b, n_v, n_c), F32),
        ],
        compiler_params=pltpu.CompilerParams(vmem_limit_bytes=28 * 2**20),
        name="direct_term",
    )(*own_blocks, *cores, *planes)
    mine = kept
    for flip in range(1, n_col):
        mine = mine + swap(sent[flip - 1], "col", n_col, flip).astype(F32)
    mine = mine.astype(BF16)
    terms = [mine] + [swap(mine, "row", n_row, flip) for flip in range(1, n_row)]
    terms = [term.astype(F32) for term in terms]
    while len(terms) > 1:
        terms = [a + b for a, b in zip(terms[::2], terms[1::2])]
    return terms[0][None]


def solution(mesh):
    placed = (
        P("ka", None, None, None),
        P("ka", None, "row"),
        P("ka", None, "col"),
        P(None, "row", "col"),
        P(),
    )
    sizes = tuple(mesh.shape[name] for name in ("ka", "row", "col"))
    return jax.shard_map(
        functools.partial(local, sizes), mesh=mesh, in_specs=placed,
        out_specs=P("ka", None, "col", None), check_vma=False,
    )
```

```python
import functools
import math

import jax
import jax.numpy as jnp
from jax import lax
from jax.experimental import pallas as pl
from jax.experimental.pallas import tpu as pltpu
from jax.sharding import PartitionSpec as P

BF16 = jnp.bfloat16
F32 = jnp.float32
LANES = 128
ROWS = 16
TILE = 128
CHUNK = 256
MIB = 2**20
IN_HBM = pl.BlockSpec(memory_space=pltpu.HBM)
IN_VMEM = pl.BlockSpec(memory_space=pltpu.VMEM)
IN_SMEM = pl.BlockSpec(memory_space=pltpu.SMEM)


def swap(value, axis, size, flip):
    return lax.ppermute(value, axis, [(i, i ^ flip) for i in range(size)])


def run(copies):
    for copy in copies:
        copy.start()
    for copy in copies:
        copy.wait()


def pack_kernel(sizes, exciton_ref, cond_ref, val_ref, slab_ref, sems):
    n_row, n_col = sizes
    row, col = lax.axis_index("row"), lax.axis_index("col")
    copies, at = [], 0
    for source, place, count in ((cond_ref, col, n_col), (exciton_ref, col, n_col), (val_ref, row, n_row)):
        part = source.shape[0] // count
        rows = pl.ds(pl.multiple_of(place * part, part), part)
        for block in range(source.shape[1] // LANES):
            copies.append(pltpu.make_async_copy(
                source.at[rows, block * LANES:(block + 1) * LANES],
                slab_ref.at[at:at + part, :], sems.at[len(copies)],
            ))
            at += part
    run(copies)


def join_kernel(rows, *refs):
    *slabs, out = refs
    for i, slab in enumerate(slabs):
        out[i * rows:(i + 1) * rows, :] = slab[slab.shape[0] - rows:, :]


def join(slabs, rows):
    return pl.pallas_call(
        functools.partial(join_kernel, rows),
        in_specs=[IN_VMEM] * len(slabs),
        out_specs=IN_VMEM,
        out_shape=jax.ShapeDtypeStruct((rows * len(slabs), LANES), BF16),
        compiler_params=pltpu.CompilerParams(vmem_limit_bytes=4 * MIB),
        name="join",
    )(*slabs)


class Group:
    def __init__(self, flips, first, last, last_flips):
        self.flips, self.first, self.last, self.last_flips = flips, first, last, last_flips
        self.all_flips = ((0,) if first else ()) + tuple(flips)
        self.ahead = first and not last


def direct_kernel(sizes, group, factor, *refs):
    n_ka, n_row, n_col = sizes
    refs = list(refs)

    def take(count):
        taken, refs[:] = refs[:count], refs[count:]
        return taken

    q_ref, w_ref, exciton_ref, cond_ref, val_ref = take(5)
    slabs = [take(n_col) for _ in group.flips]
    planes = take(n_row)
    if not group.first:
        running, = take(1)
        w_here, cond_own, val_own = take(3)
    if group.last:
        keep, *sent = take(n_col)
    else:
        summed, = take(1)
    if group.ahead:
        w_next, cond_next, val_next = take(3)
    x_all, cond_all, val_all, panels, products, w, sems = take(7)
    if group.last:
        direct, total = take(2)
    me, row, col = (lax.axis_index(name) for name in ("ka", "row", "col"))
    n_v, n_nu = val_ref.shape
    n_c, n_mu = cond_ref.shape
    n_b = exciton_ref.shape[0] // n_v
    n_tiles, n_slots = n_mu // TILE, products.shape[0]
    n_flips = len(group.all_flips)
    preloaded = group.last and not group.first

    def weight_copies(number):
        rows = pl.ds(pl.multiple_of(number * TILE, TILE), TILE)
        return [
            pltpu.make_async_copy(
                w_ref.at[q_ref[me ^ flip, me], rows, :], w.at[i, rows, :], sems.at[number, i]
            )
            for i, flip in enumerate(group.all_flips)
        ]

    own = []
    if group.first:
        own += [(exciton_ref, x_all.at[0]), (cond_ref, cond_all.at[0]), (val_ref, val_all.at[0])]
    own = [
        pltpu.make_async_copy(source, target, sems.at[n_tiles, i])
        for i, (source, target) in enumerate(own)
    ]
    ahead = []
    if group.ahead:
        ahead = [(cond_ref, cond_next), (val_ref, val_next)] + [
            (w_ref.at[q_ref[me ^ flip, me]], w_next.at[i]) for i, flip in enumerate(group.last_flips)
        ]
        ahead = [
            pltpu.make_async_copy(source, target, sems.at[n_tiles + 1, i])
            for i, (source, target) in enumerate(ahead)
        ]
    for copy in own:
        copy.start()
    if not preloaded:
        for number in range(n_tiles):
            for copy in weight_copies(number):
                copy.start()
    for copy in ahead:
        copy.start()

    part_c, part_x, part_v = n_c // n_col, exciton_ref.shape[0] // n_col, n_v // n_row
    for i, flip in enumerate(group.flips):
        place = i + group.first
        for other in range(n_col):
            source, at = slabs[i][other], 0
            rows = pl.ds(pl.multiple_of((col ^ other) * part_c, part_c), part_c)
            for block in range(n_mu // LANES):
                cond_all[place, rows, block * LANES:(block + 1) * LANES] = source[at:at + part_c, :]
                at += part_c
            rows = pl.ds(pl.multiple_of((col ^ other) * part_x, part_x), part_x)
            x_all[place, rows, :] = source[at:at + part_x, :]
        for other in range(n_row):
            at = i * (planes[other].shape[0] // len(group.flips))
            rows = pl.ds(pl.multiple_of((row ^ other) * part_v, part_v), part_v)
            for block in range(n_nu // LANES):
                val_all[place, rows, block * LANES:(block + 1) * LANES] = planes[other][at:at + part_v, :]
                at += part_v
    if group.last:
        total[...] = jnp.zeros_like(total)
    for copy in own:
        copy.wait()
    if group.first:
        cond_own, val_own = cond_all.at[0], val_all.at[0]
    weights_of = w_here if preloaded else w

    @pl.loop(0, n_tiles)
    def one_tile(number):
        start = pl.multiple_of(number * TILE, TILE)
        columns = pl.ds(start, TILE)
        for i in range(n_flips):
            by_point = lax.dot_general(
                cond_all[i, :, columns], x_all[i],
                (((0,), (1,)), ((), ())), preferred_element_type=F32,
            ).astype(BF16)
            for b in range(n_b):
                panels[i, b * TILE:(b + 1) * TILE, :] = by_point[:, b * n_v:(b + 1) * n_v]
        if not preloaded:
            for copy in weight_copies(number):
                copy.wait()
        for j in range(n_nu // CHUNK):
            at = slice(j * CHUNK, (j + 1) * CHUNK)
            slot = j % n_slots
            for i in range(n_flips):
                products[slot, i] = jnp.dot(
                    panels[i], val_all[i, :, at], preferred_element_type=F32
                )
            for m in range(0, TILE, ROWS):
                weights = [
                    weights_of[i, pl.ds(start + m, ROWS), at].astype(F32) for i in range(n_flips)
                ]
                for b in range(n_b):
                    rows = slice(b * TILE + m, b * TILE + m + ROWS)
                    at_rows = pl.ds(pl.multiple_of(number * n_b * TILE, TILE) + b * TILE + m, ROWS)
                    value = products[slot, 0, rows, :] * weights[0]
                    for i in range(1, n_flips):
                        value += products[slot, i, rows, :] * weights[i]
                    if not group.first:
                        value += running[at_rows, at]
                    if group.last:
                        direct[rows, at] = value.astype(BF16)
                    else:
                        summed[at_rows, at] = value
        if group.last:
            half = lax.dot_general(
                direct[...], val_own[...], (((1,), (1,)), ((), ())), preferred_element_type=F32
            ).astype(BF16)
            cond_tile = cond_own[:, columns]
            for b in range(n_b):
                total[b] += lax.dot_general(
                    half[b * TILE:(b + 1) * TILE, :], cond_tile,
                    (((0,), (1,)), ((), ())), preferred_element_type=F32,
                )

    for copy in ahead:
        copy.wait()
    if group.last:
        part = n_v // n_col
        for other in range(n_col):
            place = pl.multiple_of((col ^ other) * part, part)
            value = total[:, pl.ds(place, part), :] * factor
            if other == 0:
                keep[...] = value
            else:
                sent[other - 1][...] = value.astype(BF16)


def local(sizes, exciton, orb_cond, orb_val, screened, q_table):
    n_ka, n_row, n_col = sizes
    n_b, n_v, n_c = exciton.shape[1:]
    x_rows, cond, val, screened, q_table = (
        pltpu.with_memory_space_constraint(array, pltpu.HBM)
        for array in (exciton.reshape(n_b * n_v, n_c), orb_cond[0], orb_val[0], screened, q_table)
    )
    n_mu, n_nu = cond.shape[1], val.shape[1]
    plane_rows = val.size // n_row // LANES
    slab_rows = (cond.size + x_rows.size) // n_col // LANES + plane_rows
    slab = pl.pallas_call(
        functools.partial(pack_kernel, (n_row, n_col)),
        in_specs=[IN_HBM] * 3,
        out_specs=IN_VMEM,
        out_shape=jax.ShapeDtypeStruct((slab_rows, LANES), BF16),
        scratch_shapes=[pltpu.SemaphoreType.DMA(((n_mu + n_nu + n_c) // LANES,))],
        compiler_params=pltpu.CompilerParams(vmem_limit_bytes=4 * MIB),
        name="pack",
    )(x_rows, cond, val)
    slabs = [slab]
    for flip in range(1, n_ka):
        last = flip & -flip
        slabs.append(swap(slabs[flip - last], "ka", n_ka, last))

    by_count = [
        [flip for flip in range(1, n_ka) if flip.bit_count() == count]
        for count in range(1, n_ka.bit_length())
    ]
    factor = math.sqrt(n_v * n_c) / (n_mu * n_row)
    part = n_v // n_col
    slots = min(2, n_nu // CHUNK)
    running, carried = [], []
    for number, flips in enumerate(by_count):
        group = Group(flips, number == 0, number == len(by_count) - 1, by_count[-1])
        joined = join([slabs[flip] for flip in flips], plane_rows)
        operands = [
            swap(slabs[flip], "col", n_col, d) if d else slabs[flip]
            for flip in flips for d in range(n_col)
        ]
        operands += [swap(joined, "row", n_row, d) if d else joined for d in range(n_row)]
        operands += running
        if not group.first:
            operands += carried
        count = len(group.all_flips)
        n_tiles = n_mu // TILE
        sums = jax.ShapeDtypeStruct((n_b * n_mu, n_nu), F32)
        if group.last:
            out_shape = [jax.ShapeDtypeStruct((n_b, part, n_c), F32)]
            out_shape += [jax.ShapeDtypeStruct((n_b, part, n_c), BF16)] * (n_col - 1)
        else:
            out_shape = [sums]
        if group.ahead:
            out_shape += [
                jax.ShapeDtypeStruct((len(by_count[-1]), n_mu, n_nu), BF16),
                jax.ShapeDtypeStruct(cond.shape, BF16),
                jax.ShapeDtypeStruct(val.shape, BF16),
            ]
        own_weights = (1, ROWS, LANES) if group.last and not group.first else (count, n_mu, n_nu)
        scratch = [
            pltpu.VMEM((count, n_b * n_v, n_c), BF16),
            pltpu.VMEM((count, n_c, n_mu), BF16),
            pltpu.VMEM((count, n_v, n_nu), BF16),
            pltpu.VMEM((count, n_b * TILE, n_v), BF16),
            pltpu.VMEM((slots, count, n_b * TILE, CHUNK), F32),
            pltpu.VMEM(own_weights, BF16),
            pltpu.SemaphoreType.DMA((n_tiles + 2, max(count, 3, len(by_count[-1]) + 2))),
        ]
        if group.last:
            scratch += [pltpu.VMEM((n_b * TILE, n_nu), BF16), pltpu.VMEM((n_b, n_v, n_c), F32)]
        work = 2 * count * n_b * n_mu * n_nu * n_v
        outputs = pl.pallas_call(
            functools.partial(direct_kernel, sizes, group, factor),
            in_specs=[IN_SMEM] + [IN_HBM] * 4 + [IN_VMEM] * len(operands),
            out_specs=[IN_VMEM] * len(out_shape),
            out_shape=out_shape,
            scratch_shapes=scratch,
            compiler_params=pltpu.CompilerParams(vmem_limit_bytes=28 * MIB),
            cost_estimate=pl.CostEstimate(
                flops=4 * work, bytes_accessed=2 * screened.size, transcendentals=0
            ),
            name="direct_last" if group.last else "direct_sum",
        )(q_table, screened, x_rows, cond, val, *operands)
        if group.last:
            kept, *sent = outputs
        else:
            running = outputs[:1]
        if group.ahead:
            carried = outputs[1:]

    mine = kept
    for flip in range(1, n_col):
        mine = mine + swap(sent[flip - 1], "col", n_col, flip).astype(F32)
    mine = mine.astype(BF16)
    terms = [mine] + [swap(mine, "row", n_row, flip) for flip in range(1, n_row)]
    terms = [term.astype(F32) for term in terms]
    while len(terms) > 1:
        terms = [a + b for a, b in zip(terms[::2], terms[1::2])]
    return terms[0][None]


def solution(mesh):
    placed = (
        P("ka", None, None, None),
        P("ka", None, "row"),
        P("ka", None, "col"),
        P(None, "row", "col"),
        P(),
    )
    sizes = tuple(mesh.shape[name] for name in ("ka", "row", "col"))
    return jax.shard_map(
        functools.partial(local, sizes), mesh=mesh, in_specs=placed,
        out_specs=P("ka", None, "col", None), check_vma=False,
    )
```

```python
import functools
import math

import jax
import jax.numpy as jnp
from jax import lax
from jax.experimental import pallas as pl
from jax.experimental.pallas import tpu as pltpu
from jax.sharding import PartitionSpec as P

BF16 = jnp.bfloat16
F32 = jnp.float32
LANES = 128
ROWS = 16
TILE = 128
CHUNK = 256
MIB = 2**20
JOIN_FLOPS = 2 * 10**10
SPREAD_FLOPS = 2 * 10**10
IN_HBM = pl.BlockSpec(memory_space=pltpu.HBM)
IN_VMEM = pl.BlockSpec(memory_space=pltpu.VMEM)
IN_SMEM = pl.BlockSpec(memory_space=pltpu.SMEM)


def swap(value, axis, size, flip):
    return lax.ppermute(value, axis, [(i, i ^ flip) for i in range(size)])


def run(copies):
    for copy in copies:
        copy.start()
    for copy in copies:
        copy.wait()


def pack_kernel(sizes, exciton_ref, cond_ref, val_ref, core_ref, plane_ref, sems):
    n_row, n_col = sizes
    row, col = lax.axis_index("row"), lax.axis_index("col")
    part = plane_ref.shape[0]
    rows = pl.ds(pl.multiple_of(row * part, part), part)
    copies, at = [pltpu.make_async_copy(val_ref.at[rows, :], plane_ref, sems.at[0])], 0
    for source in (cond_ref, exciton_ref):
        part = source.shape[0] // n_col
        rows = pl.ds(pl.multiple_of(col * part, part), part)
        for block in range(source.shape[1] // LANES):
            copies.append(pltpu.make_async_copy(
                source.at[rows, block * LANES:(block + 1) * LANES],
                core_ref.at[at:at + part, :], sems.at[len(copies)],
            ))
            at += part
    run(copies)


def join_kernel(*refs):
    *parts, out = refs
    at = 0
    for part in parts:
        out[at:at + part.shape[0], :] = part[...]
        at += part.shape[0]


def join(parts):
    shape = (sum(part.shape[0] for part in parts), parts[0].shape[1])
    return pl.pallas_call(
        join_kernel,
        in_specs=[IN_VMEM] * len(parts),
        out_specs=IN_VMEM,
        out_shape=jax.ShapeDtypeStruct(shape, BF16),
        compiler_params=pltpu.CompilerParams(vmem_limit_bytes=4 * MIB),
        cost_estimate=pl.CostEstimate(flops=JOIN_FLOPS, bytes_accessed=0, transcendentals=0),
        name="join",
    )(*parts)


def spread_kernel(n_row, *refs):
    *parts, out = refs
    row = lax.axis_index("row")
    part = out.shape[1] // n_row
    for other in range(n_row):
        rows = pl.ds(pl.multiple_of((row ^ other) * part, part), part)
        for flip in range(out.shape[0]):
            out[flip, rows, :] = parts[other][flip * part:(flip + 1) * part, :]


def gate_kernel(*refs):
    del refs


def after(value, *others):
    return pl.pallas_call(
        gate_kernel,
        in_specs=[pl.BlockSpec(memory_space=pl.ANY)] * (1 + len(others)),
        out_specs=pl.BlockSpec(memory_space=pl.ANY),
        out_shape=jax.ShapeDtypeStruct(value.shape, value.dtype),
        input_output_aliases={0: 0},
        compiler_params=pltpu.CompilerParams(vmem_limit_bytes=MIB),
        name="after",
    )(value, *others)


def direct_kernel(sizes, factor, *refs):
    n_ka, n_row, n_col = sizes
    refs = list(refs)

    def take(count):
        taken, refs[:] = refs[:count], refs[count:]
        return taken

    q_ref, w_ref, exciton_ref, cond_ref, val_ref = take(5)
    cores = [take(n_col) for _ in range(1, n_ka)]
    spread_ref, = take(1)
    keep, *sent = take(n_col)
    x_all, cond_all, val_all, panels, products, w, direct, total, sems = refs
    me, col = lax.axis_index("ka"), lax.axis_index("col")
    n_v, n_nu = val_ref.shape
    n_c, n_mu = cond_ref.shape
    n_b = exciton_ref.shape[0] // n_v
    n_tiles, n_slots = n_mu // TILE, products.shape[0]

    def weight_copies(number):
        rows = pl.ds(pl.multiple_of(number * TILE, TILE), TILE)
        return [
            pltpu.make_async_copy(
                w_ref.at[q_ref[me ^ flip, me], rows, :], w.at[flip, rows, :], sems.at[number, flip]
            )
            for flip in range(n_ka)
        ]

    own = [
        pltpu.make_async_copy(source, target.at[0], sems.at[n_tiles, i])
        for i, (source, target) in enumerate(
            ((exciton_ref, x_all), (cond_ref, cond_all), (val_ref, val_all))
        )
    ]
    for copy in own:
        copy.start()
    for number in range(n_tiles):
        for copy in weight_copies(number):
            copy.start()

    part_c, part_x = n_c // n_col, exciton_ref.shape[0] // n_col
    for flip in range(1, n_ka):
        for other in range(n_col):
            source, at = cores[flip - 1][other], 0
            rows = pl.ds(pl.multiple_of((col ^ other) * part_c, part_c), part_c)
            for block in range(n_mu // LANES):
                cond_all[flip, rows, block * LANES:(block + 1) * LANES] = source[at:at + part_c, :]
                at += part_c
            rows = pl.ds(pl.multiple_of((col ^ other) * part_x, part_x), part_x)
            x_all[flip, rows, :] = source[at:at + part_x, :]
    val_all[1:] = spread_ref[...]
    total[...] = jnp.zeros_like(total)
    for copy in own:
        copy.wait()

    @pl.loop(0, n_tiles)
    def one_tile(number):
        start = pl.multiple_of(number * TILE, TILE)
        columns = pl.ds(start, TILE)
        for flip in range(n_ka):
            by_point = lax.dot_general(
                cond_all[flip, :, columns], x_all[flip],
                (((0,), (1,)), ((), ())), preferred_element_type=F32,
            ).astype(BF16)
            for b in range(n_b):
                panels[flip, b * TILE:(b + 1) * TILE, :] = by_point[:, b * n_v:(b + 1) * n_v]
        for copy in weight_copies(number):
            copy.wait()
        for j in range(n_nu // CHUNK):
            at = slice(j * CHUNK, (j + 1) * CHUNK)
            slot = j % n_slots
            for flip in range(n_ka):
                products[slot, flip] = jnp.dot(
                    panels[flip], val_all[flip, :, at], preferred_element_type=F32
                )
            for m in range(0, TILE, ROWS):
                weights = [
                    w[flip, pl.ds(start + m, ROWS), at].astype(F32) for flip in range(n_ka)
                ]
                for b in range(n_b):
                    rows = slice(b * TILE + m, b * TILE + m + ROWS)
                    value = products[slot, 0, rows, :] * weights[0]
                    for flip in range(1, n_ka):
                        value += products[slot, flip, rows, :] * weights[flip]
                    direct[rows, at] = value.astype(BF16)
        half = lax.dot_general(
            direct[...], val_all[0], (((1,), (1,)), ((), ())), preferred_element_type=F32
        ).astype(BF16)
        cond_tile = cond_all[0, :, columns]
        for b in range(n_b):
            total[b] += lax.dot_general(
                half[b * TILE:(b + 1) * TILE, :], cond_tile,
                (((0,), (1,)), ((), ())), preferred_element_type=F32,
            )

    part = n_v // n_col
    for other in range(n_col):
        place = pl.multiple_of((col ^ other) * part, part)
        value = total[:, pl.ds(place, part), :] * factor
        if other == 0:
            keep[...] = value
        else:
            sent[other - 1][...] = value.astype(BF16)


def local(sizes, exciton, orb_cond, orb_val, screened, q_table):
    n_ka, n_row, n_col = sizes
    n_b, n_v, n_c = exciton.shape[1:]
    x_rows, cond, val, screened, q_table = (
        pltpu.with_memory_space_constraint(array, pltpu.HBM)
        for array in (exciton.reshape(n_b * n_v, n_c), orb_cond[0], orb_val[0], screened, q_table)
    )
    n_mu, n_nu = cond.shape[1], val.shape[1]
    core_rows = (cond.size + x_rows.size) // n_col // LANES
    core, plane = pl.pallas_call(
        functools.partial(pack_kernel, (n_row, n_col)),
        in_specs=[IN_HBM] * 3,
        out_specs=[IN_VMEM] * 2,
        out_shape=[
            jax.ShapeDtypeStruct((core_rows, LANES), BF16),
            jax.ShapeDtypeStruct((n_v // n_row, n_nu), BF16),
        ],
        scratch_shapes=[pltpu.SemaphoreType.DMA(((n_mu + n_c) // LANES + 1,))],
        compiler_params=pltpu.CompilerParams(vmem_limit_bytes=4 * MIB),
        name="pack",
    )(x_rows, cond, val)
    planes = [swap(plane, "ka", n_ka, flip) for flip in range(1, n_ka)]
    joined = join(planes)
    cores = [after(core, planes[0])]
    for flip in range(1, n_ka):
        last = flip & -flip
        cores.append(swap(cores[flip - last], "ka", n_ka, last))
        if flip == 2:
            cores[2] = after(cores[2], joined, cores[1])
    operands = []
    for core in cores[1:]:
        operands += [swap(core, "col", n_col, d) if d else core for d in range(n_col)]
    parts = [swap(joined, "row", n_row, d) if d else joined for d in range(n_row)]
    operands.append(pl.pallas_call(
        functools.partial(spread_kernel, n_row),
        in_specs=[IN_VMEM] * n_row,
        out_specs=IN_VMEM,
        out_shape=jax.ShapeDtypeStruct((n_ka - 1, *val.shape), BF16),
        compiler_params=pltpu.CompilerParams(vmem_limit_bytes=4 * MIB),
        cost_estimate=pl.CostEstimate(flops=SPREAD_FLOPS, bytes_accessed=0, transcendentals=0),
        name="spread",
    )(*parts))

    factor = math.sqrt(n_v * n_c) / (n_mu * n_row)
    part = n_v // n_col
    slots = min(2, n_nu // CHUNK)
    kept, *sent = pl.pallas_call(
        functools.partial(direct_kernel, sizes, factor),
        in_specs=[IN_SMEM] + [IN_HBM] * 4 + [IN_VMEM] * len(operands),
        out_specs=[IN_VMEM] * n_col,
        out_shape=[jax.ShapeDtypeStruct((n_b, part, n_c), F32)]
        + [jax.ShapeDtypeStruct((n_b, part, n_c), BF16)] * (n_col - 1),
        scratch_shapes=[
            pltpu.VMEM((n_ka, n_b * n_v, n_c), BF16),
            pltpu.VMEM((n_ka, n_c, n_mu), BF16),
            pltpu.VMEM((n_ka, n_v, n_nu), BF16),
            pltpu.VMEM((n_ka, n_b * TILE, n_v), BF16),
            pltpu.VMEM((slots, n_ka, n_b * TILE, CHUNK), F32),
            pltpu.VMEM((n_ka, n_mu, n_nu), BF16),
            pltpu.VMEM((n_b * TILE, n_nu), BF16),
            pltpu.VMEM((n_b, n_v, n_c), F32),
            pltpu.SemaphoreType.DMA((n_mu // TILE + 1, max(n_ka, 3))),
        ],
        compiler_params=pltpu.CompilerParams(vmem_limit_bytes=32 * MIB),
        name="direct_term",
    )(q_table, screened, x_rows, cond, val, *operands)
    mine = kept
    for flip in range(1, n_col):
        mine = mine + swap(sent[flip - 1], "col", n_col, flip).astype(F32)
    mine = mine.astype(BF16)
    terms = [mine] + [swap(mine, "row", n_row, flip) for flip in range(1, n_row)]
    terms = [term.astype(F32) for term in terms]
    while len(terms) > 1:
        terms = [a + b for a, b in zip(terms[::2], terms[1::2])]
    return terms[0][None]


def solution(mesh):
    placed = (
        P("ka", None, None, None),
        P("ka", None, "row"),
        P("ka", None, "col"),
        P(None, "row", "col"),
        P(),
    )
    sizes = tuple(mesh.shape[name] for name in ("ka", "row", "col"))
    return jax.shard_map(
        functools.partial(local, sizes), mesh=mesh, in_specs=placed,
        out_specs=P("ka", None, "col", None), check_vma=False,
    )
```

```python
import functools
import math

import jax
import jax.numpy as jnp
from jax import lax
from jax.experimental import pallas as pl
from jax.experimental.pallas import tpu as pltpu
from jax.sharding import PartitionSpec as P

BF16 = jnp.bfloat16
F32 = jnp.float32
LANES = 128
ROWS = 16
TILE = 128
CHUNK = 256
MIB = 2**20
JOIN_FLOPS = 2 * 10**10
SPREAD_FLOPS = 2 * 10**10
IN_HBM = pl.BlockSpec(memory_space=pltpu.HBM)
IN_VMEM = pl.BlockSpec(memory_space=pltpu.VMEM)
IN_SMEM = pl.BlockSpec(memory_space=pltpu.SMEM)


def swap(value, axis, size, flip):
    return lax.ppermute(value, axis, [(i, i ^ flip) for i in range(size)])


def run(copies):
    for copy in copies:
        copy.start()
    for copy in copies:
        copy.wait()


def pack_kernel(sizes, exciton_ref, cond_ref, val_ref, core_ref, plane_ref, sems):
    n_row, n_col = sizes
    row, col = lax.axis_index("row"), lax.axis_index("col")
    part = plane_ref.shape[0]
    rows = pl.ds(pl.multiple_of(row * part, part), part)
    copies, at = [pltpu.make_async_copy(val_ref.at[rows, :], plane_ref, sems.at[0])], 0
    for source in (cond_ref, exciton_ref):
        part = source.shape[0] // n_col
        rows = pl.ds(pl.multiple_of(col * part, part), part)
        for block in range(source.shape[1] // LANES):
            copies.append(pltpu.make_async_copy(
                source.at[rows, block * LANES:(block + 1) * LANES],
                core_ref.at[at:at + part, :], sems.at[len(copies)],
            ))
            at += part
    run(copies)


def join_kernel(*refs):
    *parts, out = refs
    at = 0
    for part in parts:
        out[at:at + part.shape[0], :] = part[...]
        at += part.shape[0]


def join(parts):
    shape = (sum(part.shape[0] for part in parts), parts[0].shape[1])
    return pl.pallas_call(
        join_kernel,
        in_specs=[IN_VMEM] * len(parts),
        out_specs=IN_VMEM,
        out_shape=jax.ShapeDtypeStruct(shape, BF16),
        compiler_params=pltpu.CompilerParams(vmem_limit_bytes=4 * MIB),
        cost_estimate=pl.CostEstimate(flops=JOIN_FLOPS, bytes_accessed=0, transcendentals=0),
        name="join",
    )(*parts)


def spread_kernel(n_row, *refs):
    *parts, out = refs
    row = lax.axis_index("row")
    part = out.shape[1] // n_row
    for other in range(n_row):
        rows = pl.ds(pl.multiple_of((row ^ other) * part, part), part)
        for flip in range(out.shape[0]):
            out[flip, rows, :] = parts[other][flip * part:(flip + 1) * part, :]


def load_kernel(q_ref, w_ref, exciton_ref, cond_ref, val_ref, after_ref, w, x, cond, val, sems):
    del after_ref
    me, n_ka = lax.axis_index("ka"), w.shape[0]
    pairs = [(w_ref.at[q_ref[me ^ flip, me]], w.at[flip]) for flip in range(n_ka)]
    pairs += [(exciton_ref, x), (cond_ref, cond), (val_ref, val)]
    run([
        pltpu.make_async_copy(source, target, sems.at[i])
        for i, (source, target) in enumerate(pairs)
    ])


def gate_kernel(*refs):
    del refs


def after(value, *others):
    return pl.pallas_call(
        gate_kernel,
        in_specs=[pl.BlockSpec(memory_space=pl.ANY)] * (1 + len(others)),
        out_specs=pl.BlockSpec(memory_space=pl.ANY),
        out_shape=jax.ShapeDtypeStruct(value.shape, value.dtype),
        input_output_aliases={0: 0},
        compiler_params=pltpu.CompilerParams(vmem_limit_bytes=MIB),
        name="after",
    )(value, *others)


def direct_kernel(sizes, factor, *refs):
    n_ka, n_row, n_col = sizes
    refs = list(refs)

    def take(count):
        taken, refs[:] = refs[:count], refs[count:]
        return taken

    w, exciton_ref, cond_ref, val_ref = take(4)
    cores = [take(n_col) for _ in range(1, n_ka)]
    spread_ref, = take(1)
    keep, *sent = take(n_col)
    x_all, cond_all, val_all, panels, products, direct, total = refs
    col = lax.axis_index("col")
    n_v, n_nu = val_ref.shape
    n_c, n_mu = cond_ref.shape
    n_b = exciton_ref.shape[0] // n_v
    n_tiles, n_slots = n_mu // TILE, products.shape[0]

    x_all[0] = exciton_ref[...]
    cond_all[0] = cond_ref[...]
    val_all[0] = val_ref[...]
    part_c, part_x = n_c // n_col, exciton_ref.shape[0] // n_col
    for flip in range(1, n_ka):
        for other in range(n_col):
            source, at = cores[flip - 1][other], 0
            rows = pl.ds(pl.multiple_of((col ^ other) * part_c, part_c), part_c)
            for block in range(n_mu // LANES):
                cond_all[flip, rows, block * LANES:(block + 1) * LANES] = source[at:at + part_c, :]
                at += part_c
            rows = pl.ds(pl.multiple_of((col ^ other) * part_x, part_x), part_x)
            x_all[flip, rows, :] = source[at:at + part_x, :]
    val_all[1:] = spread_ref[...]
    total[...] = jnp.zeros_like(total)

    @pl.loop(0, n_tiles)
    def one_tile(number):
        start = pl.multiple_of(number * TILE, TILE)
        columns = pl.ds(start, TILE)
        for flip in range(n_ka):
            by_point = lax.dot_general(
                cond_all[flip, :, columns], x_all[flip],
                (((0,), (1,)), ((), ())), preferred_element_type=F32,
            ).astype(BF16)
            for b in range(n_b):
                panels[flip, b * TILE:(b + 1) * TILE, :] = by_point[:, b * n_v:(b + 1) * n_v]
        for j in range(n_nu // CHUNK):
            at = slice(j * CHUNK, (j + 1) * CHUNK)
            slot = j % n_slots
            for flip in range(n_ka):
                products[slot, flip] = jnp.dot(
                    panels[flip], val_all[flip, :, at], preferred_element_type=F32
                )
            for m in range(0, TILE, ROWS):
                weights = [
                    w[flip, pl.ds(start + m, ROWS), at].astype(F32) for flip in range(n_ka)
                ]
                for b in range(n_b):
                    rows = slice(b * TILE + m, b * TILE + m + ROWS)
                    value = products[slot, 0, rows, :] * weights[0]
                    for flip in range(1, n_ka):
                        value += products[slot, flip, rows, :] * weights[flip]
                    direct[rows, at] = value.astype(BF16)
        half = lax.dot_general(
            direct[...], val_all[0], (((1,), (1,)), ((), ())), preferred_element_type=F32
        ).astype(BF16)
        cond_tile = cond_all[0, :, columns]
        for b in range(n_b):
            total[b] += lax.dot_general(
                half[b * TILE:(b + 1) * TILE, :], cond_tile,
                (((0,), (1,)), ((), ())), preferred_element_type=F32,
            )

    part = n_v // n_col
    for other in range(n_col):
        place = pl.multiple_of((col ^ other) * part, part)
        value = total[:, pl.ds(place, part), :] * factor
        if other == 0:
            keep[...] = value
        else:
            sent[other - 1][...] = value.astype(BF16)


def local(sizes, exciton, orb_cond, orb_val, screened, q_table):
    n_ka, n_row, n_col = sizes
    n_b, n_v, n_c = exciton.shape[1:]
    x_rows, cond, val, screened, q_table = (
        pltpu.with_memory_space_constraint(array, pltpu.HBM)
        for array in (exciton.reshape(n_b * n_v, n_c), orb_cond[0], orb_val[0], screened, q_table)
    )
    n_mu, n_nu = cond.shape[1], val.shape[1]
    core_rows = (cond.size + x_rows.size) // n_col // LANES
    core, plane = pl.pallas_call(
        functools.partial(pack_kernel, (n_row, n_col)),
        in_specs=[IN_HBM] * 3,
        out_specs=[IN_VMEM] * 2,
        out_shape=[
            jax.ShapeDtypeStruct((core_rows, LANES), BF16),
            jax.ShapeDtypeStruct((n_v // n_row, n_nu), BF16),
        ],
        scratch_shapes=[pltpu.SemaphoreType.DMA(((n_mu + n_c) // LANES + 1,))],
        compiler_params=pltpu.CompilerParams(vmem_limit_bytes=4 * MIB),
        name="pack",
    )(x_rows, cond, val)
    planes = [swap(plane, "ka", n_ka, flip) for flip in range(1, n_ka)]
    joined = join(planes)
    cores = [after(core, planes[0])]
    loaded = pl.pallas_call(
        load_kernel,
        in_specs=[IN_SMEM] + [IN_HBM] * 4 + [pl.BlockSpec(memory_space=pl.ANY)],
        out_specs=[IN_VMEM] * 4,
        out_shape=[
            jax.ShapeDtypeStruct(block.shape, BF16) for block in (screened, x_rows, cond, val)
        ],
        scratch_shapes=[pltpu.SemaphoreType.DMA((n_ka + 3,))],
        compiler_params=pltpu.CompilerParams(vmem_limit_bytes=8 * MIB),
        cost_estimate=pl.CostEstimate(
            flops=0, bytes_accessed=4 * screened.size, transcendentals=0
        ),
        name="load",
    )(q_table, screened, x_rows, cond, val, cores[0])
    for flip in range(1, n_ka):
        last = flip & -flip
        cores.append(swap(cores[flip - last], "ka", n_ka, last))
        if flip == 2:
            cores[2] = after(cores[2], joined, cores[1], loaded[0])
    operands = []
    for core in cores[1:]:
        operands += [swap(core, "col", n_col, d) if d else core for d in range(n_col)]
    parts = [swap(joined, "row", n_row, d) if d else joined for d in range(n_row)]
    operands.append(pl.pallas_call(
        functools.partial(spread_kernel, n_row),
        in_specs=[IN_VMEM] * n_row,
        out_specs=IN_VMEM,
        out_shape=jax.ShapeDtypeStruct((n_ka - 1, *val.shape), BF16),
        compiler_params=pltpu.CompilerParams(vmem_limit_bytes=4 * MIB),
        cost_estimate=pl.CostEstimate(flops=SPREAD_FLOPS, bytes_accessed=0, transcendentals=0),
        name="spread",
    )(*parts))

    factor = math.sqrt(n_v * n_c) / (n_mu * n_row)
    part = n_v // n_col
    slots = min(2, n_nu // CHUNK)
    kept, *sent = pl.pallas_call(
        functools.partial(direct_kernel, sizes, factor),
        in_specs=[IN_VMEM] * (len(loaded) + len(operands)),
        out_specs=[IN_VMEM] * n_col,
        out_shape=[jax.ShapeDtypeStruct((n_b, part, n_c), F32)]
        + [jax.ShapeDtypeStruct((n_b, part, n_c), BF16)] * (n_col - 1),
        scratch_shapes=[
            pltpu.VMEM((n_ka, n_b * n_v, n_c), BF16),
            pltpu.VMEM((n_ka, n_c, n_mu), BF16),
            pltpu.VMEM((n_ka, n_v, n_nu), BF16),
            pltpu.VMEM((n_ka, n_b * TILE, n_v), BF16),
            pltpu.VMEM((slots, n_ka, n_b * TILE, CHUNK), F32),
            pltpu.VMEM((n_b * TILE, n_nu), BF16),
            pltpu.VMEM((n_b, n_v, n_c), F32),
        ],
        compiler_params=pltpu.CompilerParams(vmem_limit_bytes=28 * MIB),
        name="direct_term",
    )(*loaded, *operands)
    mine = kept
    for flip in range(1, n_col):
        mine = mine + swap(sent[flip - 1], "col", n_col, flip).astype(F32)
    mine = mine.astype(BF16)
    terms = [swap(mine, "row", n_row, flip) for flip in reversed(range(1, n_row))] + [mine]
    terms = [term.astype(F32) for term in terms]
    while len(terms) > 1:
        terms = [a + b for a, b in zip(terms[::2], terms[1::2])]
    return terms[0][None]


def solution(mesh):
    placed = (
        P("ka", None, None, None),
        P("ka", None, "row"),
        P("ka", None, "col"),
        P(None, "row", "col"),
        P(),
    )
    sizes = tuple(mesh.shape[name] for name in ("ka", "row", "col"))
    return jax.shard_map(
        functools.partial(local, sizes), mesh=mesh, in_specs=placed,
        out_specs=P("ka", None, "col", None), check_vma=False,
    )
```

```python
import functools
import math

import jax
import jax.numpy as jnp
from jax import lax
from jax.experimental import pallas as pl
from jax.experimental.pallas import tpu as pltpu
from jax.sharding import PartitionSpec as P

BF16 = jnp.bfloat16
F32 = jnp.float32
LANES = 128
ROWS = 16
TILE = 128
CHUNK = 256
MIB = 2**20
JOIN_FLOPS = 2 * 10**10
SPREAD_FLOPS = 2 * 10**10
IN_HBM = pl.BlockSpec(memory_space=pltpu.HBM)
IN_VMEM = pl.BlockSpec(memory_space=pltpu.VMEM)
IN_SMEM = pl.BlockSpec(memory_space=pltpu.SMEM)


def swap(value, axis, size, flip):
    return lax.ppermute(value, axis, [(i, i ^ flip) for i in range(size)])


def run(copies):
    for copy in copies:
        copy.start()
    for copy in copies:
        copy.wait()


def pack_kernel(sizes, exciton_ref, cond_ref, val_ref, core_ref, plane_ref, sems):
    n_row, n_col = sizes
    row, col = lax.axis_index("row"), lax.axis_index("col")
    part = plane_ref.shape[0]
    rows = pl.ds(pl.multiple_of(row * part, part), part)
    copies, at = [pltpu.make_async_copy(val_ref.at[rows, :], plane_ref, sems.at[0])], 0
    for source in (cond_ref, exciton_ref):
        part = source.shape[0] // n_col
        rows = pl.ds(pl.multiple_of(col * part, part), part)
        for block in range(source.shape[1] // LANES):
            copies.append(pltpu.make_async_copy(
                source.at[rows, block * LANES:(block + 1) * LANES],
                core_ref.at[at:at + part, :], sems.at[len(copies)],
            ))
            at += part
    run(copies)


def join_kernel(*refs):
    *parts, _, out = refs
    at = 0
    for part in parts:
        out[at:at + part.shape[0], :] = part[...]
        at += part.shape[0]


def join(parts, other):
    shape = (sum(part.shape[0] for part in parts), parts[0].shape[1])
    return pl.pallas_call(
        join_kernel,
        in_specs=[IN_VMEM] * len(parts) + [pl.BlockSpec(memory_space=pl.ANY)],
        out_specs=IN_VMEM,
        out_shape=jax.ShapeDtypeStruct(shape, BF16),
        compiler_params=pltpu.CompilerParams(vmem_limit_bytes=4 * MIB),
        cost_estimate=pl.CostEstimate(flops=JOIN_FLOPS, bytes_accessed=0, transcendentals=0),
        name="join",
    )(*parts, other)


def spread_kernel(n_row, *refs):
    *parts, out = refs
    row = lax.axis_index("row")
    part = out.shape[1] // n_row
    for other in range(n_row):
        rows = pl.ds(pl.multiple_of((row ^ other) * part, part), part)
        for flip in range(out.shape[0]):
            out[flip, rows, :] = parts[other][flip * part:(flip + 1) * part, :]


def load_kernel(q_ref, w_ref, exciton_ref, cond_ref, val_ref, after_ref, w, x, cond, val, sems):
    del after_ref
    me, n_ka = lax.axis_index("ka"), w.shape[0]
    pairs = [(w_ref.at[q_ref[me ^ flip, me]], w.at[flip]) for flip in range(n_ka)]
    pairs += [(exciton_ref, x), (cond_ref, cond), (val_ref, val)]
    run([
        pltpu.make_async_copy(source, target, sems.at[i])
        for i, (source, target) in enumerate(pairs)
    ])


def after_kernel(*refs):
    refs[-1][...] = refs[0][...]


def after(value, *others):
    return pl.pallas_call(
        after_kernel,
        in_specs=[IN_VMEM] + [pl.BlockSpec(memory_space=pl.ANY)] * len(others),
        out_specs=IN_VMEM,
        out_shape=jax.ShapeDtypeStruct(value.shape, value.dtype),
        compiler_params=pltpu.CompilerParams(vmem_limit_bytes=4 * MIB),
        name="after",
    )(value, *others)


def direct_kernel(sizes, factor, *refs):
    n_ka, n_row, n_col = sizes
    refs = list(refs)

    def take(count):
        taken, refs[:] = refs[:count], refs[count:]
        return taken

    w, exciton_ref, cond_ref, val_ref = take(4)
    cores = [take(n_col) for _ in range(1, n_ka)]
    spread_ref, = take(1)
    keep, *sent = take(n_col)
    x_all, cond_all, val_all, panels, products, direct, total = refs
    col = lax.axis_index("col")
    n_v, n_nu = val_ref.shape
    n_c, n_mu = cond_ref.shape
    n_b = exciton_ref.shape[0] // n_v
    n_tiles, n_slots = n_mu // TILE, products.shape[0]

    x_all[0] = exciton_ref[...]
    cond_all[0] = cond_ref[...]
    val_all[0] = val_ref[...]
    part_c, part_x = n_c // n_col, exciton_ref.shape[0] // n_col
    for flip in range(1, n_ka):
        for other in range(n_col):
            source, at = cores[flip - 1][other], 0
            rows = pl.ds(pl.multiple_of((col ^ other) * part_c, part_c), part_c)
            for block in range(n_mu // LANES):
                cond_all[flip, rows, block * LANES:(block + 1) * LANES] = source[at:at + part_c, :]
                at += part_c
            rows = pl.ds(pl.multiple_of((col ^ other) * part_x, part_x), part_x)
            x_all[flip, rows, :] = source[at:at + part_x, :]
    val_all[1:] = spread_ref[...]
    total[...] = jnp.zeros_like(total)

    @pl.loop(0, n_tiles)
    def one_tile(number):
        start = pl.multiple_of(number * TILE, TILE)
        columns = pl.ds(start, TILE)
        for flip in range(n_ka):
            by_point = lax.dot_general(
                cond_all[flip, :, columns], x_all[flip],
                (((0,), (1,)), ((), ())), preferred_element_type=F32,
            ).astype(BF16)
            for b in range(n_b):
                panels[flip, b * TILE:(b + 1) * TILE, :] = by_point[:, b * n_v:(b + 1) * n_v]
        for j in range(n_nu // CHUNK):
            at = slice(j * CHUNK, (j + 1) * CHUNK)
            slot = j % n_slots
            for flip in range(n_ka):
                products[slot, flip] = jnp.dot(
                    panels[flip], val_all[flip, :, at], preferred_element_type=F32
                )
            for m in range(0, TILE, ROWS):
                weights = [
                    w[flip, pl.ds(start + m, ROWS), at].astype(F32) for flip in range(n_ka)
                ]
                for b in range(n_b):
                    rows = slice(b * TILE + m, b * TILE + m + ROWS)
                    value = products[slot, 0, rows, :] * weights[0]
                    for flip in range(1, n_ka):
                        value += products[slot, flip, rows, :] * weights[flip]
                    direct[rows, at] = value.astype(BF16)
        half = lax.dot_general(
            direct[...], val_all[0], (((1,), (1,)), ((), ())), preferred_element_type=F32
        ).astype(BF16)
        cond_tile = cond_all[0, :, columns]
        for b in range(n_b):
            total[b] += lax.dot_general(
                half[b * TILE:(b + 1) * TILE, :], cond_tile,
                (((0,), (1,)), ((), ())), preferred_element_type=F32,
            )

    part = n_v // n_col
    for other in range(n_col):
        place = pl.multiple_of((col ^ other) * part, part)
        value = total[:, pl.ds(place, part), :] * factor
        if other == 0:
            keep[...] = value
        else:
            sent[other - 1][...] = value.astype(BF16)


def local(sizes, exciton, orb_cond, orb_val, screened, q_table):
    n_ka, n_row, n_col = sizes
    n_b, n_v, n_c = exciton.shape[1:]
    x_rows, cond, val, screened, q_table = (
        pltpu.with_memory_space_constraint(array, pltpu.HBM)
        for array in (exciton.reshape(n_b * n_v, n_c), orb_cond[0], orb_val[0], screened, q_table)
    )
    n_mu, n_nu = cond.shape[1], val.shape[1]
    core_rows = (cond.size + x_rows.size) // n_col // LANES
    core, plane = pl.pallas_call(
        functools.partial(pack_kernel, (n_row, n_col)),
        in_specs=[IN_HBM] * 3,
        out_specs=[IN_VMEM] * 2,
        out_shape=[
            jax.ShapeDtypeStruct((core_rows, LANES), BF16),
            jax.ShapeDtypeStruct((n_v // n_row, n_nu), BF16),
        ],
        scratch_shapes=[pltpu.SemaphoreType.DMA(((n_mu + n_c) // LANES + 1,))],
        compiler_params=pltpu.CompilerParams(vmem_limit_bytes=4 * MIB),
        name="pack",
    )(x_rows, cond, val)
    planes = [swap(plane, "ka", n_ka, flip) for flip in range(1, n_ka)]
    loaded = pl.pallas_call(
        load_kernel,
        in_specs=[IN_SMEM] + [IN_HBM] * 4 + [pl.BlockSpec(memory_space=pl.ANY)],
        out_specs=[IN_VMEM] * 4,
        out_shape=[
            jax.ShapeDtypeStruct(block.shape, BF16) for block in (screened, x_rows, cond, val)
        ],
        scratch_shapes=[pltpu.SemaphoreType.DMA((n_ka + 3,))],
        compiler_params=pltpu.CompilerParams(vmem_limit_bytes=8 * MIB),
        cost_estimate=pl.CostEstimate(
            flops=0, bytes_accessed=4 * screened.size, transcendentals=0
        ),
        name="load",
    )(q_table, screened, x_rows, cond, val, planes[0])
    joined = join(planes, loaded[0])
    cores = [core]
    for flip in range(1, n_ka):
        last = flip & -flip
        source = cores[flip - last]
        if flip == last:
            source = after(source, planes[flip - 1])
        cores.append(swap(source, "ka", n_ka, last))
        if flip == 2:
            cores[2] = after(cores[2], joined, cores[1])
    operands = []
    for core in cores[1:]:
        operands += [swap(core, "col", n_col, d) if d else core for d in range(n_col)]
    parts = [swap(joined, "row", n_row, d) if d else joined for d in range(n_row)]
    operands.append(pl.pallas_call(
        functools.partial(spread_kernel, n_row),
        in_specs=[IN_VMEM] * n_row,
        out_specs=IN_VMEM,
        out_shape=jax.ShapeDtypeStruct((n_ka - 1, *val.shape), BF16),
        compiler_params=pltpu.CompilerParams(vmem_limit_bytes=4 * MIB),
        cost_estimate=pl.CostEstimate(flops=SPREAD_FLOPS, bytes_accessed=0, transcendentals=0),
        name="spread",
    )(*parts))

    factor = math.sqrt(n_v * n_c) / (n_mu * n_row)
    part = n_v // n_col
    slots = min(2, n_nu // CHUNK)
    kept, *sent = pl.pallas_call(
        functools.partial(direct_kernel, sizes, factor),
        in_specs=[IN_VMEM] * (len(loaded) + len(operands)),
        out_specs=[IN_VMEM] * n_col,
        out_shape=[jax.ShapeDtypeStruct((n_b, part, n_c), F32)]
        + [jax.ShapeDtypeStruct((n_b, part, n_c), BF16)] * (n_col - 1),
        scratch_shapes=[
            pltpu.VMEM((n_ka, n_b * n_v, n_c), BF16),
            pltpu.VMEM((n_ka, n_c, n_mu), BF16),
            pltpu.VMEM((n_ka, n_v, n_nu), BF16),
            pltpu.VMEM((n_ka, n_b * TILE, n_v), BF16),
            pltpu.VMEM((slots, n_ka, n_b * TILE, CHUNK), F32),
            pltpu.VMEM((n_b * TILE, n_nu), BF16),
            pltpu.VMEM((n_b, n_v, n_c), F32),
        ],
        compiler_params=pltpu.CompilerParams(vmem_limit_bytes=28 * MIB),
        name="direct_term",
    )(*loaded, *operands)
    mine = kept
    for flip in range(1, n_col):
        mine = mine + swap(sent[flip - 1], "col", n_col, flip).astype(F32)
    mine = mine.astype(BF16)
    terms = [swap(mine, "row", n_row, flip) for flip in reversed(range(1, n_row))] + [mine]
    terms = [term.astype(F32) for term in terms]
    while len(terms) > 1:
        terms = [a + b for a, b in zip(terms[::2], terms[1::2])]
    return terms[0][None]


def solution(mesh):
    placed = (
        P("ka", None, None, None),
        P("ka", None, "row"),
        P("ka", None, "col"),
        P(None, "row", "col"),
        P(),
    )
    sizes = tuple(mesh.shape[name] for name in ("ka", "row", "col"))
    return jax.shard_map(
        functools.partial(local, sizes), mesh=mesh, in_specs=placed,
        out_specs=P("ka", None, "col", None), check_vma=False,
    )
```

```python
import functools
import math

import jax
import jax.numpy as jnp
from jax import lax
from jax.experimental import pallas as pl
from jax.experimental.pallas import tpu as pltpu
from jax.sharding import PartitionSpec as P

BF16 = jnp.bfloat16
F32 = jnp.float32
LANES = 128
ROWS = 16
TILE = 128
CHUNK = 256
MIB = 2**20
JOIN_FLOPS = 2 * 10**10
SPREAD_FLOPS = 2 * 10**10
IN_HBM = pl.BlockSpec(memory_space=pltpu.HBM)
IN_VMEM = pl.BlockSpec(memory_space=pltpu.VMEM)
IN_SMEM = pl.BlockSpec(memory_space=pltpu.SMEM)


def swap(value, axis, size, flip):
    return lax.ppermute(value, axis, [(i, i ^ flip) for i in range(size)])


def run(copies):
    for copy in copies:
        copy.start()
    for copy in copies:
        copy.wait()


def pack_kernel(sizes, exciton_ref, cond_ref, val_ref, core_ref, plane_ref, sems):
    n_row, n_col = sizes
    row, col = lax.axis_index("row"), lax.axis_index("col")
    part = plane_ref.shape[0]
    rows = pl.ds(pl.multiple_of(row * part, part), part)
    copies, at = [pltpu.make_async_copy(val_ref.at[rows, :], plane_ref, sems.at[0])], 0
    for source in (cond_ref, exciton_ref):
        part = source.shape[0] // n_col
        rows = pl.ds(pl.multiple_of(col * part, part), part)
        for block in range(source.shape[1] // LANES):
            copies.append(pltpu.make_async_copy(
                source.at[rows, block * LANES:(block + 1) * LANES],
                core_ref.at[at:at + part, :], sems.at[len(copies)],
            ))
            at += part
    run(copies)


def join_kernel(*refs):
    *parts, out = refs
    at = 0
    for part in parts:
        out[at:at + part.shape[0], :] = part[...]
        at += part.shape[0]


def join(parts):
    shape = (sum(part.shape[0] for part in parts), parts[0].shape[1])
    return pl.pallas_call(
        join_kernel,
        in_specs=[IN_VMEM] * len(parts),
        out_specs=IN_VMEM,
        out_shape=jax.ShapeDtypeStruct(shape, BF16),
        compiler_params=pltpu.CompilerParams(vmem_limit_bytes=4 * MIB),
        cost_estimate=pl.CostEstimate(flops=JOIN_FLOPS, bytes_accessed=0, transcendentals=0),
        name="join",
    )(*parts)


def spread_kernel(n_row, *refs):
    *parts, out = refs
    row = lax.axis_index("row")
    part = out.shape[1] // n_row
    for other in range(n_row):
        rows = pl.ds(pl.multiple_of((row ^ other) * part, part), part)
        for flip in range(out.shape[0]):
            out[flip, rows, :] = parts[other][flip * part:(flip + 1) * part, :]


def load_kernel(q_ref, w_ref, exciton_ref, cond_ref, val_ref, after_ref, w, x, cond, val, sems):
    del after_ref
    me, n_ka = lax.axis_index("ka"), w.shape[0]
    pairs = [(w_ref.at[q_ref[me ^ flip, me]], w.at[flip]) for flip in range(n_ka)]
    pairs += [(exciton_ref, x), (cond_ref, cond), (val_ref, val)]
    run([
        pltpu.make_async_copy(source, target, sems.at[i])
        for i, (source, target) in enumerate(pairs)
    ])


def after_kernel(*refs):
    refs[-1][...] = refs[0][...]


def after(value, *others):
    return pl.pallas_call(
        after_kernel,
        in_specs=[IN_VMEM] + [pl.BlockSpec(memory_space=pl.ANY)] * len(others),
        out_specs=IN_VMEM,
        out_shape=jax.ShapeDtypeStruct(value.shape, value.dtype),
        compiler_params=pltpu.CompilerParams(vmem_limit_bytes=4 * MIB),
        name="after",
    )(value, *others)


def direct_kernel(sizes, factor, *refs):
    n_ka, n_row, n_col = sizes
    refs = list(refs)

    def take(count):
        taken, refs[:] = refs[:count], refs[count:]
        return taken

    w, exciton_ref, cond_ref, val_ref = take(4)
    cores = [take(n_col) for _ in range(1, n_ka)]
    spread_ref, = take(1)
    keep, *sent = take(n_col)
    x_all, cond_all, val_all, panels, products, direct, total = refs
    col = lax.axis_index("col")
    n_v, n_nu = val_ref.shape
    n_c, n_mu = cond_ref.shape
    n_b = exciton_ref.shape[0] // n_v
    n_tiles, n_slots = n_mu // TILE, products.shape[0]

    x_all[0] = exciton_ref[...]
    cond_all[0] = cond_ref[...]
    val_all[0] = val_ref[...]
    part_c, part_x = n_c // n_col, exciton_ref.shape[0] // n_col
    for flip in range(1, n_ka):
        for other in range(n_col):
            source, at = cores[flip - 1][other], 0
            rows = pl.ds(pl.multiple_of((col ^ other) * part_c, part_c), part_c)
            for block in range(n_mu // LANES):
                cond_all[flip, rows, block * LANES:(block + 1) * LANES] = source[at:at + part_c, :]
                at += part_c
            rows = pl.ds(pl.multiple_of((col ^ other) * part_x, part_x), part_x)
            x_all[flip, rows, :] = source[at:at + part_x, :]
    val_all[1:] = spread_ref[...]
    total[...] = jnp.zeros_like(total)

    @pl.loop(0, n_tiles)
    def one_tile(number):
        start = pl.multiple_of(number * TILE, TILE)
        columns = pl.ds(start, TILE)
        for flip in range(n_ka):
            by_point = lax.dot_general(
                cond_all[flip, :, columns], x_all[flip],
                (((0,), (1,)), ((), ())), preferred_element_type=F32,
            ).astype(BF16)
            for b in range(n_b):
                panels[flip, b * TILE:(b + 1) * TILE, :] = by_point[:, b * n_v:(b + 1) * n_v]
        for j in range(n_nu // CHUNK):
            at = slice(j * CHUNK, (j + 1) * CHUNK)
            slot = j % n_slots
            for flip in range(n_ka):
                products[slot, flip] = jnp.dot(
                    panels[flip], val_all[flip, :, at], preferred_element_type=F32
                )
            for m in range(0, TILE, ROWS):
                weights = [
                    w[flip, pl.ds(start + m, ROWS), at].astype(F32) for flip in range(n_ka)
                ]
                for b in range(n_b):
                    rows = slice(b * TILE + m, b * TILE + m + ROWS)
                    value = products[slot, 0, rows, :] * weights[0]
                    for flip in range(1, n_ka):
                        value += products[slot, flip, rows, :] * weights[flip]
                    direct[rows, at] = value.astype(BF16)
        half = lax.dot_general(
            direct[...], val_all[0], (((1,), (1,)), ((), ())), preferred_element_type=F32
        ).astype(BF16)
        cond_tile = cond_all[0, :, columns]
        for b in range(n_b):
            total[b] += lax.dot_general(
                half[b * TILE:(b + 1) * TILE, :], cond_tile,
                (((0,), (1,)), ((), ())), preferred_element_type=F32,
            )

    part = n_v // n_col
    for other in range(n_col):
        place = pl.multiple_of((col ^ other) * part, part)
        value = total[:, pl.ds(place, part), :] * factor
        if other == 0:
            keep[...] = value
        else:
            sent[other - 1][...] = value.astype(BF16)


def local(sizes, exciton, orb_cond, orb_val, screened, q_table):
    n_ka, n_row, n_col = sizes
    n_b, n_v, n_c = exciton.shape[1:]
    x_rows, cond, val, screened, q_table = (
        pltpu.with_memory_space_constraint(array, pltpu.HBM)
        for array in (exciton.reshape(n_b * n_v, n_c), orb_cond[0], orb_val[0], screened, q_table)
    )
    n_mu, n_nu = cond.shape[1], val.shape[1]
    core_rows = (cond.size + x_rows.size) // n_col // LANES
    core, plane = pl.pallas_call(
        functools.partial(pack_kernel, (n_row, n_col)),
        in_specs=[IN_HBM] * 3,
        out_specs=[IN_VMEM] * 2,
        out_shape=[
            jax.ShapeDtypeStruct((core_rows, LANES), BF16),
            jax.ShapeDtypeStruct((n_v // n_row, n_nu), BF16),
        ],
        scratch_shapes=[pltpu.SemaphoreType.DMA(((n_mu + n_c) // LANES + 1,))],
        compiler_params=pltpu.CompilerParams(vmem_limit_bytes=4 * MIB),
        name="pack",
    )(x_rows, cond, val)
    planes = [swap(plane, "ka", n_ka, flip) for flip in range(1, n_ka)]
    joined = join(planes)
    cores = [core]
    for flip in range(1, n_ka):
        last = flip & -flip
        source = cores[flip - last]
        if flip == last:
            source = after(source, planes[flip - 1])
        cores.append(swap(source, "ka", n_ka, last))
        if flip == 2:
            cores[2] = after(cores[2], joined, cores[1])
    loaded = pl.pallas_call(
        load_kernel,
        in_specs=[IN_SMEM] + [IN_HBM] * 4 + [pl.BlockSpec(memory_space=pl.ANY)],
        out_specs=[IN_VMEM] * 4,
        out_shape=[
            jax.ShapeDtypeStruct(block.shape, BF16) for block in (screened, x_rows, cond, val)
        ],
        scratch_shapes=[pltpu.SemaphoreType.DMA((n_ka + 3,))],
        compiler_params=pltpu.CompilerParams(vmem_limit_bytes=8 * MIB),
        cost_estimate=pl.CostEstimate(
            flops=0, bytes_accessed=4 * screened.size, transcendentals=0
        ),
        name="load",
    )(q_table, screened, x_rows, cond, val, cores[n_ka // 2])
    operands = []
    for core in cores[1:]:
        operands += [swap(core, "col", n_col, d) if d else core for d in range(n_col)]
    parts = [swap(joined, "row", n_row, d) if d else joined for d in range(n_row)]
    operands.append(pl.pallas_call(
        functools.partial(spread_kernel, n_row),
        in_specs=[IN_VMEM] * n_row,
        out_specs=IN_VMEM,
        out_shape=jax.ShapeDtypeStruct((n_ka - 1, *val.shape), BF16),
        compiler_params=pltpu.CompilerParams(vmem_limit_bytes=4 * MIB),
        cost_estimate=pl.CostEstimate(flops=SPREAD_FLOPS, bytes_accessed=0, transcendentals=0),
        name="spread",
    )(*parts))

    factor = math.sqrt(n_v * n_c) / (n_mu * n_row)
    part = n_v // n_col
    slots = min(2, n_nu // CHUNK)
    kept, *sent = pl.pallas_call(
        functools.partial(direct_kernel, sizes, factor),
        in_specs=[IN_VMEM] * (len(loaded) + len(operands)),
        out_specs=[IN_VMEM] * n_col,
        out_shape=[jax.ShapeDtypeStruct((n_b, part, n_c), F32)]
        + [jax.ShapeDtypeStruct((n_b, part, n_c), BF16)] * (n_col - 1),
        scratch_shapes=[
            pltpu.VMEM((n_ka, n_b * n_v, n_c), BF16),
            pltpu.VMEM((n_ka, n_c, n_mu), BF16),
            pltpu.VMEM((n_ka, n_v, n_nu), BF16),
            pltpu.VMEM((n_ka, n_b * TILE, n_v), BF16),
            pltpu.VMEM((slots, n_ka, n_b * TILE, CHUNK), F32),
            pltpu.VMEM((n_b * TILE, n_nu), BF16),
            pltpu.VMEM((n_b, n_v, n_c), F32),
        ],
        compiler_params=pltpu.CompilerParams(vmem_limit_bytes=28 * MIB),
        name="direct_term",
    )(*loaded, *operands)
    mine = kept
    for flip in range(1, n_col):
        mine = mine + swap(sent[flip - 1], "col", n_col, flip).astype(F32)
    mine = mine.astype(BF16)
    terms = [swap(mine, "row", n_row, flip) for flip in reversed(range(1, n_row))] + [mine]
    terms = [term.astype(F32) for term in terms]
    while len(terms) > 1:
        terms = [a + b for a, b in zip(terms[::2], terms[1::2])]
    return terms[0][None]


def solution(mesh):
    placed = (
        P("ka", None, None, None),
        P("ka", None, "row"),
        P("ka", None, "col"),
        P(None, "row", "col"),
        P(),
    )
    sizes = tuple(mesh.shape[name] for name in ("ka", "row", "col"))
    return jax.shard_map(
        functools.partial(local, sizes), mesh=mesh, in_specs=placed,
        out_specs=P("ka", None, "col", None), check_vma=False,
    )
```

```python
import functools
import math

import jax
import jax.numpy as jnp
from jax import lax
from jax.experimental import pallas as pl
from jax.experimental.pallas import tpu as pltpu
from jax.sharding import PartitionSpec as P

BF16 = jnp.bfloat16
F32 = jnp.float32
LANES = 128
ROWS = 16
TILE = 128
CHUNK = 256
MIB = 2**20
JOIN_FLOPS = 2 * 10**10
SPREAD_FLOPS = 2 * 10**10
IN_HBM = pl.BlockSpec(memory_space=pltpu.HBM)
IN_VMEM = pl.BlockSpec(memory_space=pltpu.VMEM)
IN_SMEM = pl.BlockSpec(memory_space=pltpu.SMEM)


def swap(value, axis, size, flip):
    return lax.ppermute(value, axis, [(i, i ^ flip) for i in range(size)])


def run(copies):
    for copy in copies:
        copy.start()
    for copy in copies:
        copy.wait()


def pack_kernel(sizes, exciton_ref, cond_ref, val_ref, core_ref, plane_ref, sems):
    n_row, n_col = sizes
    row, col = lax.axis_index("row"), lax.axis_index("col")
    part = plane_ref.shape[0]
    rows = pl.ds(pl.multiple_of(row * part, part), part)
    copies, at = [pltpu.make_async_copy(val_ref.at[rows, :], plane_ref, sems.at[0])], 0
    for source in (cond_ref, exciton_ref):
        part = source.shape[0] // n_col
        rows = pl.ds(pl.multiple_of(col * part, part), part)
        for block in range(source.shape[1] // LANES):
            copies.append(pltpu.make_async_copy(
                source.at[rows, block * LANES:(block + 1) * LANES],
                core_ref.at[at:at + part, :], sems.at[len(copies)],
            ))
            at += part
    run(copies)


def join_kernel(*refs):
    *parts, out = refs
    at = 0
    for part in parts:
        out[at:at + part.shape[0], :] = part[...]
        at += part.shape[0]


def join(parts):
    shape = (sum(part.shape[0] for part in parts), parts[0].shape[1])
    return pl.pallas_call(
        join_kernel,
        in_specs=[IN_VMEM] * len(parts),
        out_specs=IN_VMEM,
        out_shape=jax.ShapeDtypeStruct(shape, BF16),
        compiler_params=pltpu.CompilerParams(vmem_limit_bytes=4 * MIB),
        cost_estimate=pl.CostEstimate(flops=JOIN_FLOPS, bytes_accessed=0, transcendentals=0),
        name="join",
    )(*parts)


def spread_kernel(n_row, *refs):
    *parts, out = refs
    row = lax.axis_index("row")
    part = out.shape[1] // n_row
    for other in range(n_row):
        rows = pl.ds(pl.multiple_of((row ^ other) * part, part), part)
        for flip in range(out.shape[0]):
            out[flip, rows, :] = parts[other][flip * part:(flip + 1) * part, :]


def load_kernel(q_ref, w_ref, exciton_ref, cond_ref, val_ref, after_ref, w, x, cond, val, sems):
    del after_ref
    me, n_ka = lax.axis_index("ka"), w.shape[0]
    pairs = [(w_ref.at[q_ref[me ^ flip, me]], w.at[flip]) for flip in range(n_ka)]
    pairs += [(exciton_ref, x), (cond_ref, cond), (val_ref, val)]
    run([
        pltpu.make_async_copy(source, target, sems.at[i])
        for i, (source, target) in enumerate(pairs)
    ])


def after_kernel(*refs):
    refs[-1][...] = refs[0][...]


def after(value, *others, flops=0):
    return pl.pallas_call(
        after_kernel,
        in_specs=[IN_VMEM] + [pl.BlockSpec(memory_space=pl.ANY)] * len(others),
        out_specs=IN_VMEM,
        out_shape=jax.ShapeDtypeStruct(value.shape, value.dtype),
        compiler_params=pltpu.CompilerParams(vmem_limit_bytes=4 * MIB),
        cost_estimate=pl.CostEstimate(flops=flops, bytes_accessed=0, transcendentals=0),
        name="after",
    )(value, *others)


def direct_kernel(sizes, factor, *refs):
    n_ka, n_row, n_col = sizes
    refs = list(refs)

    def take(count):
        taken, refs[:] = refs[:count], refs[count:]
        return taken

    w, exciton_ref, cond_ref, val_ref = take(4)
    cores = [take(n_col) for _ in range(1, n_ka)]
    spread_ref, = take(1)
    keep, *sent = take(n_col)
    x_all, cond_all, val_all, panels, products, direct, total = refs
    col = lax.axis_index("col")
    n_v, n_nu = val_ref.shape
    n_c, n_mu = cond_ref.shape
    n_b = exciton_ref.shape[0] // n_v
    n_tiles, n_slots = n_mu // TILE, products.shape[0]

    x_all[0] = exciton_ref[...]
    cond_all[0] = cond_ref[...]
    val_all[0] = val_ref[...]
    part_c, part_x = n_c // n_col, exciton_ref.shape[0] // n_col
    for flip in range(1, n_ka):
        for other in range(n_col):
            source, at = cores[flip - 1][other], 0
            rows = pl.ds(pl.multiple_of((col ^ other) * part_c, part_c), part_c)
            for block in range(n_mu // LANES):
                cond_all[flip, rows, block * LANES:(block + 1) * LANES] = source[at:at + part_c, :]
                at += part_c
            rows = pl.ds(pl.multiple_of((col ^ other) * part_x, part_x), part_x)
            x_all[flip, rows, :] = source[at:at + part_x, :]
    val_all[1:] = spread_ref[...]
    total[...] = jnp.zeros_like(total)

    @pl.loop(0, n_tiles)
    def one_tile(number):
        start = pl.multiple_of(number * TILE, TILE)
        columns = pl.ds(start, TILE)
        for flip in range(n_ka):
            by_point = lax.dot_general(
                cond_all[flip, :, columns], x_all[flip],
                (((0,), (1,)), ((), ())), preferred_element_type=F32,
            ).astype(BF16)
            for b in range(n_b):
                panels[flip, b * TILE:(b + 1) * TILE, :] = by_point[:, b * n_v:(b + 1) * n_v]
        for j in range(n_nu // CHUNK):
            at = slice(j * CHUNK, (j + 1) * CHUNK)
            slot = j % n_slots
            for flip in range(n_ka):
                products[slot, flip] = jnp.dot(
                    panels[flip], val_all[flip, :, at], preferred_element_type=F32
                )
            for m in range(0, TILE, ROWS):
                weights = [
                    w[flip, pl.ds(start + m, ROWS), at].astype(F32) for flip in range(n_ka)
                ]
                for b in range(n_b):
                    rows = slice(b * TILE + m, b * TILE + m + ROWS)
                    value = products[slot, 0, rows, :] * weights[0]
                    for flip in range(1, n_ka):
                        value += products[slot, flip, rows, :] * weights[flip]
                    direct[rows, at] = value.astype(BF16)
        half = lax.dot_general(
            direct[...], val_all[0], (((1,), (1,)), ((), ())), preferred_element_type=F32
        ).astype(BF16)
        cond_tile = cond_all[0, :, columns]
        for b in range(n_b):
            total[b] += lax.dot_general(
                half[b * TILE:(b + 1) * TILE, :], cond_tile,
                (((0,), (1,)), ((), ())), preferred_element_type=F32,
            )

    part = n_v // n_col
    for other in range(n_col):
        place = pl.multiple_of((col ^ other) * part, part)
        value = total[:, pl.ds(place, part), :] * factor
        if other == 0:
            keep[...] = value
        else:
            sent[other - 1][...] = value.astype(BF16)


def local(sizes, exciton, orb_cond, orb_val, screened, q_table):
    n_ka, n_row, n_col = sizes
    n_b, n_v, n_c = exciton.shape[1:]
    x_rows, cond, val, screened, q_table = (
        pltpu.with_memory_space_constraint(array, pltpu.HBM)
        for array in (exciton.reshape(n_b * n_v, n_c), orb_cond[0], orb_val[0], screened, q_table)
    )
    n_mu, n_nu = cond.shape[1], val.shape[1]
    core_rows = (cond.size + x_rows.size) // n_col // LANES
    core, plane = pl.pallas_call(
        functools.partial(pack_kernel, (n_row, n_col)),
        in_specs=[IN_HBM] * 3,
        out_specs=[IN_VMEM] * 2,
        out_shape=[
            jax.ShapeDtypeStruct((core_rows, LANES), BF16),
            jax.ShapeDtypeStruct((n_v // n_row, n_nu), BF16),
        ],
        scratch_shapes=[pltpu.SemaphoreType.DMA(((n_mu + n_c) // LANES + 1,))],
        compiler_params=pltpu.CompilerParams(vmem_limit_bytes=4 * MIB),
        name="pack",
    )(x_rows, cond, val)
    planes = [swap(plane, "ka", n_ka, flip) for flip in range(1, n_ka)]
    joined = join(planes)
    cores = [core]
    for flip in range(1, n_ka):
        last = flip & -flip
        source = cores[flip - last]
        if flip == last:
            source = after(source, planes[flip - 1])
        cores.append(swap(source, "ka", n_ka, last))
        if flip == 2:
            cores[2] = after(cores[2], joined)
    loaded = pl.pallas_call(
        load_kernel,
        in_specs=[IN_SMEM] + [IN_HBM] * 4 + [pl.BlockSpec(memory_space=pl.ANY)],
        out_specs=[IN_VMEM] * 4,
        out_shape=[
            jax.ShapeDtypeStruct(block.shape, BF16) for block in (screened, x_rows, cond, val)
        ],
        scratch_shapes=[pltpu.SemaphoreType.DMA((n_ka + 3,))],
        compiler_params=pltpu.CompilerParams(vmem_limit_bytes=8 * MIB),
        cost_estimate=pl.CostEstimate(
            flops=0, bytes_accessed=4 * screened.size, transcendentals=0
        ),
        name="load",
    )(q_table, screened, x_rows, cond, val, cores[n_ka // 2])
    operands = []
    for core in cores[1:]:
        operands += [swap(core, "col", n_col, d) if d else core for d in range(n_col)]
    parts = [swap(joined, "row", n_row, d) if d else joined for d in range(n_row)]
    operands.append(pl.pallas_call(
        functools.partial(spread_kernel, n_row),
        in_specs=[IN_VMEM] * n_row,
        out_specs=IN_VMEM,
        out_shape=jax.ShapeDtypeStruct((n_ka - 1, *val.shape), BF16),
        compiler_params=pltpu.CompilerParams(vmem_limit_bytes=4 * MIB),
        cost_estimate=pl.CostEstimate(flops=SPREAD_FLOPS, bytes_accessed=0, transcendentals=0),
        name="spread",
    )(*parts))

    factor = math.sqrt(n_v * n_c) / (n_mu * n_row)
    part = n_v // n_col
    slots = min(2, n_nu // CHUNK)
    kept, *sent = pl.pallas_call(
        functools.partial(direct_kernel, sizes, factor),
        in_specs=[IN_VMEM] * (len(loaded) + len(operands)),
        out_specs=[IN_VMEM] * n_col,
        out_shape=[jax.ShapeDtypeStruct((n_b, part, n_c), F32)]
        + [jax.ShapeDtypeStruct((n_b, part, n_c), BF16)] * (n_col - 1),
        scratch_shapes=[
            pltpu.VMEM((n_ka, n_b * n_v, n_c), BF16),
            pltpu.VMEM((n_ka, n_c, n_mu), BF16),
            pltpu.VMEM((n_ka, n_v, n_nu), BF16),
            pltpu.VMEM((n_ka, n_b * TILE, n_v), BF16),
            pltpu.VMEM((slots, n_ka, n_b * TILE, CHUNK), F32),
            pltpu.VMEM((n_b * TILE, n_nu), BF16),
            pltpu.VMEM((n_b, n_v, n_c), F32),
        ],
        compiler_params=pltpu.CompilerParams(vmem_limit_bytes=28 * MIB),
        name="direct_term",
    )(*loaded, *operands)
    mine = kept
    for flip in range(1, n_col):
        mine = mine + swap(sent[flip - 1], "col", n_col, flip).astype(F32)
    mine = mine.astype(BF16)
    terms = [after(swap(mine, "row", n_row, n_row - 1), flops=JOIN_FLOPS)]
    terms += [swap(mine, "row", n_row, flip) for flip in reversed(range(1, n_row - 1))] + [mine]
    terms = [term.astype(F32) for term in terms]
    while len(terms) > 1:
        terms = [a + b for a, b in zip(terms[::2], terms[1::2])]
    return terms[0][None]


def solution(mesh):
    placed = (
        P("ka", None, None, None),
        P("ka", None, "row"),
        P("ka", None, "col"),
        P(None, "row", "col"),
        P(),
    )
    sizes = tuple(mesh.shape[name] for name in ("ka", "row", "col"))
    return jax.shard_map(
        functools.partial(local, sizes), mesh=mesh, in_specs=placed,
        out_specs=P("ka", None, "col", None), check_vma=False,
    )
```

```python
import functools
import math

import jax
import jax.numpy as jnp
from jax import lax
from jax.experimental import pallas as pl
from jax.experimental.pallas import tpu as pltpu
from jax.sharding import PartitionSpec as P

BF16 = jnp.bfloat16
F32 = jnp.float32
LANES = 128
ROWS = 16
TILE = 128
CHUNK = 256
QUARTERS = 4
MIB = 2**20
JOIN_FLOPS = 2 * 10**10
SPREAD_FLOPS = 2 * 10**10
IN_HBM = pl.BlockSpec(memory_space=pltpu.HBM)
IN_VMEM = pl.BlockSpec(memory_space=pltpu.VMEM)
IN_SMEM = pl.BlockSpec(memory_space=pltpu.SMEM)


def swap(value, axis, size, flip):
    return lax.ppermute(value, axis, [(i, i ^ flip) for i in range(size)])


def run(copies):
    for copy in copies:
        copy.start()
    for copy in copies:
        copy.wait()


def pack_kernel(sizes, exciton_ref, cond_ref, val_ref, core_ref, plane_ref, sems):
    n_row, n_col = sizes
    row, col = lax.axis_index("row"), lax.axis_index("col")
    part = plane_ref.shape[0]
    rows = pl.ds(pl.multiple_of(row * part, part), part)
    copies, at = [pltpu.make_async_copy(val_ref.at[rows, :], plane_ref, sems.at[0])], 0
    for source in (cond_ref, exciton_ref):
        part = source.shape[0] // n_col
        rows = pl.ds(pl.multiple_of(col * part, part), part)
        for block in range(source.shape[1] // LANES):
            copies.append(pltpu.make_async_copy(
                source.at[rows, block * LANES:(block + 1) * LANES],
                core_ref.at[at:at + part, :], sems.at[len(copies)],
            ))
            at += part
    run(copies)


def join_kernel(*refs):
    *parts, out = refs
    at = 0
    for part in parts:
        out[at:at + part.shape[0], :] = part[...]
        at += part.shape[0]


def join(parts):
    shape = (sum(part.shape[0] for part in parts), parts[0].shape[1])
    return pl.pallas_call(
        join_kernel,
        in_specs=[IN_VMEM] * len(parts),
        out_specs=IN_VMEM,
        out_shape=jax.ShapeDtypeStruct(shape, BF16),
        compiler_params=pltpu.CompilerParams(vmem_limit_bytes=4 * MIB),
        cost_estimate=pl.CostEstimate(flops=JOIN_FLOPS, bytes_accessed=0, transcendentals=0),
        name="join",
    )(*parts)


def spread_kernel(n_row, *refs):
    *parts, out = refs
    row = lax.axis_index("row")
    part = out.shape[1] // n_row
    for other in range(n_row):
        rows = pl.ds(pl.multiple_of((row ^ other) * part, part), part)
        for flip in range(out.shape[0]):
            out[flip, rows, :] = parts[other][flip * part:(flip + 1) * part, :]


def load_kernel(q_ref, w_ref, exciton_ref, cond_ref, val_ref, after_ref, w, x, cond, val, sems):
    del after_ref
    me, n_ka = lax.axis_index("ka"), w.shape[0]
    pairs = [(w_ref.at[q_ref[me ^ flip, me]], w.at[flip]) for flip in range(n_ka)]
    pairs += [(exciton_ref, x), (cond_ref, cond), (val_ref, val)]
    run([
        pltpu.make_async_copy(source, target, sems.at[i])
        for i, (source, target) in enumerate(pairs)
    ])


def after_kernel(*refs):
    refs[-1][...] = refs[0][...]


def after(value, *others, flops=0):
    return pl.pallas_call(
        after_kernel,
        in_specs=[IN_VMEM] + [pl.BlockSpec(memory_space=pl.ANY)] * len(others),
        out_specs=IN_VMEM,
        out_shape=jax.ShapeDtypeStruct(value.shape, value.dtype),
        compiler_params=pltpu.CompilerParams(vmem_limit_bytes=4 * MIB),
        cost_estimate=pl.CostEstimate(flops=flops, bytes_accessed=0, transcendentals=0),
        name="after",
    )(value, *others)


def direct_kernel(sizes, factor, *refs):
    n_ka, n_row, n_col = sizes
    refs = list(refs)

    def take(count):
        taken, refs[:] = refs[:count], refs[count:]
        return taken

    w, exciton_ref, cond_ref, val_ref = take(4)
    cores = [take(n_col) for _ in range(1, n_ka)]
    spread_ref, = take(1)
    keep, *sent = take(n_col)
    x_all, cond_all, val_all, panels, products, direct, total = refs
    col = lax.axis_index("col")
    n_v, n_nu = val_ref.shape
    n_c, n_mu = cond_ref.shape
    n_b = exciton_ref.shape[0] // n_v
    n_tiles = n_mu // TILE

    x_all[0] = exciton_ref[...]
    cond_all[0] = cond_ref[...]
    val_all[0] = val_ref[...]
    part_c, part_x = n_c // n_col, exciton_ref.shape[0] // n_col
    for flip in range(1, n_ka):
        for other in range(n_col):
            source, at = cores[flip - 1][other], 0
            rows = pl.ds(pl.multiple_of((col ^ other) * part_c, part_c), part_c)
            for block in range(n_mu // LANES):
                cond_all[flip, rows, block * LANES:(block + 1) * LANES] = source[at:at + part_c, :]
                at += part_c
            rows = pl.ds(pl.multiple_of((col ^ other) * part_x, part_x), part_x)
            x_all[flip, rows, :] = source[at:at + part_x, :]
    val_all[1:] = spread_ref[...]
    total[...] = jnp.zeros_like(total)

    steps = [(t, j) for t in range(n_tiles) for j in range(n_nu // CHUNK)]
    quarter = TILE // QUARTERS

    def set_panels(t):
        for flip in range(n_ka):
            by_point = lax.dot_general(
                cond_all[flip, :, t * TILE:(t + 1) * TILE], x_all[flip],
                (((0,), (1,)), ((), ())), preferred_element_type=F32,
            ).astype(BF16)
            for b in range(n_b):
                panels[t % 2, flip, b * TILE:(b + 1) * TILE, :] = by_point[:, b * n_v:(b + 1) * n_v]

    def multiply(number, flip):
        t, j = steps[number]
        products[number % 2, flip] = jnp.dot(
            panels[t % 2, flip], val_all[flip, :, j * CHUNK:(j + 1) * CHUNK],
            preferred_element_type=F32,
        )

    def combine(number, part):
        t, j = steps[number]
        at = slice(j * CHUNK, (j + 1) * CHUNK)
        for m in range(part * quarter, (part + 1) * quarter, ROWS):
            weights = [
                w[flip, t * TILE + m:t * TILE + m + ROWS, at].astype(F32) for flip in range(n_ka)
            ]
            for b in range(n_b):
                rows = slice(b * TILE + m, b * TILE + m + ROWS)
                value = products[number % 2, 0, rows, :] * weights[0]
                for flip in range(1, n_ka):
                    value += products[number % 2, flip, rows, :] * weights[flip]
                direct[t % 2, rows, at] = value.astype(BF16)

    def reduce(t):
        half = lax.dot_general(
            direct[t % 2], val_all[0], (((1,), (1,)), ((), ())), preferred_element_type=F32
        ).astype(BF16)
        cond_tile = cond_all[0, :, t * TILE:(t + 1) * TILE]
        for b in range(n_b):
            total[b] += lax.dot_general(
                half[b * TILE:(b + 1) * TILE, :], cond_tile,
                (((0,), (1,)), ((), ())), preferred_element_type=F32,
            )

    set_panels(0)
    for flip in range(n_ka):
        multiply(0, flip)
    for number, (t, j) in enumerate(steps):
        more = number + 1 < len(steps)
        if more and steps[number + 1][0] != t:
            set_panels(t + 1)
        for i in range(max(n_ka, QUARTERS)):
            if more and i < n_ka:
                multiply(number + 1, i)
            if i < QUARTERS:
                combine(number, i)
        if not more or steps[number + 1][0] != t:
            reduce(t)

    part = n_v // n_col
    for other in range(n_col):
        place = pl.multiple_of((col ^ other) * part, part)
        value = total[:, pl.ds(place, part), :] * factor
        if other == 0:
            keep[...] = value
        else:
            sent[other - 1][...] = value.astype(BF16)


def local(sizes, exciton, orb_cond, orb_val, screened, q_table):
    n_ka, n_row, n_col = sizes
    n_b, n_v, n_c = exciton.shape[1:]
    x_rows, cond, val, screened, q_table = (
        pltpu.with_memory_space_constraint(array, pltpu.HBM)
        for array in (exciton.reshape(n_b * n_v, n_c), orb_cond[0], orb_val[0], screened, q_table)
    )
    n_mu, n_nu = cond.shape[1], val.shape[1]
    core_rows = (cond.size + x_rows.size) // n_col // LANES
    core, plane = pl.pallas_call(
        functools.partial(pack_kernel, (n_row, n_col)),
        in_specs=[IN_HBM] * 3,
        out_specs=[IN_VMEM] * 2,
        out_shape=[
            jax.ShapeDtypeStruct((core_rows, LANES), BF16),
            jax.ShapeDtypeStruct((n_v // n_row, n_nu), BF16),
        ],
        scratch_shapes=[pltpu.SemaphoreType.DMA(((n_mu + n_c) // LANES + 1,))],
        compiler_params=pltpu.CompilerParams(vmem_limit_bytes=4 * MIB),
        name="pack",
    )(x_rows, cond, val)
    planes = [swap(plane, "ka", n_ka, flip) for flip in range(1, n_ka)]
    joined = join(planes)
    cores = [core]
    for flip in range(1, n_ka):
        last = flip & -flip
        source = cores[flip - last]
        if flip == last:
            source = after(source, planes[flip - 1])
        cores.append(swap(source, "ka", n_ka, last))
        if flip == 2:
            cores[2] = after(cores[2], joined, cores[1])
    loaded = pl.pallas_call(
        load_kernel,
        in_specs=[IN_SMEM] + [IN_HBM] * 4 + [pl.BlockSpec(memory_space=pl.ANY)],
        out_specs=[IN_VMEM] * 4,
        out_shape=[
            jax.ShapeDtypeStruct(block.shape, BF16) for block in (screened, x_rows, cond, val)
        ],
        scratch_shapes=[pltpu.SemaphoreType.DMA((n_ka + 3,))],
        compiler_params=pltpu.CompilerParams(vmem_limit_bytes=8 * MIB),
        cost_estimate=pl.CostEstimate(
            flops=0, bytes_accessed=4 * screened.size, transcendentals=0
        ),
        name="load",
    )(q_table, screened, x_rows, cond, val, cores[n_ka // 2])
    operands = []
    for core in cores[1:]:
        operands += [swap(core, "col", n_col, d) if d else core for d in range(n_col)]
    parts = [swap(joined, "row", n_row, d) if d else joined for d in range(n_row)]
    operands.append(pl.pallas_call(
        functools.partial(spread_kernel, n_row),
        in_specs=[IN_VMEM] * n_row,
        out_specs=IN_VMEM,
        out_shape=jax.ShapeDtypeStruct((n_ka - 1, *val.shape), BF16),
        compiler_params=pltpu.CompilerParams(vmem_limit_bytes=4 * MIB),
        cost_estimate=pl.CostEstimate(flops=SPREAD_FLOPS, bytes_accessed=0, transcendentals=0),
        name="spread",
    )(*parts))

    factor = math.sqrt(n_v * n_c) / (n_mu * n_row)
    part = n_v // n_col
    kept, *sent = pl.pallas_call(
        functools.partial(direct_kernel, sizes, factor),
        in_specs=[IN_VMEM] * (len(loaded) + len(operands)),
        out_specs=[IN_VMEM] * n_col,
        out_shape=[jax.ShapeDtypeStruct((n_b, part, n_c), F32)]
        + [jax.ShapeDtypeStruct((n_b, part, n_c), BF16)] * (n_col - 1),
        scratch_shapes=[
            pltpu.VMEM((n_ka, n_b * n_v, n_c), BF16),
            pltpu.VMEM((n_ka, n_c, n_mu), BF16),
            pltpu.VMEM((n_ka, n_v, n_nu), BF16),
            pltpu.VMEM((2, n_ka, n_b * TILE, n_v), BF16),
            pltpu.VMEM((2, n_ka, n_b * TILE, CHUNK), F32),
            pltpu.VMEM((2, n_b * TILE, n_nu), BF16),
            pltpu.VMEM((n_b, n_v, n_c), F32),
        ],
        compiler_params=pltpu.CompilerParams(vmem_limit_bytes=36 * MIB),
        name="direct_term",
    )(*loaded, *operands)
    mine = kept
    for flip in range(1, n_col):
        mine = mine + swap(sent[flip - 1], "col", n_col, flip).astype(F32)
    mine = mine.astype(BF16)
    terms = [after(swap(mine, "row", n_row, n_row - 1), flops=JOIN_FLOPS)]
    terms += [swap(mine, "row", n_row, flip) for flip in reversed(range(1, n_row - 1))] + [mine]
    terms = [term.astype(F32) for term in terms]
    while len(terms) > 1:
        terms = [a + b for a, b in zip(terms[::2], terms[1::2])]
    return terms[0][None]


def solution(mesh):
    placed = (
        P("ka", None, None, None),
        P("ka", None, "row"),
        P("ka", None, "col"),
        P(None, "row", "col"),
        P(),
    )
    sizes = tuple(mesh.shape[name] for name in ("ka", "row", "col"))
    return jax.shard_map(
        functools.partial(local, sizes), mesh=mesh, in_specs=placed,
        out_specs=P("ka", None, "col", None), check_vma=False,
    )
```

```python
import functools
import math

import jax
import jax.numpy as jnp
from jax import lax
from jax.experimental import pallas as pl
from jax.experimental.pallas import tpu as pltpu
from jax.sharding import PartitionSpec as P

BF16 = jnp.bfloat16
F32 = jnp.float32
LANES = 128
ROWS = 16
TILE = 128
CHUNK = 256
QUARTERS = 4
MIB = 2**20
JOIN_FLOPS = 2 * 10**10
SPREAD_FLOPS = 2 * 10**10
IN_HBM = pl.BlockSpec(memory_space=pltpu.HBM)
IN_VMEM = pl.BlockSpec(memory_space=pltpu.VMEM)
IN_SMEM = pl.BlockSpec(memory_space=pltpu.SMEM)


def swap(value, axis, size, flip):
    return lax.ppermute(value, axis, [(i, i ^ flip) for i in range(size)])


def run(copies):
    for copy in copies:
        copy.start()
    for copy in copies:
        copy.wait()


def pack_kernel(sizes, exciton_ref, cond_ref, val_ref, core_ref, plane_ref, sems):
    n_row, n_col = sizes
    row, col = lax.axis_index("row"), lax.axis_index("col")
    part = plane_ref.shape[0]
    rows = pl.ds(pl.multiple_of(row * part, part), part)
    copies, at = [pltpu.make_async_copy(val_ref.at[rows, :], plane_ref, sems.at[0])], 0
    for source in (cond_ref, exciton_ref):
        part = source.shape[0] // n_col
        rows = pl.ds(pl.multiple_of(col * part, part), part)
        for block in range(source.shape[1] // LANES):
            copies.append(pltpu.make_async_copy(
                source.at[rows, block * LANES:(block + 1) * LANES],
                core_ref.at[at:at + part, :], sems.at[len(copies)],
            ))
            at += part
    run(copies)


def join_kernel(*refs):
    *parts, out = refs
    at = 0
    for part in parts:
        out[at:at + part.shape[0], :] = part[...]
        at += part.shape[0]


def join(parts):
    shape = (sum(part.shape[0] for part in parts), parts[0].shape[1])
    return pl.pallas_call(
        join_kernel,
        in_specs=[IN_VMEM] * len(parts),
        out_specs=IN_VMEM,
        out_shape=jax.ShapeDtypeStruct(shape, BF16),
        compiler_params=pltpu.CompilerParams(vmem_limit_bytes=4 * MIB),
        cost_estimate=pl.CostEstimate(flops=JOIN_FLOPS, bytes_accessed=0, transcendentals=0),
        name="join",
    )(*parts)


def spread_kernel(n_row, *refs):
    *parts, out = refs
    row = lax.axis_index("row")
    part = out.shape[1] // n_row
    for other in range(n_row):
        rows = pl.ds(pl.multiple_of((row ^ other) * part, part), part)
        for flip in range(out.shape[0]):
            out[flip, rows, :] = parts[other][flip * part:(flip + 1) * part, :]


def set_panels(panels, cond_tile, exciton, n_v):
    by_point = lax.dot_general(
        cond_tile, exciton, (((0,), (1,)), ((), ())), preferred_element_type=F32
    ).astype(BF16)
    for b in range(exciton.shape[0] // n_v):
        panels[b * TILE:(b + 1) * TILE, :] = by_point[:, b * n_v:(b + 1) * n_v]


def own_kernel(
    q_ref, w_ref, exciton_ref, cond_ref, val_ref, after_ref, sums, w, cond, val, w_own, exciton, panels, sems
):
    del after_ref
    me, n_others = lax.axis_index("ka"), w.shape[0]
    pairs = [(exciton_ref, exciton), (cond_ref, cond), (val_ref, val)]
    pairs += [(w_ref.at[q_ref[me, me]], w_own)]
    pairs += [(w_ref.at[q_ref[me ^ flip, me]], w.at[flip - 1]) for flip in range(1, n_others + 1)]
    copies = [
        pltpu.make_async_copy(source, target, sems.at[i])
        for i, (source, target) in enumerate(pairs)
    ]
    for copy in copies:
        copy.start()
    for copy in copies[:4]:
        copy.wait()
    n_v, n_nu = val.shape
    n_b = exciton.shape[0] // n_v
    for t in range(cond.shape[1] // TILE):
        set_panels(panels.at[t % 2], cond[:, t * TILE:(t + 1) * TILE], exciton[...], n_v)
        for j in range(n_nu // CHUNK):
            at = slice(j * CHUNK, (j + 1) * CHUNK)
            product = jnp.dot(panels[t % 2], val[:, at], preferred_element_type=F32)
            weights = w_own[t * TILE:(t + 1) * TILE, at].astype(F32)
            for b in range(n_b):
                rows = slice(b * TILE, (b + 1) * TILE)
                sums[t, rows, at] = product[rows, :] * weights
    for copy in copies[4:]:
        copy.wait()


def after_kernel(*refs):
    refs[-1][...] = refs[0][...]


def after(value, *others, flops=0):
    return pl.pallas_call(
        after_kernel,
        in_specs=[IN_VMEM] + [pl.BlockSpec(memory_space=pl.ANY)] * len(others),
        out_specs=IN_VMEM,
        out_shape=jax.ShapeDtypeStruct(value.shape, value.dtype),
        compiler_params=pltpu.CompilerParams(vmem_limit_bytes=4 * MIB),
        cost_estimate=pl.CostEstimate(flops=flops, bytes_accessed=0, transcendentals=0),
        name="after",
    )(value, *others)


def direct_kernel(sizes, factor, *refs):
    n_ka, n_row, n_col = sizes
    refs = list(refs)

    def take(count):
        taken, refs[:] = refs[:count], refs[count:]
        return taken

    sums, w, cond_own, val_own = take(4)
    cores = [take(n_col) for _ in range(1, n_ka)]
    val_ref, = take(1)
    keep, *sent = take(n_col)
    x_all, cond_all, panels, products, direct, half = refs
    col = lax.axis_index("col")
    n_v, n_nu = val_own.shape
    n_c, n_mu = cond_own.shape
    n_b = x_all.shape[1] // n_v
    n_tiles, n_others = n_mu // TILE, n_ka - 1

    part_c, part_x = n_c // n_col, x_all.shape[1] // n_col
    for i in range(n_others):
        for other in range(n_col):
            source, at = cores[i][other], 0
            rows = pl.ds(pl.multiple_of((col ^ other) * part_c, part_c), part_c)
            for block in range(n_mu // LANES):
                cond_all[i, rows, block * LANES:(block + 1) * LANES] = source[at:at + part_c, :]
                at += part_c
            rows = pl.ds(pl.multiple_of((col ^ other) * part_x, part_x), part_x)
            x_all[i, rows, :] = source[at:at + part_x, :]

    steps = [(t, j) for t in range(n_tiles) for j in range(n_nu // CHUNK)]
    quarter = TILE // QUARTERS

    def all_panels(t):
        for i in range(n_others):
            set_panels(panels.at[t % 2, i], cond_all[i, :, t * TILE:(t + 1) * TILE], x_all[i], n_v)

    def multiply(number, i):
        t, j = steps[number]
        products[number % 2, i] = jnp.dot(
            panels[t % 2, i], val_ref[i, :, j * CHUNK:(j + 1) * CHUNK],
            preferred_element_type=F32,
        )

    def combine(number, part):
        t, j = steps[number]
        at = slice(j * CHUNK, (j + 1) * CHUNK)
        for m in range(part * quarter, (part + 1) * quarter, ROWS):
            weights = [
                w[i, t * TILE + m:t * TILE + m + ROWS, at].astype(F32) for i in range(n_others)
            ]
            for b in range(n_b):
                rows = slice(b * TILE + m, b * TILE + m + ROWS)
                value = sums[t, rows, at]
                for i in range(n_others):
                    value += products[number % 2, i, rows, :] * weights[i]
                direct[t % 2, rows, at] = value.astype(BF16)

    def reduce(t):
        value = lax.dot_general(
            direct[t % 2], val_own[...], (((1,), (1,)), ((), ())), preferred_element_type=F32
        ).astype(BF16)
        for b in range(n_b):
            half[b, t * TILE:(t + 1) * TILE, :] = value[b * TILE:(b + 1) * TILE, :]

    all_panels(0)
    for i in range(n_others):
        multiply(0, i)
    for number, (t, j) in enumerate(steps):
        more = number + 1 < len(steps)
        if more and steps[number + 1][0] != t:
            all_panels(t + 1)
        for i in range(max(n_others, QUARTERS)):
            if more and i < n_others:
                multiply(number + 1, i)
            if i < QUARTERS:
                combine(number, i)
        if not more or steps[number + 1][0] != t:
            reduce(t)

    part = n_v // n_col
    for b in range(n_b):
        total = jnp.dot(cond_own[...], half[b], preferred_element_type=F32) * factor
        products[0, 0, b * n_v:(b + 1) * n_v, :n_c] = total.T
        for other in range(n_col):
            rows = pl.ds(pl.multiple_of(b * n_v + (col ^ other) * part, part), part)
            value = products[0, 0, rows, :n_c]
            if other == 0:
                keep[b] = value
            else:
                sent[other - 1][b] = value.astype(BF16)


def local(sizes, exciton, orb_cond, orb_val, screened, q_table):
    n_ka, n_row, n_col = sizes
    n_b, n_v, n_c = exciton.shape[1:]
    x_rows, cond, val, screened, q_table = (
        pltpu.with_memory_space_constraint(array, pltpu.HBM)
        for array in (exciton.reshape(n_b * n_v, n_c), orb_cond[0], orb_val[0], screened, q_table)
    )
    n_mu, n_nu = cond.shape[1], val.shape[1]
    core_rows = (cond.size + x_rows.size) // n_col // LANES
    core, plane = pl.pallas_call(
        functools.partial(pack_kernel, (n_row, n_col)),
        in_specs=[IN_HBM] * 3,
        out_specs=[IN_VMEM] * 2,
        out_shape=[
            jax.ShapeDtypeStruct((core_rows, LANES), BF16),
            jax.ShapeDtypeStruct((n_v // n_row, n_nu), BF16),
        ],
        scratch_shapes=[pltpu.SemaphoreType.DMA(((n_mu + n_c) // LANES + 1,))],
        compiler_params=pltpu.CompilerParams(vmem_limit_bytes=4 * MIB),
        name="pack",
    )(x_rows, cond, val)
    planes = [swap(plane, "ka", n_ka, flip) for flip in range(1, n_ka)]
    joined = join(planes)
    cores = [core]
    for flip in range(1, n_ka):
        last = flip & -flip
        source = cores[flip - last]
        if flip == last:
            source = after(source, planes[flip - 1])
        cores.append(swap(source, "ka", n_ka, last))
        if flip == 2:
            cores[2] = after(cores[2], joined, cores[1])
    n_tiles = n_mu // TILE
    loaded = pl.pallas_call(
        own_kernel,
        in_specs=[IN_SMEM] + [IN_HBM] * 4 + [pl.BlockSpec(memory_space=pl.ANY)],
        out_specs=[IN_VMEM] * 4,
        out_shape=[
            jax.ShapeDtypeStruct((n_tiles, n_b * TILE, n_nu), F32),
            jax.ShapeDtypeStruct((n_ka - 1, n_mu, n_nu), BF16),
            jax.ShapeDtypeStruct(cond.shape, BF16),
            jax.ShapeDtypeStruct(val.shape, BF16),
        ],
        scratch_shapes=[
            pltpu.VMEM((n_mu, n_nu), BF16),
            pltpu.VMEM(x_rows.shape, BF16),
            pltpu.VMEM((2, n_b * TILE, n_v), BF16),
            pltpu.SemaphoreType.DMA((n_ka + 3,)),
        ],
        compiler_params=pltpu.CompilerParams(vmem_limit_bytes=24 * MIB),
        cost_estimate=pl.CostEstimate(
            flops=0, bytes_accessed=4 * screened.size, transcendentals=0
        ),
        name="own_term",
    )(q_table, screened, x_rows, cond, val, cores[n_ka // 2])
    operands = []
    for core in cores[1:]:
        operands += [swap(core, "col", n_col, d) if d else core for d in range(n_col)]
    parts = [swap(joined, "row", n_row, d) if d else joined for d in range(n_row)]
    operands.append(pl.pallas_call(
        functools.partial(spread_kernel, n_row),
        in_specs=[IN_VMEM] * n_row,
        out_specs=IN_VMEM,
        out_shape=jax.ShapeDtypeStruct((n_ka - 1, *val.shape), BF16),
        compiler_params=pltpu.CompilerParams(vmem_limit_bytes=4 * MIB),
        cost_estimate=pl.CostEstimate(flops=SPREAD_FLOPS, bytes_accessed=0, transcendentals=0),
        name="spread",
    )(*parts))

    factor = math.sqrt(n_v * n_c) / (n_mu * n_row)
    part = n_v // n_col
    kept, *sent = pl.pallas_call(
        functools.partial(direct_kernel, sizes, factor),
        in_specs=[IN_VMEM] * (len(loaded) + len(operands)),
        out_specs=[IN_VMEM] * n_col,
        out_shape=[jax.ShapeDtypeStruct((n_b, part, n_c), F32)]
        + [jax.ShapeDtypeStruct((n_b, part, n_c), BF16)] * (n_col - 1),
        scratch_shapes=[
            pltpu.VMEM((n_ka - 1, n_b * n_v, n_c), BF16),
            pltpu.VMEM((n_ka - 1, n_c, n_mu), BF16),
            pltpu.VMEM((2, n_ka - 1, n_b * TILE, n_v), BF16),
            pltpu.VMEM((2, n_ka - 1, n_b * TILE, CHUNK), F32),
            pltpu.VMEM((2, n_b * TILE, n_nu), BF16),
            pltpu.VMEM((n_b, n_mu, n_v), BF16),
        ],
        compiler_params=pltpu.CompilerParams(vmem_limit_bytes=36 * MIB),
        name="direct_term",
    )(*loaded, *operands)
    mine = kept
    for flip in range(1, n_col):
        mine = mine + swap(sent[flip - 1], "col", n_col, flip).astype(F32)
    mine = mine.astype(BF16)
    terms = [after(swap(mine, "row", n_row, n_row - 1), flops=JOIN_FLOPS)]
    terms += [swap(mine, "row", n_row, flip) for flip in reversed(range(1, n_row - 1))] + [mine]
    terms = [term.astype(F32) for term in terms]
    while len(terms) > 1:
        terms = [a + b for a, b in zip(terms[::2], terms[1::2])]
    return terms[0][None]


def solution(mesh):
    placed = (
        P("ka", None, None, None),
        P("ka", None, "row"),
        P("ka", None, "col"),
        P(None, "row", "col"),
        P(),
    )
    sizes = tuple(mesh.shape[name] for name in ("ka", "row", "col"))
    return jax.shard_map(
        functools.partial(local, sizes), mesh=mesh, in_specs=placed,
        out_specs=P("ka", None, "col", None), check_vma=False,
    )
```

```python
import functools
import math

import jax
import jax.numpy as jnp
from jax import lax
from jax.experimental import pallas as pl
from jax.experimental.pallas import tpu as pltpu
from jax.sharding import PartitionSpec as P

BF16 = jnp.bfloat16
F32 = jnp.float32
LANES = 128
ROWS = 16
TILE = 256
CHUNK = 256
QUARTERS = 4
MIB = 2**20
JOIN_FLOPS = 2 * 10**10
SPREAD_FLOPS = 2 * 10**10
IN_HBM = pl.BlockSpec(memory_space=pltpu.HBM)
IN_VMEM = pl.BlockSpec(memory_space=pltpu.VMEM)
IN_SMEM = pl.BlockSpec(memory_space=pltpu.SMEM)


def swap(value, axis, size, flip):
    return lax.ppermute(value, axis, [(i, i ^ flip) for i in range(size)])


def run(copies):
    for copy in copies:
        copy.start()
    for copy in copies:
        copy.wait()


def pack_kernel(sizes, exciton_ref, cond_ref, val_ref, core_ref, plane_ref, sems):
    n_row, n_col = sizes
    row, col = lax.axis_index("row"), lax.axis_index("col")
    part = plane_ref.shape[0]
    rows = pl.ds(pl.multiple_of(row * part, part), part)
    copies, at = [pltpu.make_async_copy(val_ref.at[rows, :], plane_ref, sems.at[0])], 0
    for source in (cond_ref, exciton_ref):
        part = source.shape[0] // n_col
        rows = pl.ds(pl.multiple_of(col * part, part), part)
        for block in range(source.shape[1] // LANES):
            copies.append(pltpu.make_async_copy(
                source.at[rows, block * LANES:(block + 1) * LANES],
                core_ref.at[at:at + part, :], sems.at[len(copies)],
            ))
            at += part
    run(copies)


def join_kernel(*refs):
    *parts, out = refs
    at = 0
    for part in parts:
        out[at:at + part.shape[0], :] = part[...]
        at += part.shape[0]


def join(parts):
    shape = (sum(part.shape[0] for part in parts), parts[0].shape[1])
    return pl.pallas_call(
        join_kernel,
        in_specs=[IN_VMEM] * len(parts),
        out_specs=IN_VMEM,
        out_shape=jax.ShapeDtypeStruct(shape, BF16),
        compiler_params=pltpu.CompilerParams(vmem_limit_bytes=4 * MIB),
        cost_estimate=pl.CostEstimate(flops=JOIN_FLOPS, bytes_accessed=0, transcendentals=0),
        name="join",
    )(*parts)


def spread_kernel(n_row, *refs):
    *parts, out = refs
    row = lax.axis_index("row")
    part = out.shape[1] // n_row
    for other in range(n_row):
        rows = pl.ds(pl.multiple_of((row ^ other) * part, part), part)
        for flip in range(out.shape[0]):
            out[flip, rows, :] = parts[other][flip * part:(flip + 1) * part, :]


def set_panels(panels, cond_tile, exciton, n_v):
    by_point = lax.dot_general(
        cond_tile, exciton, (((0,), (1,)), ((), ())), preferred_element_type=F32
    ).astype(BF16)
    for b in range(exciton.shape[0] // n_v):
        panels[b * TILE:(b + 1) * TILE, :] = by_point[:, b * n_v:(b + 1) * n_v]


def own_kernel(
    q_ref, w_ref, exciton_ref, cond_ref, val_ref, after_ref, sums, w, cond, val, w_own, exciton, panels, sems
):
    del after_ref
    me, n_others = lax.axis_index("ka"), w.shape[0]
    pairs = [(exciton_ref, exciton), (cond_ref, cond), (val_ref, val)]
    pairs += [(w_ref.at[q_ref[me, me]], w_own)]
    pairs += [(w_ref.at[q_ref[me ^ flip, me]], w.at[flip - 1]) for flip in range(1, n_others + 1)]
    copies = [
        pltpu.make_async_copy(source, target, sems.at[i])
        for i, (source, target) in enumerate(pairs)
    ]
    for copy in copies:
        copy.start()
    for copy in copies[:4]:
        copy.wait()
    n_v, n_nu = val.shape
    n_b = exciton.shape[0] // n_v
    for t in range(cond.shape[1] // TILE):
        set_panels(panels.at[t % 2], cond[:, t * TILE:(t + 1) * TILE], exciton[...], n_v)
        for j in range(n_nu // CHUNK):
            at = slice(j * CHUNK, (j + 1) * CHUNK)
            product = jnp.dot(panels[t % 2], val[:, at], preferred_element_type=F32)
            weights = w_own[t * TILE:(t + 1) * TILE, at].astype(F32)
            for b in range(n_b):
                rows = slice(b * TILE, (b + 1) * TILE)
                sums[t, rows, at] = product[rows, :] * weights
    for copy in copies[4:]:
        copy.wait()


def after_kernel(*refs):
    refs[-1][...] = refs[0][...]


def after(value, *others, flops=0):
    return pl.pallas_call(
        after_kernel,
        in_specs=[IN_VMEM] + [pl.BlockSpec(memory_space=pl.ANY)] * len(others),
        out_specs=IN_VMEM,
        out_shape=jax.ShapeDtypeStruct(value.shape, value.dtype),
        compiler_params=pltpu.CompilerParams(vmem_limit_bytes=4 * MIB),
        cost_estimate=pl.CostEstimate(flops=flops, bytes_accessed=0, transcendentals=0),
        name="after",
    )(value, *others)


def direct_kernel(sizes, factor, *refs):
    n_ka, n_row, n_col = sizes
    refs = list(refs)

    def take(count):
        taken, refs[:] = refs[:count], refs[count:]
        return taken

    sums, w, cond_own, val_own = take(4)
    cores = [take(n_col) for _ in range(1, n_ka)]
    val_ref, = take(1)
    keep, *sent = take(n_col)
    x_all, cond_all, panels, products, direct, half, total = refs
    col = lax.axis_index("col")
    n_v, n_nu = val_own.shape
    n_c, n_mu = cond_own.shape
    n_b = x_all.shape[1] // n_v
    n_tiles, n_others = n_mu // TILE, n_ka - 1

    part_c, part_x = n_c // n_col, x_all.shape[1] // n_col
    for i in range(n_others):
        for other in range(n_col):
            source, at = cores[i][other], 0
            rows = pl.ds(pl.multiple_of((col ^ other) * part_c, part_c), part_c)
            for block in range(n_mu // LANES):
                cond_all[i, rows, block * LANES:(block + 1) * LANES] = source[at:at + part_c, :]
                at += part_c
            rows = pl.ds(pl.multiple_of((col ^ other) * part_x, part_x), part_x)
            x_all[i, rows, :] = source[at:at + part_x, :]

    steps = [(t, j) for t in range(n_tiles) for j in range(n_nu // CHUNK)]
    quarter = TILE // QUARTERS

    def all_panels(t):
        for i in range(n_others):
            set_panels(panels.at[t % 2, i], cond_all[i, :, t * TILE:(t + 1) * TILE], x_all[i], n_v)

    def multiply(number, i):
        t, j = steps[number]
        products[number % 2, i] = jnp.dot(
            panels[t % 2, i], val_ref[i, :, j * CHUNK:(j + 1) * CHUNK],
            preferred_element_type=F32,
        ).astype(BF16)

    def combine(number, part):
        t, j = steps[number]
        at = slice(j * CHUNK, (j + 1) * CHUNK)
        for m in range(part * quarter, (part + 1) * quarter, ROWS):
            weights = [
                w[i, t * TILE + m:t * TILE + m + ROWS, at].astype(F32) for i in range(n_others)
            ]
            for b in range(n_b):
                rows = slice(b * TILE + m, b * TILE + m + ROWS)
                value = sums[t, rows, at]
                for i in range(n_others):
                    value += products[number % 2, i, rows, :].astype(F32) * weights[i]
                direct[t % 2, rows, at] = value.astype(BF16)

    def reduce(t):
        value = lax.dot_general(
            direct[t % 2], val_own[...], (((1,), (1,)), ((), ())), preferred_element_type=F32
        ).astype(BF16)
        for b in range(n_b):
            half[b, t * TILE:(t + 1) * TILE, :] = value[b * TILE:(b + 1) * TILE, :]

    all_panels(0)
    for i in range(n_others):
        multiply(0, i)
    for number, (t, j) in enumerate(steps):
        more = number + 1 < len(steps)
        if more and steps[number + 1][0] != t:
            all_panels(t + 1)
        for i in range(max(n_others, QUARTERS)):
            if more and i < n_others:
                multiply(number + 1, i)
            if i < QUARTERS:
                combine(number, i)
        if not more or steps[number + 1][0] != t:
            reduce(t)

    part = n_v // n_col
    for b in range(n_b):
        total[b * n_v:(b + 1) * n_v, :] = (
            jnp.dot(cond_own[...], half[b], preferred_element_type=F32) * factor
        ).T
        for other in range(n_col):
            rows = pl.ds(pl.multiple_of(b * n_v + (col ^ other) * part, part), part)
            value = total[rows, :]
            if other == 0:
                keep[b] = value
            else:
                sent[other - 1][b] = value.astype(BF16)


def local(sizes, exciton, orb_cond, orb_val, screened, q_table):
    n_ka, n_row, n_col = sizes
    n_b, n_v, n_c = exciton.shape[1:]
    x_rows, cond, val, screened, q_table = (
        pltpu.with_memory_space_constraint(array, pltpu.HBM)
        for array in (exciton.reshape(n_b * n_v, n_c), orb_cond[0], orb_val[0], screened, q_table)
    )
    n_mu, n_nu = cond.shape[1], val.shape[1]
    core_rows = (cond.size + x_rows.size) // n_col // LANES
    core, plane = pl.pallas_call(
        functools.partial(pack_kernel, (n_row, n_col)),
        in_specs=[IN_HBM] * 3,
        out_specs=[IN_VMEM] * 2,
        out_shape=[
            jax.ShapeDtypeStruct((core_rows, LANES), BF16),
            jax.ShapeDtypeStruct((n_v // n_row, n_nu), BF16),
        ],
        scratch_shapes=[pltpu.SemaphoreType.DMA(((n_mu + n_c) // LANES + 1,))],
        compiler_params=pltpu.CompilerParams(vmem_limit_bytes=4 * MIB),
        name="pack",
    )(x_rows, cond, val)
    planes = [swap(plane, "ka", n_ka, flip) for flip in range(1, n_ka)]
    joined = join(planes)
    cores = [core]
    for flip in range(1, n_ka):
        last = flip & -flip
        source = cores[flip - last]
        if flip == last:
            source = after(source, planes[flip - 1])
        cores.append(swap(source, "ka", n_ka, last))
        if flip == 2:
            cores[2] = after(cores[2], joined, cores[1])
    n_tiles = n_mu // TILE
    loaded = pl.pallas_call(
        own_kernel,
        in_specs=[IN_SMEM] + [IN_HBM] * 4 + [pl.BlockSpec(memory_space=pl.ANY)],
        out_specs=[IN_VMEM] * 4,
        out_shape=[
            jax.ShapeDtypeStruct((n_tiles, n_b * TILE, n_nu), F32),
            jax.ShapeDtypeStruct((n_ka - 1, n_mu, n_nu), BF16),
            jax.ShapeDtypeStruct(cond.shape, BF16),
            jax.ShapeDtypeStruct(val.shape, BF16),
        ],
        scratch_shapes=[
            pltpu.VMEM((n_mu, n_nu), BF16),
            pltpu.VMEM(x_rows.shape, BF16),
            pltpu.VMEM((2, n_b * TILE, n_v), BF16),
            pltpu.SemaphoreType.DMA((n_ka + 3,)),
        ],
        compiler_params=pltpu.CompilerParams(vmem_limit_bytes=24 * MIB),
        cost_estimate=pl.CostEstimate(
            flops=0, bytes_accessed=4 * screened.size, transcendentals=0
        ),
        name="own_term",
    )(q_table, screened, x_rows, cond, val, cores[n_ka // 2])
    operands = []
    for core in cores[1:]:
        operands += [swap(core, "col", n_col, d) if d else core for d in range(n_col)]
    parts = [swap(joined, "row", n_row, d) if d else joined for d in range(n_row)]
    operands.append(pl.pallas_call(
        functools.partial(spread_kernel, n_row),
        in_specs=[IN_VMEM] * n_row,
        out_specs=IN_VMEM,
        out_shape=jax.ShapeDtypeStruct((n_ka - 1, *val.shape), BF16),
        compiler_params=pltpu.CompilerParams(vmem_limit_bytes=4 * MIB),
        cost_estimate=pl.CostEstimate(flops=SPREAD_FLOPS, bytes_accessed=0, transcendentals=0),
        name="spread",
    )(*parts))

    factor = math.sqrt(n_v * n_c) / (n_mu * n_row)
    part = n_v // n_col
    kept, *sent = pl.pallas_call(
        functools.partial(direct_kernel, sizes, factor),
        in_specs=[IN_VMEM] * (len(loaded) + len(operands)),
        out_specs=[IN_VMEM] * n_col,
        out_shape=[jax.ShapeDtypeStruct((n_b, part, n_c), F32)]
        + [jax.ShapeDtypeStruct((n_b, part, n_c), BF16)] * (n_col - 1),
        scratch_shapes=[
            pltpu.VMEM((n_ka - 1, n_b * n_v, n_c), BF16),
            pltpu.VMEM((n_ka - 1, n_c, n_mu), BF16),
            pltpu.VMEM((2, n_ka - 1, n_b * TILE, n_v), BF16),
            pltpu.VMEM((2, n_ka - 1, n_b * TILE, CHUNK), BF16),
            pltpu.VMEM((2, n_b * TILE, n_nu), BF16),
            pltpu.VMEM((n_b, n_mu, n_v), BF16),
            pltpu.VMEM((n_b * n_v, n_c), F32),
        ],
        compiler_params=pltpu.CompilerParams(vmem_limit_bytes=36 * MIB),
        name="direct_term",
    )(*loaded, *operands)
    mine = kept
    for flip in range(1, n_col):
        mine = mine + swap(sent[flip - 1], "col", n_col, flip).astype(F32)
    mine = mine.astype(BF16)
    terms = [after(swap(mine, "row", n_row, n_row - 1), flops=JOIN_FLOPS)]
    terms += [swap(mine, "row", n_row, flip) for flip in reversed(range(1, n_row - 1))] + [mine]
    terms = [term.astype(F32) for term in terms]
    while len(terms) > 1:
        terms = [a + b for a, b in zip(terms[::2], terms[1::2])]
    return terms[0][None]


def solution(mesh):
    placed = (
        P("ka", None, None, None),
        P("ka", None, "row"),
        P("ka", None, "col"),
        P(None, "row", "col"),
        P(),
    )
    sizes = tuple(mesh.shape[name] for name in ("ka", "row", "col"))
    return jax.shard_map(
        functools.partial(local, sizes), mesh=mesh, in_specs=placed,
        out_specs=P("ka", None, "col", None), check_vma=False,
    )
```

```python
import functools
import math

import jax
import jax.numpy as jnp
from jax import lax
from jax.experimental import pallas as pl
from jax.experimental.pallas import tpu as pltpu
from jax.sharding import PartitionSpec as P

BF16 = jnp.bfloat16
F32 = jnp.float32
LANES = 128
ROWS = 16
TILE = 256
CHUNK = 256
QUARTERS = 4
MIB = 2**20
JOIN_FLOPS = 2 * 10**10
SPREAD_FLOPS = 2 * 10**10
IN_HBM = pl.BlockSpec(memory_space=pltpu.HBM)
IN_VMEM = pl.BlockSpec(memory_space=pltpu.VMEM)
IN_SMEM = pl.BlockSpec(memory_space=pltpu.SMEM)


def swap(value, axis, size, flip):
    return lax.ppermute(value, axis, [(i, i ^ flip) for i in range(size)])


def run(copies):
    for copy in copies:
        copy.start()
    for copy in copies:
        copy.wait()


def pack_kernel(n_col, exciton_ref, cond_ref, after_ref, core_ref, sems):
    del after_ref
    col = lax.axis_index("col")
    copies, at = [], 0
    for source in (cond_ref, exciton_ref):
        part = source.shape[0] // n_col
        rows = pl.ds(pl.multiple_of(col * part, part), part)
        for block in range(source.shape[1] // LANES):
            copies.append(pltpu.make_async_copy(
                source.at[rows, block * LANES:(block + 1) * LANES],
                core_ref.at[at:at + part, :], sems.at[len(copies)],
            ))
            at += part
    run(copies)


def join_kernel(*refs):
    *parts, out = refs
    at = 0
    for part in parts:
        out[at:at + part.shape[0], :] = part[...]
        at += part.shape[0]


def join(parts):
    shape = (sum(part.shape[0] for part in parts), parts[0].shape[1])
    return pl.pallas_call(
        join_kernel,
        in_specs=[IN_VMEM] * len(parts),
        out_specs=IN_VMEM,
        out_shape=jax.ShapeDtypeStruct(shape, BF16),
        compiler_params=pltpu.CompilerParams(vmem_limit_bytes=4 * MIB),
        cost_estimate=pl.CostEstimate(flops=JOIN_FLOPS, bytes_accessed=0, transcendentals=0),
        name="join",
    )(*parts)


def spread_kernel(n_row, *refs):
    *parts, out = refs
    row = lax.axis_index("row")
    part = out.shape[1] // n_row
    for other in range(n_row):
        rows = pl.ds(pl.multiple_of((row ^ other) * part, part), part)
        for flip in range(out.shape[0]):
            out[flip, rows, :] = parts[other][flip * part:(flip + 1) * part, :]


def set_panels(panels, cond_tile, exciton, n_v):
    by_point = lax.dot_general(
        cond_tile, exciton, (((0,), (1,)), ((), ())), preferred_element_type=F32
    ).astype(BF16)
    for b in range(exciton.shape[0] // n_v):
        panels[b * TILE:(b + 1) * TILE, :] = by_point[:, b * n_v:(b + 1) * n_v]


def own_kernel(
    q_ref, w_ref, exciton_ref, cond_ref, val_ref, after_ref, sums, w, cond, val, w_own, exciton, panels, sems
):
    del after_ref
    me, n_others = lax.axis_index("ka"), w.shape[0]
    pairs = [(exciton_ref, exciton), (cond_ref, cond), (val_ref, val)]
    pairs += [(w_ref.at[q_ref[me, me]], w_own)]
    pairs += [(w_ref.at[q_ref[me ^ flip, me]], w.at[flip - 1]) for flip in range(1, n_others + 1)]
    copies = [
        pltpu.make_async_copy(source, target, sems.at[i])
        for i, (source, target) in enumerate(pairs)
    ]
    for copy in copies:
        copy.start()
    for copy in copies[:4]:
        copy.wait()
    n_v, n_nu = val.shape
    n_b = exciton.shape[0] // n_v
    for t in range(cond.shape[1] // TILE):
        set_panels(panels.at[t % 2], cond[:, t * TILE:(t + 1) * TILE], exciton[...], n_v)
        for j in range(n_nu // CHUNK):
            at = slice(j * CHUNK, (j + 1) * CHUNK)
            product = jnp.dot(panels[t % 2], val[:, at], preferred_element_type=F32)
            weights = w_own[t * TILE:(t + 1) * TILE, at].astype(F32)
            for b in range(n_b):
                rows = slice(b * TILE, (b + 1) * TILE)
                sums[t, rows, at] = product[rows, :] * weights
    for copy in copies[4:]:
        copy.wait()


def after_kernel(*refs):
    refs[-1][...] = refs[0][...]


def after(value, *others, flops=0):
    return pl.pallas_call(
        after_kernel,
        in_specs=[IN_VMEM] + [pl.BlockSpec(memory_space=pl.ANY)] * len(others),
        out_specs=IN_VMEM,
        out_shape=jax.ShapeDtypeStruct(value.shape, value.dtype),
        compiler_params=pltpu.CompilerParams(vmem_limit_bytes=4 * MIB),
        cost_estimate=pl.CostEstimate(flops=flops, bytes_accessed=0, transcendentals=0),
        name="after",
    )(value, *others)


def direct_kernel(sizes, factor, *refs):
    n_ka, n_row, n_col = sizes
    refs = list(refs)

    def take(count):
        taken, refs[:] = refs[:count], refs[count:]
        return taken

    sums, w, cond_own, val_own = take(4)
    cores = [take(n_col) for _ in range(1, n_ka)]
    val_ref, = take(1)
    keep, *sent = take(n_col)
    x_all, cond_all, panels, products, direct, running, half, total = refs
    col = lax.axis_index("col")
    n_v, n_nu = val_own.shape
    n_c, n_mu = cond_own.shape
    n_b = x_all.shape[1] // n_v
    n_tiles, n_others = n_mu // TILE, n_ka - 1

    part_c, part_x = n_c // n_col, x_all.shape[1] // n_col
    for i in range(n_others):
        for other in range(n_col):
            source, at = cores[i][other], 0
            rows = pl.ds(pl.multiple_of((col ^ other) * part_c, part_c), part_c)
            for block in range(n_mu // LANES):
                cond_all[i, rows, block * LANES:(block + 1) * LANES] = source[at:at + part_c, :]
                at += part_c
            rows = pl.ds(pl.multiple_of((col ^ other) * part_x, part_x), part_x)
            x_all[i, rows, :] = source[at:at + part_x, :]

    steps = [(t, j) for t in range(n_tiles) for j in range(n_nu // CHUNK)]
    quarter = TILE // QUARTERS

    def all_panels(t):
        for i in range(n_others):
            set_panels(panels.at[t % 2, i], cond_all[i, :, t * TILE:(t + 1) * TILE], x_all[i], n_v)

    def multiply(number, i):
        t, j = steps[number]
        products[number % 2, i] = jnp.dot(
            panels[t % 2, i], val_ref[i, :, j * CHUNK:(j + 1) * CHUNK],
            preferred_element_type=F32,
        ).astype(BF16)

    def combine(number, part):
        t, j = steps[number]
        at = slice(j * CHUNK, (j + 1) * CHUNK)
        for m in range(part * quarter, (part + 1) * quarter, ROWS):
            weights = [
                w[i, t * TILE + m:t * TILE + m + ROWS, at].astype(F32) for i in range(n_others)
            ]
            for b in range(n_b):
                rows = slice(b * TILE + m, b * TILE + m + ROWS)
                value = sums[t, rows, at]
                for i in range(n_others):
                    value += products[number % 2, i, rows, :].astype(F32) * weights[i]
                direct[t % 2, rows, at] = value.astype(BF16)

    def reduce(number):
        t, j = steps[number]
        at = slice(j * CHUNK, (j + 1) * CHUNK)
        value = lax.dot_general(
            direct[t % 2, :, at], val_own[:, at], (((1,), (1,)), ((), ())),
            preferred_element_type=F32,
        )
        if j:
            value += running[...]
        if j + 1 < n_nu // CHUNK:
            running[...] = value
            return
        value = value.astype(BF16)
        for b in range(n_b):
            half[b, t * TILE:(t + 1) * TILE, :] = value[b * TILE:(b + 1) * TILE, :]

    all_panels(0)
    for i in range(n_others):
        multiply(0, i)
    for number, (t, j) in enumerate(steps):
        more = number + 1 < len(steps)
        if more and steps[number + 1][0] != t:
            all_panels(t + 1)
        for i in range(max(n_others, QUARTERS)):
            if more and i < n_others:
                multiply(number + 1, i)
            if i < QUARTERS:
                combine(number, i)
        reduce(number)

    part = n_v // n_col
    for b in range(n_b):
        total[b * n_v:(b + 1) * n_v, :] = (
            jnp.dot(cond_own[...], half[b], preferred_element_type=F32) * factor
        ).T
        for other in range(n_col):
            rows = pl.ds(pl.multiple_of(b * n_v + (col ^ other) * part, part), part)
            value = total[rows, :]
            if other == 0:
                keep[b] = value
            else:
                sent[other - 1][b] = value.astype(BF16)


def local(sizes, exciton, orb_cond, orb_val, screened, q_table):
    n_ka, n_row, n_col = sizes
    n_b, n_v, n_c = exciton.shape[1:]
    x_rows, cond, val, screened, q_table = (
        pltpu.with_memory_space_constraint(array, pltpu.HBM)
        for array in (exciton.reshape(n_b * n_v, n_c), orb_cond[0], orb_val[0], screened, q_table)
    )
    n_mu, n_nu = cond.shape[1], val.shape[1]
    core_rows = (cond.size + x_rows.size) // n_col // LANES
    part = n_v // n_row
    plane = lax.dynamic_slice_in_dim(orb_val[0], lax.axis_index("row") * part, part, 0)
    planes = [swap(plane, "ka", n_ka, flip) for flip in range(1, n_ka)]
    core = pl.pallas_call(
        functools.partial(pack_kernel, n_col),
        in_specs=[IN_HBM] * 2 + [pl.BlockSpec(memory_space=pl.ANY)],
        out_specs=IN_VMEM,
        out_shape=jax.ShapeDtypeStruct((core_rows, LANES), BF16),
        scratch_shapes=[pltpu.SemaphoreType.DMA(((n_mu + n_c) // LANES,))],
        compiler_params=pltpu.CompilerParams(vmem_limit_bytes=4 * MIB),
        name="pack",
    )(x_rows, cond, planes[0])
    joined = join(planes)
    cores = [core]
    for flip in range(1, n_ka):
        last = flip & -flip
        source = cores[flip - last]
        if flip == last and flip > 1:
            source = after(source, planes[flip - 1])
        cores.append(swap(source, "ka", n_ka, last))
        if flip == 2:
            cores[2] = after(cores[2], joined, cores[1])
    n_tiles = n_mu // TILE
    loaded = pl.pallas_call(
        own_kernel,
        in_specs=[IN_SMEM] + [IN_HBM] * 4 + [pl.BlockSpec(memory_space=pl.ANY)],
        out_specs=[IN_VMEM] * 4,
        out_shape=[
            jax.ShapeDtypeStruct((n_tiles, n_b * TILE, n_nu), F32),
            jax.ShapeDtypeStruct((n_ka - 1, n_mu, n_nu), BF16),
            jax.ShapeDtypeStruct(cond.shape, BF16),
            jax.ShapeDtypeStruct(val.shape, BF16),
        ],
        scratch_shapes=[
            pltpu.VMEM((n_mu, n_nu), BF16),
            pltpu.VMEM(x_rows.shape, BF16),
            pltpu.VMEM((2, n_b * TILE, n_v), BF16),
            pltpu.SemaphoreType.DMA((n_ka + 3,)),
        ],
        compiler_params=pltpu.CompilerParams(vmem_limit_bytes=24 * MIB),
        cost_estimate=pl.CostEstimate(
            flops=0, bytes_accessed=4 * screened.size, transcendentals=0
        ),
        name="own_term",
    )(q_table, screened, x_rows, cond, val, cores[n_ka // 2])
    operands = []
    for core in cores[1:]:
        operands += [swap(core, "col", n_col, d) if d else core for d in range(n_col)]
    parts = [swap(joined, "row", n_row, d) if d else joined for d in range(n_row)]
    operands.append(pl.pallas_call(
        functools.partial(spread_kernel, n_row),
        in_specs=[IN_VMEM] * n_row,
        out_specs=IN_VMEM,
        out_shape=jax.ShapeDtypeStruct((n_ka - 1, *val.shape), BF16),
        compiler_params=pltpu.CompilerParams(vmem_limit_bytes=4 * MIB),
        cost_estimate=pl.CostEstimate(flops=SPREAD_FLOPS, bytes_accessed=0, transcendentals=0),
        name="spread",
    )(*parts))

    factor = math.sqrt(n_v * n_c) / (n_mu * n_row)
    part = n_v // n_col
    kept, *sent = pl.pallas_call(
        functools.partial(direct_kernel, sizes, factor),
        in_specs=[IN_VMEM] * (len(loaded) + len(operands)),
        out_specs=[IN_VMEM] * n_col,
        out_shape=[jax.ShapeDtypeStruct((n_b, part, n_c), F32)]
        + [jax.ShapeDtypeStruct((n_b, part, n_c), BF16)] * (n_col - 1),
        scratch_shapes=[
            pltpu.VMEM((n_ka - 1, n_b * n_v, n_c), BF16),
            pltpu.VMEM((n_ka - 1, n_c, n_mu), BF16),
            pltpu.VMEM((2, n_ka - 1, n_b * TILE, n_v), BF16),
            pltpu.VMEM((2, n_ka - 1, n_b * TILE, CHUNK), BF16),
            pltpu.VMEM((2, n_b * TILE, n_nu), BF16),
            pltpu.VMEM((n_b * TILE, n_v), F32),
            pltpu.VMEM((n_b, n_mu, n_v), BF16),
            pltpu.VMEM((n_b * n_v, n_c), F32),
        ],
        compiler_params=pltpu.CompilerParams(vmem_limit_bytes=36 * MIB),
        name="direct_term",
    )(*loaded, *operands)
    mine = kept
    for flip in range(1, n_col):
        mine = mine + swap(sent[flip - 1], "col", n_col, flip).astype(F32)
    mine = mine.astype(BF16)
    terms = [after(swap(mine, "row", n_row, n_row - 1), flops=JOIN_FLOPS)]
    terms += [swap(mine, "row", n_row, flip) for flip in reversed(range(1, n_row - 1))] + [mine]
    terms = [term.astype(F32) for term in terms]
    while len(terms) > 1:
        terms = [a + b for a, b in zip(terms[::2], terms[1::2])]
    return terms[0][None]


def solution(mesh):
    placed = (
        P("ka", None, None, None),
        P("ka", None, "row"),
        P("ka", None, "col"),
        P(None, "row", "col"),
        P(),
    )
    sizes = tuple(mesh.shape[name] for name in ("ka", "row", "col"))
    return jax.shard_map(
        functools.partial(local, sizes), mesh=mesh, in_specs=placed,
        out_specs=P("ka", None, "col", None), check_vma=False,
    )
```

```python
import functools
import math

import jax
import jax.numpy as jnp
from jax import lax
from jax.experimental import pallas as pl
from jax.experimental.pallas import tpu as pltpu
from jax.sharding import PartitionSpec as P

BF16 = jnp.bfloat16
F32 = jnp.float32
LANES = 128
ROWS = 16
TILE = 256
CHUNK = 256
QUARTERS = 4
MIB = 2**20
JOIN_FLOPS = 2 * 10**10
SPREAD_FLOPS = 2 * 10**10
PANEL_FLOPS = 10**9
IN_HBM = pl.BlockSpec(memory_space=pltpu.HBM)
IN_VMEM = pl.BlockSpec(memory_space=pltpu.VMEM)
IN_SMEM = pl.BlockSpec(memory_space=pltpu.SMEM)


def swap(value, axis, size, flip):
    return lax.ppermute(value, axis, [(i, i ^ flip) for i in range(size)])


def run(copies):
    for copy in copies:
        copy.start()
    for copy in copies:
        copy.wait()


def pack_kernel(n_col, exciton_ref, cond_ref, core_ref, sems):
    col = lax.axis_index("col")
    copies, at = [], 0
    for source in (cond_ref, exciton_ref):
        part = source.shape[0] // n_col
        rows = pl.ds(pl.multiple_of(col * part, part), part)
        for block in range(source.shape[1] // LANES):
            copies.append(pltpu.make_async_copy(
                source.at[rows, block * LANES:(block + 1) * LANES],
                core_ref.at[at:at + part, :], sems.at[len(copies)],
            ))
            at += part
    run(copies)


def join_kernel(*refs):
    *parts, out = refs
    at = 0
    for part in parts:
        out[at:at + part.shape[0], :] = part[...]
        at += part.shape[0]


def join(parts):
    shape = (sum(part.shape[0] for part in parts), parts[0].shape[1])
    return pl.pallas_call(
        join_kernel,
        in_specs=[IN_VMEM] * len(parts),
        out_specs=IN_VMEM,
        out_shape=jax.ShapeDtypeStruct(shape, BF16),
        compiler_params=pltpu.CompilerParams(vmem_limit_bytes=4 * MIB),
        cost_estimate=pl.CostEstimate(flops=JOIN_FLOPS, bytes_accessed=0, transcendentals=0),
        name="join",
    )(*parts)


def spread_kernel(n_row, *refs):
    *parts, out = refs
    row = lax.axis_index("row")
    part = out.shape[1] // n_row
    for other in range(n_row):
        rows = pl.ds(pl.multiple_of((row ^ other) * part, part), part)
        for flip in range(out.shape[0]):
            out[flip, rows, :] = parts[other][flip * part:(flip + 1) * part, :]


def set_panels(panels, cond_tile, exciton, n_v):
    by_point = lax.dot_general(
        cond_tile, exciton, (((0,), (1,)), ((), ())), preferred_element_type=F32
    ).astype(BF16)
    for b in range(exciton.shape[0] // n_v):
        panels[b * TILE:(b + 1) * TILE, :] = by_point[:, b * n_v:(b + 1) * n_v]


def own_kernel(
    q_ref, w_ref, exciton_ref, cond_ref, val_ref, after_ref, sums, w, cond, val, w_own, exciton, panels, sems
):
    del after_ref
    me, n_others = lax.axis_index("ka"), w.shape[0]
    pairs = [(exciton_ref, exciton), (cond_ref, cond), (val_ref, val)]
    pairs += [(w_ref.at[q_ref[me, me]], w_own)]
    pairs += [(w_ref.at[q_ref[me ^ flip, me]], w.at[flip - 1]) for flip in range(1, n_others + 1)]
    copies = [
        pltpu.make_async_copy(source, target, sems.at[i])
        for i, (source, target) in enumerate(pairs)
    ]
    for copy in copies:
        copy.start()
    for copy in copies[:4]:
        copy.wait()
    n_v, n_nu = val.shape
    n_b = exciton.shape[0] // n_v
    for t in range(cond.shape[1] // TILE):
        set_panels(panels.at[t % 2], cond[:, t * TILE:(t + 1) * TILE], exciton[...], n_v)
        for j in range(n_nu // CHUNK):
            at = slice(j * CHUNK, (j + 1) * CHUNK)
            product = jnp.dot(panels[t % 2], val[:, at], preferred_element_type=F32)
            weights = w_own[t * TILE:(t + 1) * TILE, at].astype(F32)
            for b in range(n_b):
                rows = slice(b * TILE, (b + 1) * TILE)
                sums[t, rows, at] = product[rows, :] * weights
    for copy in copies[4:]:
        copy.wait()


def put_together(cores, col, cond, exciton):
    n_col, n_c, n_mu = len(cores), cond.shape[0], cond.shape[1]
    part_c, part_x = n_c // n_col, exciton.shape[0] // n_col
    for other, source in enumerate(cores):
        at = 0
        rows = pl.ds(pl.multiple_of((col ^ other) * part_c, part_c), part_c)
        for block in range(n_mu // LANES):
            cond[rows, block * LANES:(block + 1) * LANES] = source[at:at + part_c, :]
            at += part_c
        rows = pl.ds(pl.multiple_of((col ^ other) * part_x, part_x), part_x)
        exciton[rows, :] = source[at:at + part_x, :]


def panels_kernel(n_col, n_v, *refs):
    *cores, panels, cond, exciton = refs
    col = lax.axis_index("col")
    for i in range(panels.shape[0]):
        put_together(cores[i * n_col:(i + 1) * n_col], col, cond.at[i], exciton.at[i])
        for t in range(panels.shape[1]):
            set_panels(panels.at[i, t], cond[i, :, t * TILE:(t + 1) * TILE], exciton[i], n_v)


def after_kernel(*refs):
    refs[-1][...] = refs[0][...]


def after(value, *others, flops=0):
    return pl.pallas_call(
        after_kernel,
        in_specs=[IN_VMEM] + [pl.BlockSpec(memory_space=pl.ANY)] * len(others),
        out_specs=IN_VMEM,
        out_shape=jax.ShapeDtypeStruct(value.shape, value.dtype),
        compiler_params=pltpu.CompilerParams(vmem_limit_bytes=4 * MIB),
        cost_estimate=pl.CostEstimate(flops=flops, bytes_accessed=0, transcendentals=0),
        name="after",
    )(value, *others)


def direct_kernel(sizes, early, factor, *refs):
    n_ka, n_row, n_col = sizes
    refs = list(refs)

    def take(count):
        taken, refs[:] = refs[:count], refs[count:]
        return taken

    sums, w, cond_own, val_own, early_panels = take(5)
    n_early = early_panels.shape[0]
    late = [flip for flip in range(1, n_ka) if flip not in early]
    cores = [take(n_col) for _ in late]
    val_ref, = take(1)
    keep, *sent = take(n_col)
    x_all, cond_all, panels, products, direct, running, half, total = refs
    col = lax.axis_index("col")
    n_v, n_nu = val_own.shape
    n_c, n_mu = cond_own.shape
    n_b = x_all.shape[1] // n_v
    n_tiles, n_others = n_mu // TILE, n_ka - 1
    order = list(early) + late

    for i in range(len(late)):
        put_together(cores[i], col, cond_all.at[i], x_all.at[i])

    steps = [(t, j) for t in range(n_tiles) for j in range(n_nu // CHUNK)]
    quarter = TILE // QUARTERS

    def all_panels(t):
        for i in range(len(late)):
            set_panels(panels.at[t % 2, i], cond_all[i, :, t * TILE:(t + 1) * TILE], x_all[i], n_v)

    def multiply(number, i):
        t, j = steps[number]
        left = early_panels[i, t] if i < n_early else panels[t % 2, i - n_early]
        products[number % 2, i] = jnp.dot(
            left, val_ref[order[i] - 1, :, j * CHUNK:(j + 1) * CHUNK],
            preferred_element_type=F32,
        ).astype(BF16)

    def combine(number, part):
        t, j = steps[number]
        at = slice(j * CHUNK, (j + 1) * CHUNK)
        for m in range(part * quarter, (part + 1) * quarter, ROWS):
            weights = [
                w[flip - 1, t * TILE + m:t * TILE + m + ROWS, at].astype(F32) for flip in order
            ]
            for b in range(n_b):
                rows = slice(b * TILE + m, b * TILE + m + ROWS)
                value = sums[t, rows, at]
                for i in range(n_others):
                    value += products[number % 2, i, rows, :].astype(F32) * weights[i]
                direct[t % 2, rows, at] = value.astype(BF16)

    def reduce(number):
        t, j = steps[number]
        at = slice(j * CHUNK, (j + 1) * CHUNK)
        value = lax.dot_general(
            direct[t % 2, :, at], val_own[:, at], (((1,), (1,)), ((), ())),
            preferred_element_type=F32,
        )
        if j:
            value += running[...]
        if j + 1 < n_nu // CHUNK:
            running[...] = value
            return
        value = value.astype(BF16)
        for b in range(n_b):
            half[b, t * TILE:(t + 1) * TILE, :] = value[b * TILE:(b + 1) * TILE, :]

    all_panels(0)
    for i in range(n_others):
        multiply(0, i)
    for number, (t, j) in enumerate(steps):
        more = number + 1 < len(steps)
        if more and steps[number + 1][0] != t:
            all_panels(t + 1)
        for i in range(max(n_others, QUARTERS)):
            if more and i < n_others:
                multiply(number + 1, i)
            if i < QUARTERS:
                combine(number, i)
        reduce(number)

    part = n_v // n_col
    for b in range(n_b):
        total[b * n_v:(b + 1) * n_v, :] = (
            jnp.dot(cond_own[...], half[b], preferred_element_type=F32) * factor
        ).T
        for other in range(n_col):
            rows = pl.ds(pl.multiple_of(b * n_v + (col ^ other) * part, part), part)
            value = total[rows, :]
            if other == 0:
                keep[b] = value
            else:
                sent[other - 1][b] = value.astype(BF16)


def local(sizes, exciton, orb_cond, orb_val, screened, q_table):
    n_ka, n_row, n_col = sizes
    n_b, n_v, n_c = exciton.shape[1:]
    x_rows, cond, val, screened, q_table = (
        pltpu.with_memory_space_constraint(array, pltpu.HBM)
        for array in (exciton.reshape(n_b * n_v, n_c), orb_cond[0], orb_val[0], screened, q_table)
    )
    n_mu, n_nu = cond.shape[1], val.shape[1]
    core_rows = (cond.size + x_rows.size) // n_col // LANES
    part = n_v // n_row
    plane = lax.dynamic_slice_in_dim(orb_val[0], lax.axis_index("row") * part, part, 0)
    planes = [swap(plane, "ka", n_ka, flip) for flip in range(1, n_ka)]
    core = pl.pallas_call(
        functools.partial(pack_kernel, n_col),
        in_specs=[IN_HBM] * 2,
        out_specs=IN_VMEM,
        out_shape=jax.ShapeDtypeStruct((core_rows, LANES), BF16),
        scratch_shapes=[pltpu.SemaphoreType.DMA(((n_mu + n_c) // LANES,))],
        compiler_params=pltpu.CompilerParams(vmem_limit_bytes=4 * MIB),
        name="pack",
    )(x_rows, cond)
    joined = join(planes)
    cores = [after(core, planes[n_ka // 2 - 1])]
    for flip in range(1, n_ka):
        last = flip & -flip
        cores.append(swap(cores[flip - last], "ka", n_ka, last))
        if flip == 2:
            cores[2] = after(cores[2], joined, cores[1])
    n_tiles = n_mu // TILE
    loaded = pl.pallas_call(
        own_kernel,
        in_specs=[IN_SMEM] + [IN_HBM] * 4 + [pl.BlockSpec(memory_space=pl.ANY)],
        out_specs=[IN_VMEM] * 4,
        out_shape=[
            jax.ShapeDtypeStruct((n_tiles, n_b * TILE, n_nu), F32),
            jax.ShapeDtypeStruct((n_ka - 1, n_mu, n_nu), BF16),
            jax.ShapeDtypeStruct(cond.shape, BF16),
            jax.ShapeDtypeStruct(val.shape, BF16),
        ],
        scratch_shapes=[
            pltpu.VMEM((n_mu, n_nu), BF16),
            pltpu.VMEM(x_rows.shape, BF16),
            pltpu.VMEM((2, n_b * TILE, n_v), BF16),
            pltpu.SemaphoreType.DMA((n_ka + 3,)),
        ],
        compiler_params=pltpu.CompilerParams(vmem_limit_bytes=24 * MIB),
        cost_estimate=pl.CostEstimate(
            flops=0, bytes_accessed=4 * screened.size, transcendentals=0
        ),
        name="own_term",
    )(q_table, screened, x_rows, cond, val, cores[n_ka // 2])
    early = [flip for flip in range(1, n_ka) if flip.bit_count() == 1]
    both = {
        flip: [swap(cores[flip], "col", n_col, d) if d else cores[flip] for d in range(n_col)]
        for flip in range(1, n_ka)
    }
    operands = [pl.pallas_call(
        functools.partial(panels_kernel, n_col, n_v),
        in_specs=[IN_VMEM] * (len(early) * n_col),
        out_specs=IN_VMEM,
        out_shape=jax.ShapeDtypeStruct((len(early), n_tiles, n_b * TILE, n_v), BF16),
        scratch_shapes=[
            pltpu.VMEM((len(early), n_c, n_mu), BF16),
            pltpu.VMEM((len(early), n_b * n_v, n_c), BF16),
        ],
        compiler_params=pltpu.CompilerParams(vmem_limit_bytes=12 * MIB),
        cost_estimate=pl.CostEstimate(flops=PANEL_FLOPS, bytes_accessed=0, transcendentals=0),
        name="panels",
    )(*(part for flip in early for part in both[flip]))]
    operands += [part for flip in both if flip not in early for part in both[flip]]
    parts = [swap(joined, "row", n_row, d) if d else joined for d in range(n_row)]
    operands.append(pl.pallas_call(
        functools.partial(spread_kernel, n_row),
        in_specs=[IN_VMEM] * n_row,
        out_specs=IN_VMEM,
        out_shape=jax.ShapeDtypeStruct((n_ka - 1, *val.shape), BF16),
        compiler_params=pltpu.CompilerParams(vmem_limit_bytes=4 * MIB),
        cost_estimate=pl.CostEstimate(flops=SPREAD_FLOPS, bytes_accessed=0, transcendentals=0),
        name="spread",
    )(*parts))

    factor = math.sqrt(n_v * n_c) / (n_mu * n_row)
    part = n_v // n_col
    n_late = n_ka - 1 - len(early)
    kept, *sent = pl.pallas_call(
        functools.partial(direct_kernel, sizes, early, factor),
        in_specs=[IN_VMEM] * (len(loaded) + len(operands)),
        out_specs=[IN_VMEM] * n_col,
        out_shape=[jax.ShapeDtypeStruct((n_b, part, n_c), F32)]
        + [jax.ShapeDtypeStruct((n_b, part, n_c), BF16)] * (n_col - 1),
        scratch_shapes=[
            pltpu.VMEM((n_late, n_b * n_v, n_c), BF16),
            pltpu.VMEM((n_late, n_c, n_mu), BF16),
            pltpu.VMEM((2, n_late, n_b * TILE, n_v), BF16),
            pltpu.VMEM((2, n_ka - 1, n_b * TILE, CHUNK), BF16),
            pltpu.VMEM((2, n_b * TILE, n_nu), BF16),
            pltpu.VMEM((n_b * TILE, n_v), F32),
            pltpu.VMEM((n_b, n_mu, n_v), BF16),
            pltpu.VMEM((n_b * n_v, n_c), F32),
        ],
        compiler_params=pltpu.CompilerParams(vmem_limit_bytes=36 * MIB),
        name="direct_term",
    )(*loaded, *operands)
    mine = kept
    for flip in range(1, n_col):
        mine = mine + swap(sent[flip - 1], "col", n_col, flip).astype(F32)
    mine = mine.astype(BF16)
    terms = [after(swap(mine, "row", n_row, n_row - 1), flops=JOIN_FLOPS)]
    terms += [swap(mine, "row", n_row, flip) for flip in reversed(range(1, n_row - 1))] + [mine]
    terms = [term.astype(F32) for term in terms]
    while len(terms) > 1:
        terms = [a + b for a, b in zip(terms[::2], terms[1::2])]
    return terms[0][None]


def solution(mesh):
    placed = (
        P("ka", None, None, None),
        P("ka", None, "row"),
        P("ka", None, "col"),
        P(None, "row", "col"),
        P(),
    )
    sizes = tuple(mesh.shape[name] for name in ("ka", "row", "col"))
    return jax.shard_map(
        functools.partial(local, sizes), mesh=mesh, in_specs=placed,
        out_specs=P("ka", None, "col", None), check_vma=False,
    )
```

```python
import functools
import math

import jax
import jax.numpy as jnp
from jax import lax
from jax.experimental import pallas as pl
from jax.experimental.pallas import tpu as pltpu
from jax.sharding import PartitionSpec as P

BF16 = jnp.bfloat16
F32 = jnp.float32
LANES = 128
ROWS = 16
TILE = 128
CHUNK = 256
QUARTERS = 4
MIB = 2**20
JOIN_FLOPS = 2 * 10**10
SPREAD_FLOPS = 2 * 10**10
PANEL_FLOPS = 10**9
IN_HBM = pl.BlockSpec(memory_space=pltpu.HBM)
IN_VMEM = pl.BlockSpec(memory_space=pltpu.VMEM)
IN_SMEM = pl.BlockSpec(memory_space=pltpu.SMEM)


def swap(value, axis, size, flip):
    return lax.ppermute(value, axis, [(i, i ^ flip) for i in range(size)])


def run(copies):
    for copy in copies:
        copy.start()
    for copy in copies:
        copy.wait()


def pack_kernel(n_col, exciton_ref, cond_ref, after_ref, core_ref, sems):
    del after_ref
    col = lax.axis_index("col")
    copies, at = [], 0
    for source in (cond_ref, exciton_ref):
        part = source.shape[0] // n_col
        rows = pl.ds(pl.multiple_of(col * part, part), part)
        for block in range(source.shape[1] // LANES):
            copies.append(pltpu.make_async_copy(
                source.at[rows, block * LANES:(block + 1) * LANES],
                core_ref.at[at:at + part, :], sems.at[len(copies)],
            ))
            at += part
    run(copies)


def join_kernel(*refs):
    *parts, out = refs
    at = 0
    for part in parts:
        out[at:at + part.shape[0], :] = part[...]
        at += part.shape[0]


def join(parts):
    shape = (sum(part.shape[0] for part in parts), parts[0].shape[1])
    return pl.pallas_call(
        join_kernel,
        in_specs=[IN_VMEM] * len(parts),
        out_specs=IN_VMEM,
        out_shape=jax.ShapeDtypeStruct(shape, BF16),
        compiler_params=pltpu.CompilerParams(vmem_limit_bytes=4 * MIB),
        cost_estimate=pl.CostEstimate(flops=JOIN_FLOPS, bytes_accessed=0, transcendentals=0),
        name="join",
    )(*parts)


def spread_kernel(n_row, *refs):
    *parts, out = refs
    row = lax.axis_index("row")
    part = out.shape[1] // n_row
    for other in range(n_row):
        rows = pl.ds(pl.multiple_of((row ^ other) * part, part), part)
        for flip in range(out.shape[0]):
            out[flip, rows, :] = parts[other][flip * part:(flip + 1) * part, :]


def set_panels(panels, cond_tile, exciton, n_v):
    by_point = lax.dot_general(
        cond_tile, exciton, (((0,), (1,)), ((), ())), preferred_element_type=F32
    ).astype(BF16)
    for b in range(exciton.shape[0] // n_v):
        panels[b * TILE:(b + 1) * TILE, :] = by_point[:, b * n_v:(b + 1) * n_v]


def own_kernel(
    q_ref, w_ref, exciton_ref, cond_ref, val_ref, after_ref, sums, w, cond, val, w_own, exciton, panels, sems
):
    del after_ref
    me, n_others = lax.axis_index("ka"), w.shape[0]
    pairs = [(exciton_ref, exciton), (cond_ref, cond), (val_ref, val)]
    pairs += [(w_ref.at[q_ref[me, me]], w_own)]
    pairs += [(w_ref.at[q_ref[me ^ flip, me]], w.at[flip - 1]) for flip in range(1, n_others + 1)]
    copies = [
        pltpu.make_async_copy(source, target, sems.at[i])
        for i, (source, target) in enumerate(pairs)
    ]
    for copy in copies:
        copy.start()
    for copy in copies[:4]:
        copy.wait()
    n_v, n_nu = val.shape
    n_b = exciton.shape[0] // n_v
    for t in range(cond.shape[1] // TILE):
        set_panels(panels.at[t % 2], cond[:, t * TILE:(t + 1) * TILE], exciton[...], n_v)
        for j in range(n_nu // CHUNK):
            at = slice(j * CHUNK, (j + 1) * CHUNK)
            product = jnp.dot(panels[t % 2], val[:, at], preferred_element_type=F32)
            weights = w_own[t * TILE:(t + 1) * TILE, at].astype(F32)
            for b in range(n_b):
                rows = slice(b * TILE, (b + 1) * TILE)
                sums[t, rows, at] = product[rows, :] * weights
    for copy in copies[4:]:
        copy.wait()


def put_together(cores, col, cond, exciton):
    n_col, n_c, n_mu = len(cores), cond.shape[0], cond.shape[1]
    part_c, part_x = n_c // n_col, exciton.shape[0] // n_col
    for other, source in enumerate(cores):
        at = 0
        rows = pl.ds(pl.multiple_of((col ^ other) * part_c, part_c), part_c)
        for block in range(n_mu // LANES):
            cond[rows, block * LANES:(block + 1) * LANES] = source[at:at + part_c, :]
            at += part_c
        rows = pl.ds(pl.multiple_of((col ^ other) * part_x, part_x), part_x)
        exciton[rows, :] = source[at:at + part_x, :]


def panels_kernel(n_col, n_v, *refs):
    *cores, panels, cond, exciton = refs
    col = lax.axis_index("col")
    for i in range(panels.shape[0]):
        put_together(cores[i * n_col:(i + 1) * n_col], col, cond.at[i], exciton.at[i])
        for t in range(panels.shape[1]):
            set_panels(panels.at[i, t], cond[i, :, t * TILE:(t + 1) * TILE], exciton[i], n_v)


def after_kernel(*refs):
    refs[-1][...] = refs[0][...]


def after(value, *others, flops=0):
    return pl.pallas_call(
        after_kernel,
        in_specs=[IN_VMEM] + [pl.BlockSpec(memory_space=pl.ANY)] * len(others),
        out_specs=IN_VMEM,
        out_shape=jax.ShapeDtypeStruct(value.shape, value.dtype),
        compiler_params=pltpu.CompilerParams(vmem_limit_bytes=4 * MIB),
        cost_estimate=pl.CostEstimate(flops=flops, bytes_accessed=0, transcendentals=0),
        name="after",
    )(value, *others)


def direct_kernel(sizes, early, factor, *refs):
    n_ka, n_row, n_col = sizes
    refs = list(refs)

    def take(count):
        taken, refs[:] = refs[:count], refs[count:]
        return taken

    sums, w, cond_own, val_own, early_panels = take(5)
    n_early = early_panels.shape[0]
    late = [flip for flip in range(1, n_ka) if flip not in early]
    cores = [take(n_col) for _ in late]
    val_ref, = take(1)
    keep, *sent = take(n_col)
    x_all, cond_all, panels, products, direct, running, half, total = refs
    col = lax.axis_index("col")
    n_v, n_nu = val_own.shape
    n_c, n_mu = cond_own.shape
    n_b = x_all.shape[1] // n_v
    n_tiles, n_others = n_mu // TILE, n_ka - 1
    order = list(early) + late

    for i in range(len(late)):
        put_together(cores[i], col, cond_all.at[i], x_all.at[i])

    steps = [(t, j) for t in range(n_tiles) for j in range(n_nu // CHUNK)]
    quarter = TILE // QUARTERS

    def all_panels(t):
        for i in range(len(late)):
            set_panels(panels.at[t % 2, i], cond_all[i, :, t * TILE:(t + 1) * TILE], x_all[i], n_v)

    def multiply(number, i):
        t, j = steps[number]
        left = early_panels[i, t] if i < n_early else panels[t % 2, i - n_early]
        products[number % 2, i] = jnp.dot(
            left, val_ref[order[i] - 1, :, j * CHUNK:(j + 1) * CHUNK],
            preferred_element_type=F32,
        ).astype(BF16)

    def combine(number, part):
        t, j = steps[number]
        at = slice(j * CHUNK, (j + 1) * CHUNK)
        for m in range(part * quarter, (part + 1) * quarter, ROWS):
            weights = [
                w[flip - 1, t * TILE + m:t * TILE + m + ROWS, at].astype(F32) for flip in order
            ]
            for b in range(n_b):
                rows = slice(b * TILE + m, b * TILE + m + ROWS)
                value = sums[t, rows, at]
                for i in range(n_others):
                    value += products[number % 2, i, rows, :].astype(F32) * weights[i]
                direct[t % 2, rows, at] = value.astype(BF16)

    def reduce(number):
        t, j = steps[number]
        at = slice(j * CHUNK, (j + 1) * CHUNK)
        value = lax.dot_general(
            direct[t % 2, :, at], val_own[:, at], (((1,), (1,)), ((), ())),
            preferred_element_type=F32,
        )
        if j:
            value += running[...]
        if j + 1 < n_nu // CHUNK:
            running[...] = value
            return
        value = value.astype(BF16)
        for b in range(n_b):
            half[b, t * TILE:(t + 1) * TILE, :] = value[b * TILE:(b + 1) * TILE, :]

    all_panels(0)
    for i in range(n_others):
        multiply(0, i)
    for number, (t, j) in enumerate(steps):
        more = number + 1 < len(steps)
        if more and steps[number + 1][0] != t:
            all_panels(t + 1)
        for i in range(max(n_others, QUARTERS)):
            if more and i < n_others:
                multiply(number + 1, i)
            if i < QUARTERS:
                combine(number, i)
        reduce(number)

    part = n_v // n_col
    for b in range(n_b):
        total[b * n_v:(b + 1) * n_v, :] = (
            jnp.dot(cond_own[...], half[b], preferred_element_type=F32) * factor
        ).T
        for other in range(n_col):
            rows = pl.ds(pl.multiple_of(b * n_v + (col ^ other) * part, part), part)
            value = total[rows, :]
            if other == 0:
                keep[b] = value
            else:
                sent[other - 1][b] = value.astype(BF16)


def local(sizes, exciton, orb_cond, orb_val, screened, q_table):
    n_ka, n_row, n_col = sizes
    n_b, n_v, n_c = exciton.shape[1:]
    x_rows, cond, val, screened, q_table = (
        pltpu.with_memory_space_constraint(array, pltpu.HBM)
        for array in (exciton.reshape(n_b * n_v, n_c), orb_cond[0], orb_val[0], screened, q_table)
    )
    n_mu, n_nu = cond.shape[1], val.shape[1]
    core_rows = (cond.size + x_rows.size) // n_col // LANES
    part = n_v // n_row
    plane = lax.dynamic_slice_in_dim(orb_val[0], lax.axis_index("row") * part, part, 0)
    planes = [swap(plane, "ka", n_ka, flip) for flip in range(1, n_ka)]
    core = pl.pallas_call(
        functools.partial(pack_kernel, n_col),
        in_specs=[IN_HBM] * 2 + [pl.BlockSpec(memory_space=pl.ANY)],
        out_specs=IN_VMEM,
        out_shape=jax.ShapeDtypeStruct((core_rows, LANES), BF16),
        scratch_shapes=[pltpu.SemaphoreType.DMA(((n_mu + n_c) // LANES,))],
        compiler_params=pltpu.CompilerParams(vmem_limit_bytes=4 * MIB),
        name="pack",
    )(x_rows, cond, planes[0])
    joined = join(planes)
    cores = [core]
    for flip in range(1, n_ka):
        last = flip & -flip
        source = cores[flip - last]
        if flip == last and flip > 1:
            source = after(source, planes[flip - 1])
        cores.append(swap(source, "ka", n_ka, last))
        if flip == 2:
            cores[2] = after(cores[2], joined, cores[1])
    n_tiles = n_mu // TILE
    loaded = pl.pallas_call(
        own_kernel,
        in_specs=[IN_SMEM] + [IN_HBM] * 4 + [pl.BlockSpec(memory_space=pl.ANY)],
        out_specs=[IN_VMEM] * 4,
        out_shape=[
            jax.ShapeDtypeStruct((n_tiles, n_b * TILE, n_nu), F32),
            jax.ShapeDtypeStruct((n_ka - 1, n_mu, n_nu), BF16),
            jax.ShapeDtypeStruct(cond.shape, BF16),
            jax.ShapeDtypeStruct(val.shape, BF16),
        ],
        scratch_shapes=[
            pltpu.VMEM((n_mu, n_nu), BF16),
            pltpu.VMEM(x_rows.shape, BF16),
            pltpu.VMEM((2, n_b * TILE, n_v), BF16),
            pltpu.SemaphoreType.DMA((n_ka + 3,)),
        ],
        compiler_params=pltpu.CompilerParams(vmem_limit_bytes=24 * MIB),
        cost_estimate=pl.CostEstimate(
            flops=0, bytes_accessed=4 * screened.size, transcendentals=0
        ),
        name="own_term",
    )(q_table, screened, x_rows, cond, val, cores[n_ka // 2])
    early = [flip for flip in range(1, n_ka) if flip.bit_count() == 1]
    both = {
        flip: [swap(cores[flip], "col", n_col, d) if d else cores[flip] for d in range(n_col)]
        for flip in range(1, n_ka)
    }
    operands = [pl.pallas_call(
        functools.partial(panels_kernel, n_col, n_v),
        in_specs=[IN_VMEM] * (len(early) * n_col),
        out_specs=IN_VMEM,
        out_shape=jax.ShapeDtypeStruct((len(early), n_tiles, n_b * TILE, n_v), BF16),
        scratch_shapes=[
            pltpu.VMEM((len(early), n_c, n_mu), BF16),
            pltpu.VMEM((len(early), n_b * n_v, n_c), BF16),
        ],
        compiler_params=pltpu.CompilerParams(vmem_limit_bytes=12 * MIB),
        cost_estimate=pl.CostEstimate(flops=PANEL_FLOPS, bytes_accessed=0, transcendentals=0),
        name="panels",
    )(*(part for flip in early for part in both[flip]))]
    operands += [part for flip in both if flip not in early for part in both[flip]]
    parts = [swap(joined, "row", n_row, d) if d else joined for d in range(n_row)]
    operands.append(pl.pallas_call(
        functools.partial(spread_kernel, n_row),
        in_specs=[IN_VMEM] * n_row,
        out_specs=IN_VMEM,
        out_shape=jax.ShapeDtypeStruct((n_ka - 1, *val.shape), BF16),
        compiler_params=pltpu.CompilerParams(vmem_limit_bytes=4 * MIB),
        cost_estimate=pl.CostEstimate(flops=SPREAD_FLOPS, bytes_accessed=0, transcendentals=0),
        name="spread",
    )(*parts))

    factor = math.sqrt(n_v * n_c) / (n_mu * n_row)
    part = n_v // n_col
    n_late = n_ka - 1 - len(early)
    kept, *sent = pl.pallas_call(
        functools.partial(direct_kernel, sizes, early, factor),
        in_specs=[IN_VMEM] * (len(loaded) + len(operands)),
        out_specs=[IN_VMEM] * n_col,
        out_shape=[jax.ShapeDtypeStruct((n_b, part, n_c), F32)]
        + [jax.ShapeDtypeStruct((n_b, part, n_c), BF16)] * (n_col - 1),
        scratch_shapes=[
            pltpu.VMEM((n_late, n_b * n_v, n_c), BF16),
            pltpu.VMEM((n_late, n_c, n_mu), BF16),
            pltpu.VMEM((2, n_late, n_b * TILE, n_v), BF16),
            pltpu.VMEM((2, n_ka - 1, n_b * TILE, CHUNK), BF16),
            pltpu.VMEM((2, n_b * TILE, n_nu), BF16),
            pltpu.VMEM((n_b * TILE, n_v), F32),
            pltpu.VMEM((n_b, n_mu, n_v), BF16),
            pltpu.VMEM((n_b * n_v, n_c), F32),
        ],
        compiler_params=pltpu.CompilerParams(vmem_limit_bytes=36 * MIB),
        name="direct_term",
    )(*loaded, *operands)
    mine = kept
    for flip in range(1, n_col):
        mine = mine + swap(sent[flip - 1], "col", n_col, flip).astype(F32)
    mine = mine.astype(BF16)
    terms = [after(swap(mine, "row", n_row, n_row - 1), flops=JOIN_FLOPS)]
    terms += [swap(mine, "row", n_row, flip) for flip in reversed(range(1, n_row - 1))] + [mine]
    terms = [term.astype(F32) for term in terms]
    while len(terms) > 1:
        terms = [a + b for a, b in zip(terms[::2], terms[1::2])]
    return terms[0][None]


def solution(mesh):
    placed = (
        P("ka", None, None, None),
        P("ka", None, "row"),
        P("ka", None, "col"),
        P(None, "row", "col"),
        P(),
    )
    sizes = tuple(mesh.shape[name] for name in ("ka", "row", "col"))
    return jax.shard_map(
        functools.partial(local, sizes), mesh=mesh, in_specs=placed,
        out_specs=P("ka", None, "col", None), check_vma=False,
    )
```

```python
import functools
import math

import jax
import jax.numpy as jnp
from jax import lax
from jax.experimental import pallas as pl
from jax.experimental.pallas import tpu as pltpu
from jax.sharding import PartitionSpec as P

BF16 = jnp.bfloat16
F32 = jnp.float32
LANES = 128
ROWS = 16
TILE = 128
CHUNK = 256
QUARTERS = 4
MIB = 2**20
JOIN_FLOPS = 2 * 10**10
SPREAD_FLOPS = 2 * 10**10
PANEL_FLOPS = 10**9
IN_HBM = pl.BlockSpec(memory_space=pltpu.HBM)
IN_VMEM = pl.BlockSpec(memory_space=pltpu.VMEM)
IN_SMEM = pl.BlockSpec(memory_space=pltpu.SMEM)


def swap(value, axis, size, flip):
    return lax.ppermute(value, axis, [(i, i ^ flip) for i in range(size)])


def run(copies):
    for copy in copies:
        copy.start()
    for copy in copies:
        copy.wait()


def pack_kernel(n_col, exciton_ref, cond_ref, after_ref, core_ref, sems):
    del after_ref
    col = lax.axis_index("col")
    copies, at = [], 0
    for source in (cond_ref, exciton_ref):
        part = source.shape[0] // n_col
        rows = pl.ds(pl.multiple_of(col * part, part), part)
        for block in range(source.shape[1] // LANES):
            copies.append(pltpu.make_async_copy(
                source.at[rows, block * LANES:(block + 1) * LANES],
                core_ref.at[at:at + part, :], sems.at[len(copies)],
            ))
            at += part
    run(copies)


def join_kernel(*refs):
    *parts, out = refs
    at = 0
    for part in parts:
        out[at:at + part.shape[0], :] = part[...]
        at += part.shape[0]


def join(parts):
    shape = (sum(part.shape[0] for part in parts), parts[0].shape[1])
    return pl.pallas_call(
        join_kernel,
        in_specs=[IN_VMEM] * len(parts),
        out_specs=IN_VMEM,
        out_shape=jax.ShapeDtypeStruct(shape, BF16),
        compiler_params=pltpu.CompilerParams(vmem_limit_bytes=4 * MIB),
        cost_estimate=pl.CostEstimate(flops=JOIN_FLOPS, bytes_accessed=0, transcendentals=0),
        name="join",
    )(*parts)


def spread_kernel(n_row, *refs):
    *parts, out = refs
    row = lax.axis_index("row")
    part = out.shape[1] // n_row
    for other in range(n_row):
        rows = pl.ds(pl.multiple_of((row ^ other) * part, part), part)
        for flip in range(out.shape[0]):
            out[flip, rows, :] = parts[other][flip * part:(flip + 1) * part, :]


def set_panels(panels, cond_tile, exciton, n_v):
    by_point = lax.dot_general(
        cond_tile, exciton, (((0,), (1,)), ((), ())), preferred_element_type=F32
    ).astype(BF16)
    for b in range(exciton.shape[0] // n_v):
        panels[b * TILE:(b + 1) * TILE, :] = by_point[:, b * n_v:(b + 1) * n_v]


def own_kernel(
    q_ref, w_ref, exciton_ref, cond_ref, val_ref, after_ref, sums, w, cond, val, w_own, exciton, panels, sems
):
    del after_ref
    me, n_others = lax.axis_index("ka"), w.shape[0]
    pairs = [(exciton_ref, exciton), (cond_ref, cond), (val_ref, val)]
    pairs += [(w_ref.at[q_ref[me, me]], w_own)]
    pairs += [(w_ref.at[q_ref[me ^ flip, me]], w.at[flip - 1]) for flip in range(1, n_others + 1)]
    copies = [
        pltpu.make_async_copy(source, target, sems.at[i])
        for i, (source, target) in enumerate(pairs)
    ]
    for copy in copies:
        copy.start()
    for copy in copies[:4]:
        copy.wait()
    n_v, n_nu = val.shape
    n_b = exciton.shape[0] // n_v
    for t in range(cond.shape[1] // TILE):
        set_panels(panels.at[t % 2], cond[:, t * TILE:(t + 1) * TILE], exciton[...], n_v)
        for j in range(n_nu // CHUNK):
            at = slice(j * CHUNK, (j + 1) * CHUNK)
            product = jnp.dot(panels[t % 2], val[:, at], preferred_element_type=F32)
            weights = w_own[t * TILE:(t + 1) * TILE, at].astype(F32)
            for b in range(n_b):
                rows = slice(b * TILE, (b + 1) * TILE)
                sums[t, rows, at] = product[rows, :] * weights
    for copy in copies[4:]:
        copy.wait()


def put_together(cores, col, cond, exciton):
    n_col, n_c, n_mu = len(cores), cond.shape[0], cond.shape[1]
    part_c, part_x = n_c // n_col, exciton.shape[0] // n_col
    for other, source in enumerate(cores):
        at = 0
        rows = pl.ds(pl.multiple_of((col ^ other) * part_c, part_c), part_c)
        for block in range(n_mu // LANES):
            cond[rows, block * LANES:(block + 1) * LANES] = source[at:at + part_c, :]
            at += part_c
        rows = pl.ds(pl.multiple_of((col ^ other) * part_x, part_x), part_x)
        exciton[rows, :] = source[at:at + part_x, :]


def panels_kernel(n_col, n_v, *refs):
    *cores, panels, cond, exciton = refs
    col = lax.axis_index("col")
    for i in range(panels.shape[0]):
        put_together(cores[i * n_col:(i + 1) * n_col], col, cond.at[i], exciton.at[i])
        for t in range(panels.shape[1]):
            set_panels(panels.at[i, t], cond[i, :, t * TILE:(t + 1) * TILE], exciton[i], n_v)


def after_kernel(*refs):
    refs[-1][...] = refs[0][...]


def after(value, *others, flops=0):
    return pl.pallas_call(
        after_kernel,
        in_specs=[IN_VMEM] + [pl.BlockSpec(memory_space=pl.ANY)] * len(others),
        out_specs=IN_VMEM,
        out_shape=jax.ShapeDtypeStruct(value.shape, value.dtype),
        compiler_params=pltpu.CompilerParams(vmem_limit_bytes=4 * MIB),
        cost_estimate=pl.CostEstimate(flops=flops, bytes_accessed=0, transcendentals=0),
        name="after",
    )(value, *others)


def direct_kernel(sizes, early, factor, *refs):
    n_ka, n_row, n_col = sizes
    refs = list(refs)

    def take(count):
        taken, refs[:] = refs[:count], refs[count:]
        return taken

    sums, w, cond_own, val_own, early_panels = take(5)
    n_early = early_panels.shape[0]
    late = [flip for flip in range(1, n_ka) if flip not in early]
    cores = [take(n_col) for _ in late]
    val_ref, = take(1)
    keep, *sent = take(n_col)
    x_all, cond_all, panels, products, direct, running, total, result = refs
    col = lax.axis_index("col")
    n_v, n_nu = val_own.shape
    n_c, n_mu = cond_own.shape
    n_b = x_all.shape[1] // n_v
    n_tiles, n_others = n_mu // TILE, n_ka - 1
    order = list(early) + late

    for i in range(len(late)):
        put_together(cores[i], col, cond_all.at[i], x_all.at[i])

    steps = [(t, j) for t in range(n_tiles) for j in range(n_nu // CHUNK)]
    quarter = TILE // QUARTERS

    def all_panels(t):
        for i in range(len(late)):
            set_panels(panels.at[t % 2, i], cond_all[i, :, t * TILE:(t + 1) * TILE], x_all[i], n_v)

    def multiply(number, i):
        t, j = steps[number]
        left = early_panels[i, t] if i < n_early else panels[t % 2, i - n_early]
        products[number % 2, i] = jnp.dot(
            left, val_ref[order[i] - 1, :, j * CHUNK:(j + 1) * CHUNK],
            preferred_element_type=F32,
        ).astype(BF16)

    def combine(number, part):
        t, j = steps[number]
        at = slice(j * CHUNK, (j + 1) * CHUNK)
        for m in range(part * quarter, (part + 1) * quarter, ROWS):
            weights = [
                w[flip - 1, t * TILE + m:t * TILE + m + ROWS, at].astype(F32) for flip in order
            ]
            for b in range(n_b):
                rows = slice(b * TILE + m, b * TILE + m + ROWS)
                value = sums[t, rows, at]
                for i in range(n_others):
                    value += products[number % 2, i, rows, :].astype(F32) * weights[i]
                direct[t % 2, rows, at] = value.astype(BF16)

    def reduce(number):
        t, j = steps[number]
        at = slice(j * CHUNK, (j + 1) * CHUNK)
        value = lax.dot_general(
            direct[t % 2, :, at], val_own[:, at], (((1,), (1,)), ((), ())),
            preferred_element_type=F32,
        )
        if j:
            value += running[...]
        if j + 1 < n_nu // CHUNK:
            running[...] = value
            return
        value = value.astype(BF16)
        for b in range(n_b):
            part = jnp.dot(
                cond_own[:, t * TILE:(t + 1) * TILE], value[b * TILE:(b + 1) * TILE, :],
                preferred_element_type=F32,
            )
            total[b] = total[b] + part if t else part

    all_panels(0)
    for i in range(n_others):
        multiply(0, i)
    for number, (t, j) in enumerate(steps):
        more = number + 1 < len(steps)
        if more and steps[number + 1][0] != t:
            all_panels(t + 1)
        for i in range(max(n_others, QUARTERS)):
            if more and i < n_others:
                multiply(number + 1, i)
            if i < QUARTERS:
                combine(number, i)
            if i == 0 and number:
                reduce(number - 1)
    reduce(len(steps) - 1)

    part = n_v // n_col
    for b in range(n_b):
        result[...] = (total[b] * factor).T
        for other in range(n_col):
            rows = pl.ds(pl.multiple_of((col ^ other) * part, part), part)
            if other == 0:
                keep[b] = result[rows, :]
            else:
                sent[other - 1][b] = result[rows, :].astype(BF16)


def local(sizes, exciton, orb_cond, orb_val, screened, q_table):
    n_ka, n_row, n_col = sizes
    n_b, n_v, n_c = exciton.shape[1:]
    x_rows, cond, val, screened, q_table = (
        pltpu.with_memory_space_constraint(array, pltpu.HBM)
        for array in (exciton.reshape(n_b * n_v, n_c), orb_cond[0], orb_val[0], screened, q_table)
    )
    n_mu, n_nu = cond.shape[1], val.shape[1]
    core_rows = (cond.size + x_rows.size) // n_col // LANES
    part = n_v // n_row
    plane = lax.dynamic_slice_in_dim(orb_val[0], lax.axis_index("row") * part, part, 0)
    planes = [swap(plane, "ka", n_ka, flip) for flip in range(1, n_ka)]
    core = pl.pallas_call(
        functools.partial(pack_kernel, n_col),
        in_specs=[IN_HBM] * 2 + [pl.BlockSpec(memory_space=pl.ANY)],
        out_specs=IN_VMEM,
        out_shape=jax.ShapeDtypeStruct((core_rows, LANES), BF16),
        scratch_shapes=[pltpu.SemaphoreType.DMA(((n_mu + n_c) // LANES,))],
        compiler_params=pltpu.CompilerParams(vmem_limit_bytes=4 * MIB),
        name="pack",
    )(x_rows, cond, planes[0])
    joined = join(planes)
    cores = [core]
    for flip in range(1, n_ka):
        last = flip & -flip
        source = cores[flip - last]
        if flip == last and flip > 1:
            source = after(source, planes[flip - 1])
        cores.append(swap(source, "ka", n_ka, last))
        if flip == 2:
            cores[2] = after(cores[2], joined, cores[1])
    n_tiles = n_mu // TILE
    loaded = pl.pallas_call(
        own_kernel,
        in_specs=[IN_SMEM] + [IN_HBM] * 4 + [pl.BlockSpec(memory_space=pl.ANY)],
        out_specs=[IN_VMEM] * 4,
        out_shape=[
            jax.ShapeDtypeStruct((n_tiles, n_b * TILE, n_nu), F32),
            jax.ShapeDtypeStruct((n_ka - 1, n_mu, n_nu), BF16),
            jax.ShapeDtypeStruct(cond.shape, BF16),
            jax.ShapeDtypeStruct(val.shape, BF16),
        ],
        scratch_shapes=[
            pltpu.VMEM((n_mu, n_nu), BF16),
            pltpu.VMEM(x_rows.shape, BF16),
            pltpu.VMEM((2, n_b * TILE, n_v), BF16),
            pltpu.SemaphoreType.DMA((n_ka + 3,)),
        ],
        compiler_params=pltpu.CompilerParams(vmem_limit_bytes=24 * MIB),
        cost_estimate=pl.CostEstimate(
            flops=0, bytes_accessed=4 * screened.size, transcendentals=0
        ),
        name="own_term",
    )(q_table, screened, x_rows, cond, val, cores[n_ka // 2])
    early = [flip for flip in range(1, n_ka) if flip.bit_count() == 1]
    both = {
        flip: [swap(cores[flip], "col", n_col, d) if d else cores[flip] for d in range(n_col)]
        for flip in range(1, n_ka)
    }
    operands = [pl.pallas_call(
        functools.partial(panels_kernel, n_col, n_v),
        in_specs=[IN_VMEM] * (len(early) * n_col),
        out_specs=IN_VMEM,
        out_shape=jax.ShapeDtypeStruct((len(early), n_tiles, n_b * TILE, n_v), BF16),
        scratch_shapes=[
            pltpu.VMEM((len(early), n_c, n_mu), BF16),
            pltpu.VMEM((len(early), n_b * n_v, n_c), BF16),
        ],
        compiler_params=pltpu.CompilerParams(vmem_limit_bytes=12 * MIB),
        cost_estimate=pl.CostEstimate(flops=PANEL_FLOPS, bytes_accessed=0, transcendentals=0),
        name="panels",
    )(*(part for flip in early for part in both[flip]))]
    operands += [part for flip in both if flip not in early for part in both[flip]]
    parts = [swap(joined, "row", n_row, d) if d else joined for d in range(n_row)]
    operands.append(pl.pallas_call(
        functools.partial(spread_kernel, n_row),
        in_specs=[IN_VMEM] * n_row,
        out_specs=IN_VMEM,
        out_shape=jax.ShapeDtypeStruct((n_ka - 1, *val.shape), BF16),
        compiler_params=pltpu.CompilerParams(vmem_limit_bytes=4 * MIB),
        cost_estimate=pl.CostEstimate(flops=SPREAD_FLOPS, bytes_accessed=0, transcendentals=0),
        name="spread",
    )(*parts))

    factor = math.sqrt(n_v * n_c) / (n_mu * n_row)
    part = n_v // n_col
    n_late = n_ka - 1 - len(early)
    kept, *sent = pl.pallas_call(
        functools.partial(direct_kernel, sizes, early, factor),
        in_specs=[IN_VMEM] * (len(loaded) + len(operands)),
        out_specs=[IN_VMEM] * n_col,
        out_shape=[jax.ShapeDtypeStruct((n_b, part, n_c), F32)]
        + [jax.ShapeDtypeStruct((n_b, part, n_c), BF16)] * (n_col - 1),
        scratch_shapes=[
            pltpu.VMEM((n_late, n_b * n_v, n_c), BF16),
            pltpu.VMEM((n_late, n_c, n_mu), BF16),
            pltpu.VMEM((2, n_late, n_b * TILE, n_v), BF16),
            pltpu.VMEM((2, n_ka - 1, n_b * TILE, CHUNK), BF16),
            pltpu.VMEM((2, n_b * TILE, n_nu), BF16),
            pltpu.VMEM((n_b * TILE, n_v), F32),
            pltpu.VMEM((n_b, n_c, n_v), F32),
            pltpu.VMEM((n_v, n_c), F32),
        ],
        compiler_params=pltpu.CompilerParams(vmem_limit_bytes=36 * MIB),
        name="direct_term",
    )(*loaded, *operands)
    mine = kept
    for flip in range(1, n_col):
        mine = mine + swap(sent[flip - 1], "col", n_col, flip).astype(F32)
    mine = mine.astype(BF16)
    terms = [after(swap(mine, "row", n_row, n_row - 1), flops=JOIN_FLOPS)]
    terms += [swap(mine, "row", n_row, flip) for flip in reversed(range(1, n_row - 1))] + [mine]
    terms = [term.astype(F32) for term in terms]
    while len(terms) > 1:
        terms = [a + b for a, b in zip(terms[::2], terms[1::2])]
    return terms[0][None]


def solution(mesh):
    placed = (
        P("ka", None, None, None),
        P("ka", None, "row"),
        P("ka", None, "col"),
        P(None, "row", "col"),
        P(),
    )
    sizes = tuple(mesh.shape[name] for name in ("ka", "row", "col"))
    return jax.shard_map(
        functools.partial(local, sizes), mesh=mesh, in_specs=placed,
        out_specs=P("ka", None, "col", None), check_vma=False,
    )
```

```python
import functools
import math

import jax
import jax.numpy as jnp
from jax import lax
from jax.experimental import pallas as pl
from jax.experimental.pallas import tpu as pltpu
from jax.sharding import PartitionSpec as P

BF16 = jnp.bfloat16
F32 = jnp.float32
LANES = 128
ROWS = 16
TILE = 128
CHUNK = 256
QUARTERS = 4
MIB = 2**20
JOIN_FLOPS = 2 * 10**10
SPREAD_FLOPS = 2 * 10**10
PANEL_FLOPS = 10**9
IN_HBM = pl.BlockSpec(memory_space=pltpu.HBM)
IN_VMEM = pl.BlockSpec(memory_space=pltpu.VMEM)
IN_SMEM = pl.BlockSpec(memory_space=pltpu.SMEM)


def swap(value, axis, size, flip):
    return lax.ppermute(value, axis, [(i, i ^ flip) for i in range(size)])


def run(copies):
    for copy in copies:
        copy.start()
    for copy in copies:
        copy.wait()


def pack_kernel(n_col, exciton_ref, cond_ref, core_ref, sems):
    col = lax.axis_index("col")
    copies, at = [], 0
    for source in (cond_ref, exciton_ref):
        part = source.shape[0] // n_col
        rows = pl.ds(pl.multiple_of(col * part, part), part)
        for block in range(source.shape[1] // LANES):
            copies.append(pltpu.make_async_copy(
                source.at[rows, block * LANES:(block + 1) * LANES],
                core_ref.at[at:at + part, :], sems.at[len(copies)],
            ))
            at += part
    run(copies)


def join_kernel(*refs):
    *parts, out = refs
    at = 0
    for part in parts:
        out[at:at + part.shape[0], :] = part[...]
        at += part.shape[0]


def join(parts):
    shape = (sum(part.shape[0] for part in parts), parts[0].shape[1])
    return pl.pallas_call(
        join_kernel,
        in_specs=[IN_VMEM] * len(parts),
        out_specs=IN_VMEM,
        out_shape=jax.ShapeDtypeStruct(shape, BF16),
        compiler_params=pltpu.CompilerParams(vmem_limit_bytes=4 * MIB),
        cost_estimate=pl.CostEstimate(flops=JOIN_FLOPS, bytes_accessed=0, transcendentals=0),
        name="join",
    )(*parts)


def spread_kernel(n_row, *refs):
    *parts, out = refs
    row = lax.axis_index("row")
    part = out.shape[1] // n_row
    for other in range(n_row):
        rows = pl.ds(pl.multiple_of((row ^ other) * part, part), part)
        for flip in range(out.shape[0]):
            out[flip, rows, :] = parts[other][flip * part:(flip + 1) * part, :]


def set_panels(panels, cond_tile, exciton, n_v):
    by_point = lax.dot_general(
        cond_tile, exciton, (((0,), (1,)), ((), ())), preferred_element_type=F32
    ).astype(BF16)
    for b in range(exciton.shape[0] // n_v):
        panels[b * TILE:(b + 1) * TILE, :] = by_point[:, b * n_v:(b + 1) * n_v]


def own_kernel(
    q_ref, w_ref, exciton_ref, cond_ref, val_ref, after_ref, sums, w, cond, val, w_own, exciton, panels, sems
):
    del after_ref
    me, n_others = lax.axis_index("ka"), w.shape[0]
    pairs = [(exciton_ref, exciton), (cond_ref, cond), (val_ref, val)]
    pairs += [(w_ref.at[q_ref[me, me]], w_own)]
    pairs += [(w_ref.at[q_ref[me ^ flip, me]], w.at[flip - 1]) for flip in range(1, n_others + 1)]
    copies = [
        pltpu.make_async_copy(source, target, sems.at[i])
        for i, (source, target) in enumerate(pairs)
    ]
    for copy in copies:
        copy.start()
    for copy in copies[:4]:
        copy.wait()
    n_v, n_nu = val.shape
    n_b = exciton.shape[0] // n_v
    for t in range(cond.shape[1] // TILE):
        set_panels(panels.at[t % 2], cond[:, t * TILE:(t + 1) * TILE], exciton[...], n_v)
        for j in range(n_nu // CHUNK):
            at = slice(j * CHUNK, (j + 1) * CHUNK)
            product = jnp.dot(panels[t % 2], val[:, at], preferred_element_type=F32)
            weights = w_own[t * TILE:(t + 1) * TILE, at].astype(F32)
            for b in range(n_b):
                rows = slice(b * TILE, (b + 1) * TILE)
                sums[t, rows, at] = product[rows, :] * weights
    for copy in copies[4:]:
        copy.wait()


def put_together(cores, col, cond, exciton):
    n_col, n_c, n_mu = len(cores), cond.shape[0], cond.shape[1]
    part_c, part_x = n_c // n_col, exciton.shape[0] // n_col
    for other, source in enumerate(cores):
        at = 0
        rows = pl.ds(pl.multiple_of((col ^ other) * part_c, part_c), part_c)
        for block in range(n_mu // LANES):
            cond[rows, block * LANES:(block + 1) * LANES] = source[at:at + part_c, :]
            at += part_c
        rows = pl.ds(pl.multiple_of((col ^ other) * part_x, part_x), part_x)
        exciton[rows, :] = source[at:at + part_x, :]


def panels_kernel(n_col, n_v, *refs):
    *cores, panels, cond, exciton = refs
    col = lax.axis_index("col")
    for i in range(panels.shape[0]):
        put_together(cores[i * n_col:(i + 1) * n_col], col, cond.at[i], exciton.at[i])
        for t in range(panels.shape[1]):
            set_panels(panels.at[i, t], cond[i, :, t * TILE:(t + 1) * TILE], exciton[i], n_v)


def after_kernel(*refs):
    refs[-1][...] = refs[0][...]


def after(value, *others, flops=0):
    return pl.pallas_call(
        after_kernel,
        in_specs=[IN_VMEM] + [pl.BlockSpec(memory_space=pl.ANY)] * len(others),
        out_specs=IN_VMEM,
        out_shape=jax.ShapeDtypeStruct(value.shape, value.dtype),
        compiler_params=pltpu.CompilerParams(vmem_limit_bytes=4 * MIB),
        cost_estimate=pl.CostEstimate(flops=flops, bytes_accessed=0, transcendentals=0),
        name="after",
    )(value, *others)


def direct_kernel(sizes, early, factor, *refs):
    n_ka, n_row, n_col = sizes
    refs = list(refs)

    def take(count):
        taken, refs[:] = refs[:count], refs[count:]
        return taken

    sums, w, cond_own, val_own, early_panels = take(5)
    n_early = early_panels.shape[0]
    late = [flip for flip in range(1, n_ka) if flip not in early]
    cores = [take(n_col) for _ in late]
    val_ref, = take(1)
    keep, *sent = take(n_col)
    x_all, cond_all, panels, products, direct, running, half, total = refs
    col = lax.axis_index("col")
    n_v, n_nu = val_own.shape
    n_c, n_mu = cond_own.shape
    n_b = x_all.shape[1] // n_v
    n_tiles, n_others = n_mu // TILE, n_ka - 1
    order = list(early) + late

    for i in range(len(late)):
        put_together(cores[i], col, cond_all.at[i], x_all.at[i])

    steps = [(t, j) for t in range(n_tiles) for j in range(n_nu // CHUNK)]
    quarter = TILE // QUARTERS

    def all_panels(t):
        for i in range(len(late)):
            set_panels(panels.at[t % 2, i], cond_all[i, :, t * TILE:(t + 1) * TILE], x_all[i], n_v)

    def multiply(number, i):
        t, j = steps[number]
        left = early_panels[i, t] if i < n_early else panels[t % 2, i - n_early]
        products[number % 2, i] = jnp.dot(
            left, val_ref[order[i] - 1, :, j * CHUNK:(j + 1) * CHUNK],
            preferred_element_type=F32,
        ).astype(BF16)

    def combine(number, part):
        t, j = steps[number]
        at = slice(j * CHUNK, (j + 1) * CHUNK)
        for m in range(part * quarter, (part + 1) * quarter, ROWS):
            weights = [
                w[flip - 1, t * TILE + m:t * TILE + m + ROWS, at].astype(F32) for flip in order
            ]
            for b in range(n_b):
                rows = slice(b * TILE + m, b * TILE + m + ROWS)
                value = sums[t, rows, at]
                for i in range(n_others):
                    value += products[number % 2, i, rows, :].astype(F32) * weights[i]
                direct[t % 2, rows, at] = value.astype(BF16)

    def reduce(number):
        t, j = steps[number]
        at = slice(j * CHUNK, (j + 1) * CHUNK)
        value = lax.dot_general(
            direct[t % 2, :, at], val_own[:, at], (((1,), (1,)), ((), ())),
            preferred_element_type=F32,
        )
        if j:
            value += running[...]
        if j + 1 < n_nu // CHUNK:
            running[...] = value
            return
        value = value.astype(BF16)
        for b in range(n_b):
            half[b, t * TILE:(t + 1) * TILE, :] = value[b * TILE:(b + 1) * TILE, :]

    all_panels(0)
    for i in range(n_others):
        multiply(0, i)
    for number, (t, j) in enumerate(steps):
        more = number + 1 < len(steps)
        if more and steps[number + 1][0] != t:
            all_panels(t + 1)
        for i in range(max(n_others, QUARTERS)):
            if more and i < n_others:
                multiply(number + 1, i)
            if i < QUARTERS:
                combine(number, i)
        reduce(number)

    part = n_v // n_col
    for b in range(n_b):
        total[b * n_v:(b + 1) * n_v, :] = (
            jnp.dot(cond_own[...], half[b], preferred_element_type=F32) * factor
        ).T
        for other in range(n_col):
            rows = pl.ds(pl.multiple_of(b * n_v + (col ^ other) * part, part), part)
            value = total[rows, :]
            if other == 0:
                keep[b] = value
            else:
                sent[other - 1][b] = value.astype(BF16)


def local(sizes, exciton, orb_cond, orb_val, screened, q_table):
    n_ka, n_row, n_col = sizes
    n_b, n_v, n_c = exciton.shape[1:]
    x_rows, cond, val, screened, q_table = (
        pltpu.with_memory_space_constraint(array, pltpu.HBM)
        for array in (exciton.reshape(n_b * n_v, n_c), orb_cond[0], orb_val[0], screened, q_table)
    )
    n_mu, n_nu = cond.shape[1], val.shape[1]
    core_rows = (cond.size + x_rows.size) // n_col // LANES
    part = n_v // n_row
    plane = lax.dynamic_slice_in_dim(orb_val[0], lax.axis_index("row") * part, part, 0)
    core = pl.pallas_call(
        functools.partial(pack_kernel, n_col),
        in_specs=[IN_HBM] * 2,
        out_specs=IN_VMEM,
        out_shape=jax.ShapeDtypeStruct((core_rows, LANES), BF16),
        scratch_shapes=[pltpu.SemaphoreType.DMA(((n_mu + n_c) // LANES,))],
        compiler_params=pltpu.CompilerParams(vmem_limit_bytes=4 * MIB),
        name="pack",
    )(x_rows, cond)
    planes = [plane]
    for flip in range(1, n_ka):
        last = flip & -flip
        source = planes[flip - last]
        if flip > last:
            source = after(source, core)
        planes.append(swap(source, "ka", n_ka, last))
    planes = planes[1:]
    joined = join(planes)
    cores = [core]
    for flip in range(1, n_ka):
        last = flip & -flip
        source = cores[flip - last]
        if flip == last:
            source = after(source, planes[flip - 1])
        cores.append(swap(source, "ka", n_ka, last))
        if flip == 2:
            cores[2] = after(cores[2], joined, cores[1])
    n_tiles = n_mu // TILE
    loaded = pl.pallas_call(
        own_kernel,
        in_specs=[IN_SMEM] + [IN_HBM] * 4 + [pl.BlockSpec(memory_space=pl.ANY)],
        out_specs=[IN_VMEM] * 4,
        out_shape=[
            jax.ShapeDtypeStruct((n_tiles, n_b * TILE, n_nu), F32),
            jax.ShapeDtypeStruct((n_ka - 1, n_mu, n_nu), BF16),
            jax.ShapeDtypeStruct(cond.shape, BF16),
            jax.ShapeDtypeStruct(val.shape, BF16),
        ],
        scratch_shapes=[
            pltpu.VMEM((n_mu, n_nu), BF16),
            pltpu.VMEM(x_rows.shape, BF16),
            pltpu.VMEM((2, n_b * TILE, n_v), BF16),
            pltpu.SemaphoreType.DMA((n_ka + 3,)),
        ],
        compiler_params=pltpu.CompilerParams(vmem_limit_bytes=24 * MIB),
        cost_estimate=pl.CostEstimate(
            flops=0, bytes_accessed=4 * screened.size, transcendentals=0
        ),
        name="own_term",
    )(q_table, screened, x_rows, cond, val, cores[n_ka // 2])
    early = [flip for flip in range(1, n_ka) if flip.bit_count() == 1]
    both = {
        flip: [swap(cores[flip], "col", n_col, d) if d else cores[flip] for d in range(n_col)]
        for flip in range(1, n_ka)
    }
    operands = [pl.pallas_call(
        functools.partial(panels_kernel, n_col, n_v),
        in_specs=[IN_VMEM] * (len(early) * n_col),
        out_specs=IN_VMEM,
        out_shape=jax.ShapeDtypeStruct((len(early), n_tiles, n_b * TILE, n_v), BF16),
        scratch_shapes=[
            pltpu.VMEM((len(early), n_c, n_mu), BF16),
            pltpu.VMEM((len(early), n_b * n_v, n_c), BF16),
        ],
        compiler_params=pltpu.CompilerParams(vmem_limit_bytes=12 * MIB),
        cost_estimate=pl.CostEstimate(flops=PANEL_FLOPS, bytes_accessed=0, transcendentals=0),
        name="panels",
    )(*(part for flip in early for part in both[flip]))]
    operands += [part for flip in both if flip not in early for part in both[flip]]
    parts = [swap(joined, "row", n_row, d) if d else joined for d in range(n_row)]
    operands.append(pl.pallas_call(
        functools.partial(spread_kernel, n_row),
        in_specs=[IN_VMEM] * n_row,
        out_specs=IN_VMEM,
        out_shape=jax.ShapeDtypeStruct((n_ka - 1, *val.shape), BF16),
        compiler_params=pltpu.CompilerParams(vmem_limit_bytes=4 * MIB),
        cost_estimate=pl.CostEstimate(flops=SPREAD_FLOPS, bytes_accessed=0, transcendentals=0),
        name="spread",
    )(*parts))

    factor = math.sqrt(n_v * n_c) / (n_mu * n_row)
    part = n_v // n_col
    n_late = n_ka - 1 - len(early)
    kept, *sent = pl.pallas_call(
        functools.partial(direct_kernel, sizes, early, factor),
        in_specs=[IN_VMEM] * (len(loaded) + len(operands)),
        out_specs=[IN_VMEM] * n_col,
        out_shape=[jax.ShapeDtypeStruct((n_b, part, n_c), F32)]
        + [jax.ShapeDtypeStruct((n_b, part, n_c), BF16)] * (n_col - 1),
        scratch_shapes=[
            pltpu.VMEM((n_late, n_b * n_v, n_c), BF16),
            pltpu.VMEM((n_late, n_c, n_mu), BF16),
            pltpu.VMEM((2, n_late, n_b * TILE, n_v), BF16),
            pltpu.VMEM((2, n_ka - 1, n_b * TILE, CHUNK), BF16),
            pltpu.VMEM((2, n_b * TILE, n_nu), BF16),
            pltpu.VMEM((n_b * TILE, n_v), F32),
            pltpu.VMEM((n_b, n_mu, n_v), BF16),
            pltpu.VMEM((n_b * n_v, n_c), F32),
        ],
        compiler_params=pltpu.CompilerParams(vmem_limit_bytes=36 * MIB),
        name="direct_term",
    )(*loaded, *operands)
    mine = kept
    for flip in range(1, n_col):
        mine = mine + swap(sent[flip - 1], "col", n_col, flip).astype(F32)
    mine = mine.astype(BF16)
    terms = [after(swap(mine, "row", n_row, n_row - 1), flops=JOIN_FLOPS)]
    terms += [swap(mine, "row", n_row, flip) for flip in reversed(range(1, n_row - 1))] + [mine]
    terms = [term.astype(F32) for term in terms]
    while len(terms) > 1:
        terms = [a + b for a, b in zip(terms[::2], terms[1::2])]
    return terms[0][None]


def solution(mesh):
    placed = (
        P("ka", None, None, None),
        P("ka", None, "row"),
        P("ka", None, "col"),
        P(None, "row", "col"),
        P(),
    )
    sizes = tuple(mesh.shape[name] for name in ("ka", "row", "col"))
    return jax.shard_map(
        functools.partial(local, sizes), mesh=mesh, in_specs=placed,
        out_specs=P("ka", None, "col", None), check_vma=False,
    )
```

```python
import functools
import math

import jax
import jax.numpy as jnp
from jax import lax
from jax.experimental import pallas as pl
from jax.experimental.pallas import tpu as pltpu
from jax.sharding import PartitionSpec as P

BF16 = jnp.bfloat16
F32 = jnp.float32
LANES = 128
ROWS = 16
TILE = 64
CHUNK = 256
QUARTERS = 4
MIB = 2**20
JOIN_FLOPS = 2 * 10**10
SPREAD_FLOPS = 2 * 10**10
PANEL_FLOPS = 10**9
IN_HBM = pl.BlockSpec(memory_space=pltpu.HBM)
IN_VMEM = pl.BlockSpec(memory_space=pltpu.VMEM)
IN_SMEM = pl.BlockSpec(memory_space=pltpu.SMEM)


def swap(value, axis, size, flip):
    return lax.ppermute(value, axis, [(i, i ^ flip) for i in range(size)])


def run(copies):
    for copy in copies:
        copy.start()
    for copy in copies:
        copy.wait()


def pack_kernel(n_col, exciton_ref, cond_ref, after_ref, core_ref, sems):
    del after_ref
    col = lax.axis_index("col")
    copies, at = [], 0
    for source in (cond_ref, exciton_ref):
        part = source.shape[0] // n_col
        rows = pl.ds(pl.multiple_of(col * part, part), part)
        for block in range(source.shape[1] // LANES):
            copies.append(pltpu.make_async_copy(
                source.at[rows, block * LANES:(block + 1) * LANES],
                core_ref.at[at:at + part, :], sems.at[len(copies)],
            ))
            at += part
    run(copies)


def join_kernel(*refs):
    *parts, out = refs
    at = 0
    for part in parts:
        out[at:at + part.shape[0], :] = part[...]
        at += part.shape[0]


def join(parts):
    shape = (sum(part.shape[0] for part in parts), parts[0].shape[1])
    return pl.pallas_call(
        join_kernel,
        in_specs=[IN_VMEM] * len(parts),
        out_specs=IN_VMEM,
        out_shape=jax.ShapeDtypeStruct(shape, BF16),
        compiler_params=pltpu.CompilerParams(vmem_limit_bytes=4 * MIB),
        cost_estimate=pl.CostEstimate(flops=JOIN_FLOPS, bytes_accessed=0, transcendentals=0),
        name="join",
    )(*parts)


def spread_kernel(n_row, *refs):
    *parts, out = refs
    row = lax.axis_index("row")
    part = out.shape[1] // n_row
    for other in range(n_row):
        rows = pl.ds(pl.multiple_of((row ^ other) * part, part), part)
        for flip in range(out.shape[0]):
            out[flip, rows, :] = parts[other][flip * part:(flip + 1) * part, :]


def set_panels(panels, cond_tile, exciton, n_v):
    by_point = lax.dot_general(
        cond_tile, exciton, (((0,), (1,)), ((), ())), preferred_element_type=F32
    ).astype(BF16)
    for b in range(exciton.shape[0] // n_v):
        panels[b * TILE:(b + 1) * TILE, :] = by_point[:, b * n_v:(b + 1) * n_v]


def own_kernel(
    q_ref, w_ref, exciton_ref, cond_ref, val_ref, after_ref, sums, w, cond, val, w_own, exciton, panels, sems
):
    del after_ref
    me, n_others = lax.axis_index("ka"), w.shape[0]
    pairs = [(exciton_ref, exciton), (cond_ref, cond), (val_ref, val)]
    pairs += [(w_ref.at[q_ref[me, me]], w_own)]
    pairs += [(w_ref.at[q_ref[me ^ flip, me]], w.at[flip - 1]) for flip in range(1, n_others + 1)]
    copies = [
        pltpu.make_async_copy(source, target, sems.at[i])
        for i, (source, target) in enumerate(pairs)
    ]
    for copy in copies:
        copy.start()
    for copy in copies[:4]:
        copy.wait()
    n_v, n_nu = val.shape
    n_b = exciton.shape[0] // n_v
    for t in range(cond.shape[1] // TILE):
        set_panels(panels.at[t % 2], cond[:, t * TILE:(t + 1) * TILE], exciton[...], n_v)
        for j in range(n_nu // CHUNK):
            at = slice(j * CHUNK, (j + 1) * CHUNK)
            product = jnp.dot(panels[t % 2], val[:, at], preferred_element_type=F32)
            weights = w_own[t * TILE:(t + 1) * TILE, at].astype(F32)
            for b in range(n_b):
                rows = slice(b * TILE, (b + 1) * TILE)
                sums[t, rows, at] = product[rows, :] * weights
    for copy in copies[4:]:
        copy.wait()


def put_together(cores, col, cond, exciton):
    n_col, n_c, n_mu = len(cores), cond.shape[0], cond.shape[1]
    part_c, part_x = n_c // n_col, exciton.shape[0] // n_col
    for other, source in enumerate(cores):
        at = 0
        rows = pl.ds(pl.multiple_of((col ^ other) * part_c, part_c), part_c)
        for block in range(n_mu // LANES):
            cond[rows, block * LANES:(block + 1) * LANES] = source[at:at + part_c, :]
            at += part_c
        rows = pl.ds(pl.multiple_of((col ^ other) * part_x, part_x), part_x)
        exciton[rows, :] = source[at:at + part_x, :]


def panels_kernel(n_col, n_v, *refs):
    *cores, panels, cond, exciton = refs
    col = lax.axis_index("col")
    for i in range(panels.shape[0]):
        put_together(cores[i * n_col:(i + 1) * n_col], col, cond.at[i], exciton.at[i])
        for t in range(panels.shape[1]):
            set_panels(panels.at[i, t], cond[i, :, t * TILE:(t + 1) * TILE], exciton[i], n_v)


def after_kernel(*refs):
    refs[-1][...] = refs[0][...]


def after(value, *others, flops=0):
    return pl.pallas_call(
        after_kernel,
        in_specs=[IN_VMEM] + [pl.BlockSpec(memory_space=pl.ANY)] * len(others),
        out_specs=IN_VMEM,
        out_shape=jax.ShapeDtypeStruct(value.shape, value.dtype),
        compiler_params=pltpu.CompilerParams(vmem_limit_bytes=4 * MIB),
        cost_estimate=pl.CostEstimate(flops=flops, bytes_accessed=0, transcendentals=0),
        name="after",
    )(value, *others)


def direct_kernel(sizes, early, factor, *refs):
    n_ka, n_row, n_col = sizes
    refs = list(refs)

    def take(count):
        taken, refs[:] = refs[:count], refs[count:]
        return taken

    sums, w, cond_own, val_own, early_panels = take(5)
    n_early = early_panels.shape[0]
    late = [flip for flip in range(1, n_ka) if flip not in early]
    cores = [take(n_col) for _ in late]
    val_ref, = take(1)
    keep, *sent = take(n_col)
    x_all, cond_all, panels, products, direct, running, half, total = refs
    col = lax.axis_index("col")
    n_v, n_nu = val_own.shape
    n_c, n_mu = cond_own.shape
    n_b = x_all.shape[1] // n_v
    n_tiles, n_others = n_mu // TILE, n_ka - 1
    order = list(early) + late

    for i in range(len(late)):
        put_together(cores[i], col, cond_all.at[i], x_all.at[i])

    steps = [(t, j) for t in range(n_tiles) for j in range(n_nu // CHUNK)]
    quarter = TILE // QUARTERS

    def all_panels(t):
        for i in range(len(late)):
            set_panels(panels.at[t % 2, i], cond_all[i, :, t * TILE:(t + 1) * TILE], x_all[i], n_v)

    def multiply(number, i):
        t, j = steps[number]
        left = early_panels[i, t] if i < n_early else panels[t % 2, i - n_early]
        products[number % 2, i] = jnp.dot(
            left, val_ref[order[i] - 1, :, j * CHUNK:(j + 1) * CHUNK],
            preferred_element_type=F32,
        ).astype(BF16)

    def combine(number, part):
        t, j = steps[number]
        at = slice(j * CHUNK, (j + 1) * CHUNK)
        for m in range(part * quarter, (part + 1) * quarter, ROWS):
            weights = [
                w[flip - 1, t * TILE + m:t * TILE + m + ROWS, at].astype(F32) for flip in order
            ]
            for b in range(n_b):
                rows = slice(b * TILE + m, b * TILE + m + ROWS)
                value = sums[t, rows, at]
                for i in range(n_others):
                    value += products[number % 2, i, rows, :].astype(F32) * weights[i]
                direct[t % 2, rows, at] = value.astype(BF16)

    def reduce(number):
        t, j = steps[number]
        at = slice(j * CHUNK, (j + 1) * CHUNK)
        value = lax.dot_general(
            direct[t % 2, :, at], val_own[:, at], (((1,), (1,)), ((), ())),
            preferred_element_type=F32,
        )
        if j:
            value += running[...]
        if j + 1 < n_nu // CHUNK:
            running[...] = value
            return
        value = value.astype(BF16)
        for b in range(n_b):
            half[b, t * TILE:(t + 1) * TILE, :] = value[b * TILE:(b + 1) * TILE, :]

    all_panels(0)
    for i in range(n_others):
        multiply(0, i)
    for number, (t, j) in enumerate(steps):
        more = number + 1 < len(steps)
        if more and steps[number + 1][0] != t:
            all_panels(t + 1)
        for i in range(max(n_others, QUARTERS)):
            if more and i < n_others:
                multiply(number + 1, i)
            if i < QUARTERS:
                combine(number, i)
        reduce(number)

    part = n_v // n_col
    for b in range(n_b):
        total[b * n_v:(b + 1) * n_v, :] = (
            jnp.dot(cond_own[...], half[b], preferred_element_type=F32) * factor
        ).T
        for other in range(n_col):
            rows = pl.ds(pl.multiple_of(b * n_v + (col ^ other) * part, part), part)
            value = total[rows, :]
            if other == 0:
                keep[b] = value
            else:
                sent[other - 1][b] = value.astype(BF16)


def local(sizes, exciton, orb_cond, orb_val, screened, q_table):
    n_ka, n_row, n_col = sizes
    n_b, n_v, n_c = exciton.shape[1:]
    x_rows, cond, val, screened, q_table = (
        pltpu.with_memory_space_constraint(array, pltpu.HBM)
        for array in (exciton.reshape(n_b * n_v, n_c), orb_cond[0], orb_val[0], screened, q_table)
    )
    n_mu, n_nu = cond.shape[1], val.shape[1]
    core_rows = (cond.size + x_rows.size) // n_col // LANES
    part = n_v // n_row
    plane = lax.dynamic_slice_in_dim(orb_val[0], lax.axis_index("row") * part, part, 0)
    planes = [swap(plane, "ka", n_ka, flip) for flip in range(1, n_ka)]
    core = pl.pallas_call(
        functools.partial(pack_kernel, n_col),
        in_specs=[IN_HBM] * 2 + [pl.BlockSpec(memory_space=pl.ANY)],
        out_specs=IN_VMEM,
        out_shape=jax.ShapeDtypeStruct((core_rows, LANES), BF16),
        scratch_shapes=[pltpu.SemaphoreType.DMA(((n_mu + n_c) // LANES,))],
        compiler_params=pltpu.CompilerParams(vmem_limit_bytes=4 * MIB),
        name="pack",
    )(x_rows, cond, planes[0])
    joined = join(planes)
    cores = [core]
    for flip in range(1, n_ka):
        last = flip & -flip
        source = cores[flip - last]
        if flip == last and flip > 1:
            source = after(source, planes[flip - 1])
        cores.append(swap(source, "ka", n_ka, last))
        if flip == 2:
            cores[2] = after(cores[2], joined, cores[1])
    n_tiles = n_mu // TILE
    loaded = pl.pallas_call(
        own_kernel,
        in_specs=[IN_SMEM] + [IN_HBM] * 4 + [pl.BlockSpec(memory_space=pl.ANY)],
        out_specs=[IN_VMEM] * 4,
        out_shape=[
            jax.ShapeDtypeStruct((n_tiles, n_b * TILE, n_nu), F32),
            jax.ShapeDtypeStruct((n_ka - 1, n_mu, n_nu), BF16),
            jax.ShapeDtypeStruct(cond.shape, BF16),
            jax.ShapeDtypeStruct(val.shape, BF16),
        ],
        scratch_shapes=[
            pltpu.VMEM((n_mu, n_nu), BF16),
            pltpu.VMEM(x_rows.shape, BF16),
            pltpu.VMEM((2, n_b * TILE, n_v), BF16),
            pltpu.SemaphoreType.DMA((n_ka + 3,)),
        ],
        compiler_params=pltpu.CompilerParams(vmem_limit_bytes=24 * MIB),
        cost_estimate=pl.CostEstimate(
            flops=0, bytes_accessed=4 * screened.size, transcendentals=0
        ),
        name="own_term",
    )(q_table, screened, x_rows, cond, val, cores[n_ka // 2])
    early = [flip for flip in range(1, n_ka) if flip.bit_count() == 1]
    both = {
        flip: [swap(cores[flip], "col", n_col, d) if d else cores[flip] for d in range(n_col)]
        for flip in range(1, n_ka)
    }
    operands = [pl.pallas_call(
        functools.partial(panels_kernel, n_col, n_v),
        in_specs=[IN_VMEM] * (len(early) * n_col),
        out_specs=IN_VMEM,
        out_shape=jax.ShapeDtypeStruct((len(early), n_tiles, n_b * TILE, n_v), BF16),
        scratch_shapes=[
            pltpu.VMEM((len(early), n_c, n_mu), BF16),
            pltpu.VMEM((len(early), n_b * n_v, n_c), BF16),
        ],
        compiler_params=pltpu.CompilerParams(vmem_limit_bytes=12 * MIB),
        cost_estimate=pl.CostEstimate(flops=PANEL_FLOPS, bytes_accessed=0, transcendentals=0),
        name="panels",
    )(*(part for flip in early for part in both[flip]))]
    operands += [part for flip in both if flip not in early for part in both[flip]]
    parts = [swap(joined, "row", n_row, d) if d else joined for d in range(n_row)]
    operands.append(pl.pallas_call(
        functools.partial(spread_kernel, n_row),
        in_specs=[IN_VMEM] * n_row,
        out_specs=IN_VMEM,
        out_shape=jax.ShapeDtypeStruct((n_ka - 1, *val.shape), BF16),
        compiler_params=pltpu.CompilerParams(vmem_limit_bytes=4 * MIB),
        cost_estimate=pl.CostEstimate(flops=SPREAD_FLOPS, bytes_accessed=0, transcendentals=0),
        name="spread",
    )(*parts))

    factor = math.sqrt(n_v * n_c) / (n_mu * n_row)
    part = n_v // n_col
    n_late = n_ka - 1 - len(early)
    kept, *sent = pl.pallas_call(
        functools.partial(direct_kernel, sizes, early, factor),
        in_specs=[IN_VMEM] * (len(loaded) + len(operands)),
        out_specs=[IN_VMEM] * n_col,
        out_shape=[jax.ShapeDtypeStruct((n_b, part, n_c), F32)]
        + [jax.ShapeDtypeStruct((n_b, part, n_c), BF16)] * (n_col - 1),
        scratch_shapes=[
            pltpu.VMEM((n_late, n_b * n_v, n_c), BF16),
            pltpu.VMEM((n_late, n_c, n_mu), BF16),
            pltpu.VMEM((2, n_late, n_b * TILE, n_v), BF16),
            pltpu.VMEM((2, n_ka - 1, n_b * TILE, CHUNK), BF16),
            pltpu.VMEM((2, n_b * TILE, n_nu), BF16),
            pltpu.VMEM((n_b * TILE, n_v), F32),
            pltpu.VMEM((n_b, n_mu, n_v), BF16),
            pltpu.VMEM((n_b * n_v, n_c), F32),
        ],
        compiler_params=pltpu.CompilerParams(vmem_limit_bytes=36 * MIB),
        name="direct_term",
    )(*loaded, *operands)
    mine = kept
    for flip in range(1, n_col):
        mine = mine + swap(sent[flip - 1], "col", n_col, flip).astype(F32)
    mine = mine.astype(BF16)
    terms = [after(swap(mine, "row", n_row, n_row - 1), flops=JOIN_FLOPS)]
    terms += [swap(mine, "row", n_row, flip) for flip in reversed(range(1, n_row - 1))] + [mine]
    terms = [term.astype(F32) for term in terms]
    while len(terms) > 1:
        terms = [a + b for a, b in zip(terms[::2], terms[1::2])]
    return terms[0][None]


def solution(mesh):
    placed = (
        P("ka", None, None, None),
        P("ka", None, "row"),
        P("ka", None, "col"),
        P(None, "row", "col"),
        P(),
    )
    sizes = tuple(mesh.shape[name] for name in ("ka", "row", "col"))
    return jax.shard_map(
        functools.partial(local, sizes), mesh=mesh, in_specs=placed,
        out_specs=P("ka", None, "col", None), check_vma=False,
    )
```

```python
import functools
import math

import jax
import jax.numpy as jnp
from jax import lax
from jax.experimental import pallas as pl
from jax.experimental.pallas import tpu as pltpu
from jax.sharding import PartitionSpec as P

BF16 = jnp.bfloat16
F32 = jnp.float32
LANES = 128
ROWS = 16
TILE = 128
CHUNK = 256
QUARTERS = 4
MIB = 2**20
JOIN_FLOPS = 2 * 10**10
SPREAD_FLOPS = 2 * 10**10
PANEL_FLOPS = 10**9
IN_HBM = pl.BlockSpec(memory_space=pltpu.HBM)
IN_VMEM = pl.BlockSpec(memory_space=pltpu.VMEM)
IN_SMEM = pl.BlockSpec(memory_space=pltpu.SMEM)


def swap(value, axis, size, flip):
    return lax.ppermute(value, axis, [(i, i ^ flip) for i in range(size)])


def run(copies):
    for copy in copies:
        copy.start()
    for copy in copies:
        copy.wait()


def pack_kernel(n_col, exciton_ref, cond_ref, after_ref, core_ref, sems):
    del after_ref
    col = lax.axis_index("col")
    copies, at = [], 0
    for source in (cond_ref, exciton_ref):
        part = source.shape[0] // n_col
        rows = pl.ds(pl.multiple_of(col * part, part), part)
        for block in range(source.shape[1] // LANES):
            copies.append(pltpu.make_async_copy(
                source.at[rows, block * LANES:(block + 1) * LANES],
                core_ref.at[at:at + part, :], sems.at[len(copies)],
            ))
            at += part
    run(copies)


def join_kernel(*refs):
    *parts, out = refs
    at = 0
    for part in parts:
        out[at:at + part.shape[0], :] = part[...]
        at += part.shape[0]


def join(parts):
    shape = (sum(part.shape[0] for part in parts), parts[0].shape[1])
    return pl.pallas_call(
        join_kernel,
        in_specs=[IN_VMEM] * len(parts),
        out_specs=IN_VMEM,
        out_shape=jax.ShapeDtypeStruct(shape, BF16),
        compiler_params=pltpu.CompilerParams(vmem_limit_bytes=4 * MIB),
        cost_estimate=pl.CostEstimate(flops=JOIN_FLOPS, bytes_accessed=0, transcendentals=0),
        name="join",
    )(*parts)


def spread_kernel(n_row, *refs):
    *parts, out = refs
    row = lax.axis_index("row")
    part = out.shape[1] // n_row
    for other in range(n_row):
        rows = pl.ds(pl.multiple_of((row ^ other) * part, part), part)
        for flip in range(out.shape[0]):
            out[flip, rows, :] = parts[other][flip * part:(flip + 1) * part, :]


def set_panels(panels, cond_tile, exciton, n_v):
    by_point = lax.dot_general(
        cond_tile, exciton, (((0,), (1,)), ((), ())), preferred_element_type=F32
    ).astype(BF16)
    for b in range(exciton.shape[0] // n_v):
        panels[b * TILE:(b + 1) * TILE, :] = by_point[:, b * n_v:(b + 1) * n_v]


def own_kernel(
    q_ref, w_ref, exciton_ref, cond_ref, val_ref, after_ref, sums, w, cond, val, w_own, exciton, panels, sems
):
    del after_ref
    me, n_others = lax.axis_index("ka"), w.shape[0]
    pairs = [(exciton_ref, exciton), (cond_ref, cond), (val_ref, val)]
    pairs += [(w_ref.at[q_ref[me, me]], w_own)]
    pairs += [(w_ref.at[q_ref[me ^ flip, me]], w.at[flip - 1]) for flip in range(1, n_others + 1)]
    copies = [
        pltpu.make_async_copy(source, target, sems.at[i])
        for i, (source, target) in enumerate(pairs)
    ]
    for copy in copies:
        copy.start()
    for copy in copies[:3]:
        copy.wait()
    n_v, n_nu = val.shape
    n_b = exciton.shape[0] // n_v
    for t in range(cond.shape[1] // TILE):
        set_panels(panels.at[t % 2], cond[:, t * TILE:(t + 1) * TILE], exciton[...], n_v)
        for j in range(n_nu // CHUNK):
            at = slice(j * CHUNK, (j + 1) * CHUNK)
            product = jnp.dot(panels[t % 2], val[:, at], preferred_element_type=F32)
            if t == 0 and j == 0:
                copies[3].wait()
            weights = w_own[t * TILE:(t + 1) * TILE, at].astype(F32)
            for b in range(n_b):
                rows = slice(b * TILE, (b + 1) * TILE)
                sums[t, rows, at] = product[rows, :] * weights
    for copy in copies[4:]:
        copy.wait()


def put_together(cores, col, cond, exciton):
    n_col, n_c, n_mu = len(cores), cond.shape[0], cond.shape[1]
    part_c, part_x = n_c // n_col, exciton.shape[0] // n_col
    for other, source in enumerate(cores):
        at = 0
        rows = pl.ds(pl.multiple_of((col ^ other) * part_c, part_c), part_c)
        for block in range(n_mu // LANES):
            cond[rows, block * LANES:(block + 1) * LANES] = source[at:at + part_c, :]
            at += part_c
        rows = pl.ds(pl.multiple_of((col ^ other) * part_x, part_x), part_x)
        exciton[rows, :] = source[at:at + part_x, :]


def panels_kernel(n_col, n_v, *refs):
    *cores, panels, cond, exciton = refs
    col = lax.axis_index("col")
    for i in range(panels.shape[0]):
        put_together(cores[i * n_col:(i + 1) * n_col], col, cond.at[i], exciton.at[i])
        for t in range(panels.shape[1]):
            set_panels(panels.at[i, t], cond[i, :, t * TILE:(t + 1) * TILE], exciton[i], n_v)


def after_kernel(*refs):
    refs[-1][...] = refs[0][...]


def after(value, *others, flops=0):
    return pl.pallas_call(
        after_kernel,
        in_specs=[IN_VMEM] + [pl.BlockSpec(memory_space=pl.ANY)] * len(others),
        out_specs=IN_VMEM,
        out_shape=jax.ShapeDtypeStruct(value.shape, value.dtype),
        compiler_params=pltpu.CompilerParams(vmem_limit_bytes=4 * MIB),
        cost_estimate=pl.CostEstimate(flops=flops, bytes_accessed=0, transcendentals=0),
        name="after",
    )(value, *others)


def direct_kernel(sizes, early, factor, *refs):
    n_ka, n_row, n_col = sizes
    refs = list(refs)

    def take(count):
        taken, refs[:] = refs[:count], refs[count:]
        return taken

    sums, w, cond_own, val_own, early_panels = take(5)
    n_early = early_panels.shape[0]
    late = [flip for flip in range(1, n_ka) if flip not in early]
    cores = [take(n_col) for _ in late]
    val_ref, = take(1)
    keep, *sent = take(n_col)
    x_all, cond_all, panels, products, direct, running, half, total = refs
    col = lax.axis_index("col")
    n_v, n_nu = val_own.shape
    n_c, n_mu = cond_own.shape
    n_b = x_all.shape[1] // n_v
    n_tiles, n_others = n_mu // TILE, n_ka - 1
    order = list(early) + late

    for i in range(len(late)):
        put_together(cores[i], col, cond_all.at[i], x_all.at[i])

    steps = [(t, j) for t in range(n_tiles) for j in range(n_nu // CHUNK)]
    quarter = TILE // QUARTERS

    def all_panels(t):
        for i in range(len(late)):
            set_panels(panels.at[t % 2, i], cond_all[i, :, t * TILE:(t + 1) * TILE], x_all[i], n_v)

    def multiply(number, i):
        t, j = steps[number]
        left = early_panels[i, t] if i < n_early else panels[t % 2, i - n_early]
        products[number % 2, i] = jnp.dot(
            left, val_ref[order[i] - 1, :, j * CHUNK:(j + 1) * CHUNK],
            preferred_element_type=F32,
        ).astype(BF16)

    def combine(number, part):
        t, j = steps[number]
        at = slice(j * CHUNK, (j + 1) * CHUNK)
        for m in range(part * quarter, (part + 1) * quarter, ROWS):
            weights = [
                w[flip - 1, t * TILE + m:t * TILE + m + ROWS, at].astype(F32) for flip in order
            ]
            for b in range(n_b):
                rows = slice(b * TILE + m, b * TILE + m + ROWS)
                value = sums[t, rows, at]
                for i in range(n_others):
                    value += products[number % 2, i, rows, :].astype(F32) * weights[i]
                direct[t % 2, rows, at] = value.astype(BF16)

    per_tile = n_nu // CHUNK
    span = 2 if per_tile % 2 == 0 else 1

    def reduce(number):
        t, j = steps[number]
        if (j + 1) % span:
            return
        at = slice((j + 1 - span) * CHUNK, (j + 1) * CHUNK)
        value = lax.dot_general(
            direct[t % 2, :, at], val_own[:, at], (((1,), (1,)), ((), ())),
            preferred_element_type=F32,
        )
        if j + 1 > span:
            value += running[...]
        if j + 1 < per_tile:
            running[...] = value
            return
        value = value.astype(BF16)
        for b in range(n_b):
            half[b, t * TILE:(t + 1) * TILE, :] = value[b * TILE:(b + 1) * TILE, :]

    all_panels(0)
    for i in range(n_others):
        multiply(0, i)
    for number, (t, j) in enumerate(steps):
        more = number + 1 < len(steps)
        if more and steps[number + 1][0] != t:
            all_panels(t + 1)
        for i in range(max(n_others, QUARTERS)):
            if more and i < n_others:
                multiply(number + 1, i)
            if i < QUARTERS:
                combine(number, i)
        reduce(number)

    part = n_v // n_col
    for b in range(n_b):
        total[b * n_v:(b + 1) * n_v, :] = (
            jnp.dot(cond_own[...], half[b], preferred_element_type=F32) * factor
        ).T
        for other in range(n_col):
            rows = pl.ds(pl.multiple_of(b * n_v + (col ^ other) * part, part), part)
            value = total[rows, :]
            if other == 0:
                keep[b] = value
            else:
                sent[other - 1][b] = value.astype(BF16)


def local(sizes, exciton, orb_cond, orb_val, screened, q_table):
    n_ka, n_row, n_col = sizes
    n_b, n_v, n_c = exciton.shape[1:]
    x_rows, cond, val, screened, q_table = (
        pltpu.with_memory_space_constraint(array, pltpu.HBM)
        for array in (exciton.reshape(n_b * n_v, n_c), orb_cond[0], orb_val[0], screened, q_table)
    )
    n_mu, n_nu = cond.shape[1], val.shape[1]
    core_rows = (cond.size + x_rows.size) // n_col // LANES
    part = n_v // n_row
    plane = lax.dynamic_slice_in_dim(orb_val[0], lax.axis_index("row") * part, part, 0)
    planes = [swap(plane, "ka", n_ka, flip) for flip in range(1, n_ka)]
    core = pl.pallas_call(
        functools.partial(pack_kernel, n_col),
        in_specs=[IN_HBM] * 2 + [pl.BlockSpec(memory_space=pl.ANY)],
        out_specs=IN_VMEM,
        out_shape=jax.ShapeDtypeStruct((core_rows, LANES), BF16),
        scratch_shapes=[pltpu.SemaphoreType.DMA(((n_mu + n_c) // LANES,))],
        compiler_params=pltpu.CompilerParams(vmem_limit_bytes=4 * MIB),
        name="pack",
    )(x_rows, cond, planes[0])
    joined = join(planes)
    cores = [core]
    for flip in range(1, n_ka):
        last = flip & -flip
        source = cores[flip - last]
        if flip == last and flip > 1:
            source = after(source, planes[flip - 1])
        cores.append(swap(source, "ka", n_ka, last))
        if flip == 2:
            cores[2] = after(cores[2], joined, cores[1])
    n_tiles = n_mu // TILE
    loaded = pl.pallas_call(
        own_kernel,
        in_specs=[IN_SMEM] + [IN_HBM] * 4 + [pl.BlockSpec(memory_space=pl.ANY)],
        out_specs=[IN_VMEM] * 4,
        out_shape=[
            jax.ShapeDtypeStruct((n_tiles, n_b * TILE, n_nu), F32),
            jax.ShapeDtypeStruct((n_ka - 1, n_mu, n_nu), BF16),
            jax.ShapeDtypeStruct(cond.shape, BF16),
            jax.ShapeDtypeStruct(val.shape, BF16),
        ],
        scratch_shapes=[
            pltpu.VMEM((n_mu, n_nu), BF16),
            pltpu.VMEM(x_rows.shape, BF16),
            pltpu.VMEM((2, n_b * TILE, n_v), BF16),
            pltpu.SemaphoreType.DMA((n_ka + 3,)),
        ],
        compiler_params=pltpu.CompilerParams(vmem_limit_bytes=24 * MIB),
        cost_estimate=pl.CostEstimate(
            flops=0, bytes_accessed=4 * screened.size, transcendentals=0
        ),
        name="own_term",
    )(q_table, screened, x_rows, cond, val, cores[n_ka // 2])
    early = [flip for flip in range(1, n_ka) if flip.bit_count() == 1]
    both = {
        flip: [swap(cores[flip], "col", n_col, d) if d else cores[flip] for d in range(n_col)]
        for flip in range(1, n_ka)
    }
    operands = [pl.pallas_call(
        functools.partial(panels_kernel, n_col, n_v),
        in_specs=[IN_VMEM] * (len(early) * n_col),
        out_specs=IN_VMEM,
        out_shape=jax.ShapeDtypeStruct((len(early), n_tiles, n_b * TILE, n_v), BF16),
        scratch_shapes=[
            pltpu.VMEM((len(early), n_c, n_mu), BF16),
            pltpu.VMEM((len(early), n_b * n_v, n_c), BF16),
        ],
        compiler_params=pltpu.CompilerParams(vmem_limit_bytes=12 * MIB),
        cost_estimate=pl.CostEstimate(flops=PANEL_FLOPS, bytes_accessed=0, transcendentals=0),
        name="panels",
    )(*(part for flip in early for part in both[flip]))]
    operands += [part for flip in both if flip not in early for part in both[flip]]
    parts = [swap(joined, "row", n_row, d) if d else joined for d in range(n_row)]
    operands.append(pl.pallas_call(
        functools.partial(spread_kernel, n_row),
        in_specs=[IN_VMEM] * n_row,
        out_specs=IN_VMEM,
        out_shape=jax.ShapeDtypeStruct((n_ka - 1, *val.shape), BF16),
        compiler_params=pltpu.CompilerParams(vmem_limit_bytes=4 * MIB),
        cost_estimate=pl.CostEstimate(flops=SPREAD_FLOPS, bytes_accessed=0, transcendentals=0),
        name="spread",
    )(*parts))

    factor = math.sqrt(n_v * n_c) / (n_mu * n_row)
    part = n_v // n_col
    n_late = n_ka - 1 - len(early)
    kept, *sent = pl.pallas_call(
        functools.partial(direct_kernel, sizes, early, factor),
        in_specs=[IN_VMEM] * (len(loaded) + len(operands)),
        out_specs=[IN_VMEM] * n_col,
        out_shape=[jax.ShapeDtypeStruct((n_b, part, n_c), F32)]
        + [jax.ShapeDtypeStruct((n_b, part, n_c), BF16)] * (n_col - 1),
        scratch_shapes=[
            pltpu.VMEM((n_late, n_b * n_v, n_c), BF16),
            pltpu.VMEM((n_late, n_c, n_mu), BF16),
            pltpu.VMEM((2, n_late, n_b * TILE, n_v), BF16),
            pltpu.VMEM((2, n_ka - 1, n_b * TILE, CHUNK), BF16),
            pltpu.VMEM((2, n_b * TILE, n_nu), BF16),
            pltpu.VMEM((n_b * TILE, n_v), F32),
            pltpu.VMEM((n_b, n_mu, n_v), BF16),
            pltpu.VMEM((n_b * n_v, n_c), F32),
        ],
        compiler_params=pltpu.CompilerParams(vmem_limit_bytes=36 * MIB),
        name="direct_term",
    )(*loaded, *operands)
    mine = kept
    for flip in range(1, n_col):
        mine = mine + swap(sent[flip - 1], "col", n_col, flip).astype(F32)
    mine = mine.astype(BF16)
    terms = [after(swap(mine, "row", n_row, n_row - 1), flops=JOIN_FLOPS)]
    terms += [swap(mine, "row", n_row, flip) for flip in reversed(range(1, n_row - 1))] + [mine]
    terms = [term.astype(F32) for term in terms]
    while len(terms) > 1:
        terms = [a + b for a, b in zip(terms[::2], terms[1::2])]
    return terms[0][None]


def solution(mesh):
    placed = (
        P("ka", None, None, None),
        P("ka", None, "row"),
        P("ka", None, "col"),
        P(None, "row", "col"),
        P(),
    )
    sizes = tuple(mesh.shape[name] for name in ("ka", "row", "col"))
    return jax.shard_map(
        functools.partial(local, sizes), mesh=mesh, in_specs=placed,
        out_specs=P("ka", None, "col", None), check_vma=False,
    )
```

```python
import functools
import math

import jax
import jax.numpy as jnp
from jax import lax
from jax.experimental import pallas as pl
from jax.experimental.pallas import tpu as pltpu
from jax.sharding import PartitionSpec as P

BF16 = jnp.bfloat16
F32 = jnp.float32
LANES = 128
ROWS = 16
TILE = 128
CHUNK = 256
QUARTERS = 4
MIB = 2**20
JOIN_FLOPS = 2 * 10**10
SPREAD_FLOPS = 2 * 10**10
PANEL_FLOPS = 10**9
IN_HBM = pl.BlockSpec(memory_space=pltpu.HBM)
IN_VMEM = pl.BlockSpec(memory_space=pltpu.VMEM)
IN_SMEM = pl.BlockSpec(memory_space=pltpu.SMEM)


def swap(value, axis, size, flip):
    return lax.ppermute(value, axis, [(i, i ^ flip) for i in range(size)])


def run(copies):
    for copy in copies:
        copy.start()
    for copy in copies:
        copy.wait()


def pack_kernel(n_col, exciton_ref, cond_ref, after_ref, core_ref, sems):
    del after_ref
    col = lax.axis_index("col")
    copies, at = [], 0
    for source in (cond_ref, exciton_ref):
        part = source.shape[0] // n_col
        rows = pl.ds(pl.multiple_of(col * part, part), part)
        for block in range(source.shape[1] // LANES):
            copies.append(pltpu.make_async_copy(
                source.at[rows, block * LANES:(block + 1) * LANES],
                core_ref.at[at:at + part, :], sems.at[len(copies)],
            ))
            at += part
    run(copies)


def join_kernel(*refs):
    *parts, out = refs
    at = 0
    for part in parts:
        out[at:at + part.shape[0], :] = part[...]
        at += part.shape[0]


def join(parts):
    shape = (sum(part.shape[0] for part in parts), parts[0].shape[1])
    return pl.pallas_call(
        join_kernel,
        in_specs=[IN_VMEM] * len(parts),
        out_specs=IN_VMEM,
        out_shape=jax.ShapeDtypeStruct(shape, BF16),
        compiler_params=pltpu.CompilerParams(vmem_limit_bytes=4 * MIB),
        cost_estimate=pl.CostEstimate(flops=JOIN_FLOPS, bytes_accessed=0, transcendentals=0),
        name="join",
    )(*parts)


def spread_kernel(n_row, *refs):
    *parts, out = refs
    row = lax.axis_index("row")
    part = out.shape[1] // n_row
    for other in range(n_row):
        rows = pl.ds(pl.multiple_of((row ^ other) * part, part), part)
        for flip in range(out.shape[0]):
            out[flip, rows, :] = parts[other][flip * part:(flip + 1) * part, :]


def set_panels(panels, cond_tile, exciton, n_v):
    by_point = lax.dot_general(
        cond_tile, exciton, (((0,), (1,)), ((), ())), preferred_element_type=F32
    ).astype(BF16)
    for b in range(exciton.shape[0] // n_v):
        panels[b * TILE:(b + 1) * TILE, :] = by_point[:, b * n_v:(b + 1) * n_v]


def own_kernel(
    q_ref, w_ref, exciton_ref, cond_ref, val_ref, after_ref, sums, w, cond, val, w_own, exciton, panels, sems
):
    del after_ref
    me, n_others = lax.axis_index("ka"), w.shape[0]
    pairs = [(exciton_ref, exciton), (cond_ref, cond), (val_ref, val)]
    pairs += [(w_ref.at[q_ref[me, me]], w_own)]
    pairs += [(w_ref.at[q_ref[me ^ flip, me]], w.at[flip - 1]) for flip in range(1, n_others + 1)]
    copies = [
        pltpu.make_async_copy(source, target, sems.at[i])
        for i, (source, target) in enumerate(pairs)
    ]
    for copy in copies:
        copy.start()
    for copy in copies[:3]:
        copy.wait()
    n_v, n_nu = val.shape
    n_b = exciton.shape[0] // n_v
    for t in range(cond.shape[1] // TILE):
        set_panels(panels.at[t % 2], cond[:, t * TILE:(t + 1) * TILE], exciton[...], n_v)
        for j in range(n_nu // CHUNK):
            at = slice(j * CHUNK, (j + 1) * CHUNK)
            product = jnp.dot(panels[t % 2], val[:, at], preferred_element_type=F32)
            if t == 0 and j == 0:
                copies[3].wait()
            weights = w_own[t * TILE:(t + 1) * TILE, at].astype(F32)
            for b in range(n_b):
                rows = slice(b * TILE, (b + 1) * TILE)
                sums[t, rows, at] = product[rows, :] * weights
    for copy in copies[4:]:
        copy.wait()


def put_together(cores, col, cond, exciton):
    n_col, n_c, n_mu = len(cores), cond.shape[0], cond.shape[1]
    part_c, part_x = n_c // n_col, exciton.shape[0] // n_col
    for other, source in enumerate(cores):
        at = 0
        rows = pl.ds(pl.multiple_of((col ^ other) * part_c, part_c), part_c)
        for block in range(n_mu // LANES):
            cond[rows, block * LANES:(block + 1) * LANES] = source[at:at + part_c, :]
            at += part_c
        rows = pl.ds(pl.multiple_of((col ^ other) * part_x, part_x), part_x)
        exciton[rows, :] = source[at:at + part_x, :]


def panels_kernel(n_col, n_v, *refs):
    *cores, panels, cond, exciton = refs
    col = lax.axis_index("col")
    for i in range(panels.shape[0]):
        put_together(cores[i * n_col:(i + 1) * n_col], col, cond.at[i], exciton.at[i])
        for t in range(panels.shape[1]):
            set_panels(panels.at[i, t], cond[i, :, t * TILE:(t + 1) * TILE], exciton[i], n_v)


def after_kernel(*refs):
    refs[-1][...] = refs[0][...]


def after(value, *others, flops=0):
    return pl.pallas_call(
        after_kernel,
        in_specs=[IN_VMEM] + [pl.BlockSpec(memory_space=pl.ANY)] * len(others),
        out_specs=IN_VMEM,
        out_shape=jax.ShapeDtypeStruct(value.shape, value.dtype),
        compiler_params=pltpu.CompilerParams(vmem_limit_bytes=4 * MIB),
        cost_estimate=pl.CostEstimate(flops=flops, bytes_accessed=0, transcendentals=0),
        name="after",
    )(value, *others)


def direct_kernel(sizes, early, factor, *refs):
    n_ka, n_row, n_col = sizes
    refs = list(refs)

    def take(count):
        taken, refs[:] = refs[:count], refs[count:]
        return taken

    sums, w, cond_own, val_own, early_panels = take(5)
    n_early = early_panels.shape[0]
    late = [flip for flip in range(1, n_ka) if flip not in early]
    cores = [take(n_col) for _ in late]
    val_ref, = take(1)
    keep, *sent = take(n_col)
    x_all, cond_all, panels, products, direct, running, half, total = refs
    col = lax.axis_index("col")
    n_v, n_nu = val_own.shape
    n_c, n_mu = cond_own.shape
    n_b = x_all.shape[1] // n_v
    n_tiles, n_others = n_mu // TILE, n_ka - 1
    order = list(early) + late

    for i in range(len(late)):
        put_together(cores[i], col, cond_all.at[i], x_all.at[i])

    steps = [(t, j) for t in range(n_tiles) for j in range(n_nu // CHUNK)]
    quarter = TILE // QUARTERS

    def all_panels(t):
        for i in range(len(late)):
            set_panels(panels.at[t % 2, i], cond_all[i, :, t * TILE:(t + 1) * TILE], x_all[i], n_v)

    def multiply(number, i):
        t, j = steps[number]
        left = early_panels[i, t] if i < n_early else panels[t % 2, i - n_early]
        products[number % 2, i] = jnp.dot(
            left, val_ref[order[i] - 1, :, j * CHUNK:(j + 1) * CHUNK],
            preferred_element_type=F32,
        ).astype(BF16)

    def combine(number, part):
        t, j = steps[number]
        at = slice(j * CHUNK, (j + 1) * CHUNK)
        for m in range(part * quarter, (part + 1) * quarter, ROWS):
            weights = [
                w[flip - 1, t * TILE + m:t * TILE + m + ROWS, at].astype(F32) for flip in order
            ]
            for b in range(n_b):
                rows = slice(b * TILE + m, b * TILE + m + ROWS)
                value = sums[t, rows, at]
                for i in range(n_others):
                    value += products[number % 2, i, rows, :].astype(F32) * weights[i]
                direct[t % 2, rows, at] = value.astype(BF16)

    def reduce(number):
        t, j = steps[number]
        at = slice(j * CHUNK, (j + 1) * CHUNK)
        value = lax.dot_general(
            direct[t % 2, :, at], val_own[:, at], (((1,), (1,)), ((), ())),
            preferred_element_type=F32,
        )
        if j:
            value += running[...]
        if j + 1 < n_nu // CHUNK:
            running[...] = value
            return
        value = value.astype(BF16)
        for b in range(n_b):
            half[b, t * TILE:(t + 1) * TILE, :] = value[b * TILE:(b + 1) * TILE, :]

    all_panels(0)
    for i in range(n_others):
        multiply(0, i)
    for number, (t, j) in enumerate(steps):
        more = number + 1 < len(steps)
        if more and steps[number + 1][0] != t:
            all_panels(t + 1)
        for i in range(max(n_others, QUARTERS)):
            if more and i < n_others:
                multiply(number + 1, i)
            if i < QUARTERS:
                combine(number, i)
        reduce(number)

    part = n_v // n_col
    for b in range(n_b):
        total[b * n_v:(b + 1) * n_v, :] = (
            jnp.dot(cond_own[...], half[b], preferred_element_type=F32) * factor
        ).T
        for other in range(n_col):
            rows = pl.ds(pl.multiple_of(b * n_v + (col ^ other) * part, part), part)
            value = total[rows, :]
            if other == 0:
                keep[b] = value
            else:
                sent[other - 1][b] = value.astype(BF16)


def local(sizes, exciton, orb_cond, orb_val, screened, q_table):
    n_ka, n_row, n_col = sizes
    n_b, n_v, n_c = exciton.shape[1:]
    x_rows, cond, val, screened, q_table = (
        pltpu.with_memory_space_constraint(array, pltpu.HBM)
        for array in (exciton.reshape(n_b * n_v, n_c), orb_cond[0], orb_val[0], screened, q_table)
    )
    n_mu, n_nu = cond.shape[1], val.shape[1]
    core_rows = (cond.size + x_rows.size) // n_col // LANES
    part = n_v // n_row
    plane = lax.dynamic_slice_in_dim(orb_val[0], lax.axis_index("row") * part, part, 0)
    planes = [swap(plane, "ka", n_ka, flip) for flip in range(1, n_ka)]
    core = pl.pallas_call(
        functools.partial(pack_kernel, n_col),
        in_specs=[IN_HBM] * 2 + [pl.BlockSpec(memory_space=pl.ANY)],
        out_specs=IN_VMEM,
        out_shape=jax.ShapeDtypeStruct((core_rows, LANES), BF16),
        scratch_shapes=[pltpu.SemaphoreType.DMA(((n_mu + n_c) // LANES,))],
        compiler_params=pltpu.CompilerParams(vmem_limit_bytes=4 * MIB),
        name="pack",
    )(x_rows, cond, planes[0])
    joined = join(planes)
    cores = [core]
    for flip in range(1, n_ka):
        last = flip & -flip
        source = cores[flip - last]
        if flip == last and flip > 1:
            source = after(source, planes[flip - 1])
        cores.append(swap(source, "ka", n_ka, last))
        if flip == 2:
            cores[2] = after(cores[2], joined, cores[1])
    n_tiles = n_mu // TILE
    loaded = pl.pallas_call(
        own_kernel,
        in_specs=[IN_SMEM] + [IN_HBM] * 4 + [pl.BlockSpec(memory_space=pl.ANY)],
        out_specs=[IN_VMEM] * 4,
        out_shape=[
            jax.ShapeDtypeStruct((n_tiles, n_b * TILE, n_nu), F32),
            jax.ShapeDtypeStruct((n_ka - 1, n_mu, n_nu), BF16),
            jax.ShapeDtypeStruct(cond.shape, BF16),
            jax.ShapeDtypeStruct(val.shape, BF16),
        ],
        scratch_shapes=[
            pltpu.VMEM((n_mu, n_nu), BF16),
            pltpu.VMEM(x_rows.shape, BF16),
            pltpu.VMEM((2, n_b * TILE, n_v), BF16),
            pltpu.SemaphoreType.DMA((n_ka + 3,)),
        ],
        compiler_params=pltpu.CompilerParams(vmem_limit_bytes=24 * MIB),
        cost_estimate=pl.CostEstimate(
            flops=0, bytes_accessed=4 * screened.size, transcendentals=0
        ),
        name="own_term",
    )(q_table, screened, x_rows, cond, val, cores[n_ka // 2])
    early = [flip for flip in range(1, n_ka) if flip.bit_count() == 1]
    both = {
        flip: [swap(cores[flip], "col", n_col, d) if d else cores[flip] for d in range(n_col)]
        for flip in range(1, n_ka)
    }
    operands = [pl.pallas_call(
        functools.partial(panels_kernel, n_col, n_v),
        in_specs=[IN_VMEM] * (len(early) * n_col),
        out_specs=IN_VMEM,
        out_shape=jax.ShapeDtypeStruct((len(early), n_tiles, n_b * TILE, n_v), BF16),
        scratch_shapes=[
            pltpu.VMEM((len(early), n_c, n_mu), BF16),
            pltpu.VMEM((len(early), n_b * n_v, n_c), BF16),
        ],
        compiler_params=pltpu.CompilerParams(vmem_limit_bytes=12 * MIB),
        cost_estimate=pl.CostEstimate(flops=PANEL_FLOPS, bytes_accessed=0, transcendentals=0),
        name="panels",
    )(*(part for flip in early for part in both[flip]))]
    operands += [part for flip in both if flip not in early for part in both[flip]]
    parts = [swap(joined, "row", n_row, d) if d else joined for d in range(n_row)]
    operands.append(pl.pallas_call(
        functools.partial(spread_kernel, n_row),
        in_specs=[IN_VMEM] * n_row,
        out_specs=IN_VMEM,
        out_shape=jax.ShapeDtypeStruct((n_ka - 1, *val.shape), BF16),
        compiler_params=pltpu.CompilerParams(vmem_limit_bytes=4 * MIB),
        cost_estimate=pl.CostEstimate(flops=SPREAD_FLOPS, bytes_accessed=0, transcendentals=0),
        name="spread",
    )(*parts))

    factor = math.sqrt(n_v * n_c) / (n_mu * n_row)
    part = n_v // n_col
    n_late = n_ka - 1 - len(early)
    kept, *sent = pl.pallas_call(
        functools.partial(direct_kernel, sizes, early, factor),
        in_specs=[IN_VMEM] * (len(loaded) + len(operands)),
        out_specs=[IN_VMEM] * n_col,
        out_shape=[jax.ShapeDtypeStruct((n_b, part, n_c), F32)]
        + [jax.ShapeDtypeStruct((n_b, part, n_c), BF16)] * (n_col - 1),
        scratch_shapes=[
            pltpu.VMEM((n_late, n_b * n_v, n_c), BF16),
            pltpu.VMEM((n_late, n_c, n_mu), BF16),
            pltpu.VMEM((2, n_late, n_b * TILE, n_v), BF16),
            pltpu.VMEM((2, n_ka - 1, n_b * TILE, CHUNK), BF16),
            pltpu.VMEM((2, n_b * TILE, n_nu), BF16),
            pltpu.VMEM((n_b * TILE, n_v), F32),
            pltpu.VMEM((n_b, n_mu, n_v), BF16),
            pltpu.VMEM((n_b * n_v, n_c), F32),
        ],
        compiler_params=pltpu.CompilerParams(vmem_limit_bytes=36 * MIB),
        name="direct_term",
    )(*loaded, *operands)
    mine = kept
    for flip in range(1, n_col):
        mine = mine + swap(sent[flip - 1], "col", n_col, flip).astype(F32)
    mine = mine.astype(BF16)
    terms = [after(swap(mine, "row", n_row, n_row - 1), flops=JOIN_FLOPS)]
    terms += [swap(mine, "row", n_row, flip) for flip in reversed(range(1, n_row - 1))] + [mine]
    terms = [term.astype(F32) for term in terms]
    while len(terms) > 1:
        terms = [a + b for a, b in zip(terms[::2], terms[1::2])]
    return terms[0][None]


def solution(mesh):
    placed = (
        P("ka", None, None, None),
        P("ka", None, "row"),
        P("ka", None, "col"),
        P(None, "row", "col"),
        P(),
    )
    sizes = tuple(mesh.shape[name] for name in ("ka", "row", "col"))
    return jax.shard_map(
        functools.partial(local, sizes), mesh=mesh, in_specs=placed,
        out_specs=P("ka", None, "col", None), check_vma=False,
    )
```
